32 devices in a mesh: row: 4 (over y, core), col: 8 (over z, x).
Axes of the slice: x: 2, y: 2, z: 4, core: 2. Of those that a mesh axis runs over, the one named last changes fastest.
Arguments:
- tokens: bfloat16 [8192, 2048], P('row', 'col'), may hold values from -7 to 7
- lengths: int32 [8, 4], P('row'), may hold values from 1 to 800, 1024 in all within a row
- w_query: bfloat16 [2048, 2048], P('row', 'col'), may hold values from -0.1875 to 0.1875
- b_query: float32 [2048], P('col'), may hold values from -3 to 3
- w_key: bfloat16 [2048, 2048], P('row', 'col'), may hold values from -0.125 to 0.125
- w_value: bfloat16 [2048, 2048], P('row', 'col'), may hold values from -0.125 to 0.125
- b_value: float32 [2048], P('col'), may hold values from -3 to 3
- w_proj: bfloat16 [2048, 2048], P('col', 'row'), may hold values from -0.5 to 0.5
- b_proj: float32 [2048], P('col'), may hold values from -2 to 2
- norm_gain: float32 [2048], P('col'), may hold values from 0.5 to 1.5
- norm_shift: float32 [2048], P('col'), may hold values from -2 to 2
- w_up: bfloat16 [2048, 8192], P('row', 'col'), may hold values from -0.125 to 0.125
- b_up: float32 [8192], P('col'), may hold values from -3 to 3
- w_down: bfloat16 [8192, 2048], P('col', 'row'), may hold values from -0.0625 to 0.0625
- b_down: float32 [2048], P('col'), may hold values from -2 to 2
- final_gain: float32 [2048], P('col'), may hold values from 0.5 to 1.5
- final_shift: float32 [2048], P('col'), may hold values from -2 to 2
- cotangent: bfloat16 [8192, 2048], P('row', 'col'), may hold values from -6 to 6
Outputs:
- layer_out: bfloat16 [8192, 2048], P('row', 'col')
- grad_tokens: float32 [8192, 2048], P('row', 'col')
- grad_query: float32 [2048, 2048], P('row', 'col')
- grad_qbias: float32 [2048], P('col')
- grad_key: float32 [2048, 2048], P('row', 'col')
- grad_value: float32 [2048, 2048], P('row', 'col')
- grad_vbias: float32 [2048], P('col')
- grad_proj: float32 [2048, 2048], P('col', 'row')
- grad_pbias: float32 [2048], P('col')
- grad_ngain: float32 [2048], P('col')
- grad_nshift: float32 [2048], P('col')
- grad_up: float32 [2048, 8192], P('row', 'col')
- grad_ubias: float32 [8192], P('col')
- grad_down: float32 [8192, 2048], P('col', 'row')
- grad_dbias: float32 [2048], P('col')
- grad_fgain: float32 [2048], P('col')
- grad_fshift: float32 [2048], P('col')
- norms: float32 [3], replicated
The draws below stay inside these ranges and needn't reach their ends.
Inputs may be any that keep to these rules, and one draw needn't show every extreme that they name: Each row of 4 entries sums to 1024; its first 3 entries are the lengths of its documents in order, the last counts the padding tokens at the sequence's end.
All inputs are finite; a program needn't handle non-finite values.
Results may differ from the reference program's by a relative error of at most 0.017.
Values may be sent and summed in bfloat16 or wider, within the bound.
No kernel may reach another device: no remote copies, remote signals or barrier semaphores. Data moves between devices by JAX's collectives and lax.ppermute only.
A program may use at most 192 MiB of HBM per device.

```python
import math
from functools import partial
import jax
import jax.numpy as jnp
import numpy as np
from jax import lax

D = 2048
H = 16
FF = 8192
HD = 128
LEN = 1024
DOCS = 4
DOC_MOST = 800
SEQS = 8
TOKENS = 8192


def draw_tokens(key, part):
    key = jax.random.fold_in(key, 11)
    first, second = jax.random.split(key)
    place = jnp.arange(TOKENS, dtype=jnp.float32) / max(TOKENS - 1, 1)
    rise = jnp.exp(0.5 * jnp.log(3.0) * (place - 0.5))
    base = jnp.clip(jax.random.normal(first, (TOKENS, D), jnp.float32), -4.5, 4.5)
    jitter = jax.random.uniform(second, (TOKENS, 1), jnp.float32, 0.9, 1.1)
    return (base * rise[:, None] * jitter).astype(jnp.bfloat16)


def block_levels(stream_key, extent, cuts, low, high):
    def one(dim, parts):
        draws = jax.random.uniform(jax.random.fold_in(jax.random.fold_in(stream_key, 6), dim), (parts,), jnp.float32, low / len(cuts), high / len(cuts))
        return jnp.repeat(jnp.exp(draws), extent[dim] // parts).reshape((-1,) + (1,) * (len(extent) - dim - 1))

    level = one(*cuts[0])
    for cut in cuts[1:]:
        level = level * one(*cut)
    return level


def length_profile(amount, total, bound, slope):
    weights = [(1 << 20) // math.isqrt(grade ** slope) + 1 for grade in range(2, amount + 1)]
    surplus, counts = total - bound - (amount - 1), [1] * (amount - 1)
    while surplus > 0:
        movable = [i for i in range(amount - 1) if counts[i] < bound]
        pool, remaining = sum([weights[i] for i in movable]), surplus
        for i in movable:
            more = min(bound - counts[i], max(1, remaining * weights[i] // pool), surplus)
            counts[i] = counts[i] + more
            surplus = surplus - more
    return np.array([bound] + counts)


def uneven(own_key, number_of, total, bound, slope):
    if number_of == 2:
        one = jax.random.randint(own_key, (), max(1, total - bound), min(bound, total - 1) + 1)
        return jnp.stack([one, total - one])
    sizes = jnp.asarray(length_profile(number_of, total, bound, slope), jnp.int32)
    twos = (number_of - 1) // 2
    source_of, taker = sizes[1:1 + 2 * twos:2], sizes[2:2 + 2 * twos:2]
    margin = jnp.minimum(source_of - 1, bound - taker)
    moved = jax.random.randint(jax.random.fold_in(own_key, 1), (twos,), 0, 1 << 20) % (margin + 1)
    sizes = sizes.at[1:1 + 2 * twos:2].set(source_of - moved).at[2:2 + 2 * twos:2].set(taker + moved)
    return sizes[jax.random.permutation(jax.random.fold_in(own_key, 2), number_of)]


def scatter_about(rng, extent, width, limit, shards=(), kind=jnp.bfloat16):
    loudness = block_levels(rng, extent, shards, -0.22, 0.18) if shards else 1.0
    drawn = jax.random.normal(rng, extent, jnp.float32) * width * loudness
    return jnp.minimum(jnp.maximum(drawn, -limit), limit).astype(kind)


def setup_inputs(seed: int = 0) -> dict:
    seeds = jax.random.split(jax.random.key(seed), 19)
    tokens = draw_tokens(jax.random.fold_in(seeds[18], 71), 0)
    lengths = jax.vmap(lambda own: uneven(own, DOCS, LEN, DOC_MOST, 1))(jax.random.split(seeds[1], SEQS)).reshape((SEQS, DOCS)).astype(jnp.int32)
    w_query = scatter_about(seeds[2], (D, D), (D // 2) ** -0.5, 0.1875, ((0, 4), (1, 8)))
    b_query = scatter_about(seeds[3], (D,), 0.5, 3.0, ((0, 8),), jnp.float32)
    w_key = scatter_about(seeds[4], (D, D), D ** -0.5, 0.125, ((0, 4), (1, 8)))
    w_value = scatter_about(seeds[5], (D, D), D ** -0.5, 0.125, ((0, 4), (1, 8)))
    b_value = scatter_about(seeds[6], (D,), 0.5, 3.0, ((0, 8),), jnp.float32)
    w_proj = scatter_about(seeds[7], (D, D), (D // 16) ** -0.5, 0.5, ((0, 8), (1, 4)))
    b_proj = scatter_about(seeds[8], (D,), 0.3, 2.0, ((0, 8),), jnp.float32)
    norm_gain = jnp.clip(1.0 + 0.1 * jax.random.normal(seeds[9], (D,), jnp.float32), 0.5, 1.5)
    norm_shift = scatter_about(seeds[10], (D,), 0.3, 2.0, ((0, 8),), jnp.float32)
    w_up = scatter_about(seeds[11], (D, FF), D ** -0.5, 0.125, ((0, 4), (1, 8)))
    b_up = scatter_about(seeds[12], (FF,), 0.5, 3.0, ((0, 8),), jnp.float32)
    w_down = scatter_about(seeds[13], (FF, D), FF ** -0.5, 0.0625, ((0, 8), (1, 4)))
    b_down = scatter_about(seeds[14], (D,), 0.3, 2.0, ((0, 8),), jnp.float32)
    final_gain = jnp.clip(1.0 + 0.1 * jax.random.normal(seeds[15], (D,), jnp.float32), 0.5, 1.5)
    final_shift = scatter_about(seeds[16], (D,), 0.3, 2.0, ((0, 8),), jnp.float32)
    cotangent = scatter_about(seeds[17], (TOKENS, D), 1.0, 6.0, ((0, 4), (1, 8)))
    return {"tokens": tokens, "lengths": lengths, "w_query": w_query, "b_query": b_query, "w_key": w_key, "w_value": w_value, "b_value": b_value, "w_proj": w_proj, "b_proj": b_proj, "norm_gain": norm_gain, "norm_shift": norm_shift, "w_up": w_up, "b_up": b_up, "w_down": w_down, "b_down": b_down, "final_gain": final_gain, "final_shift": final_shift, "cotangent": cotangent}


EPS = 1e-06
NEGATIVE = -1000000000.0
HIGH = lax.Precision.HIGHEST

@jax.custom_vjp
def low(v):
    return lax.optimization_barrier(v.astype(jnp.bfloat16)).astype(jnp.float32)

@jax.custom_vjp
def low_back(v):
    return v

def low_keep(v):
    return (low(v), None)

def low_pass(kept, grad):
    return (grad,)

def back_keep(v):
    return (v, None)

def back_low(kept, grad):
    return (low(grad),)
low.defvjp(low_keep, low_pass)
low_back.defvjp(back_keep, back_low)

def dense(left, right):
    return jnp.dot(left, right, precision=HIGH)

def segment_ids(lengths):
    ends = jnp.cumsum(lengths, axis=1).astype(jnp.int32)
    places = jnp.arange(LEN, dtype=jnp.int32)
    hits = (places[None, :, None] >= ends[:, None, :DOCS - 1]).astype(jnp.int32)
    return lax.optimization_barrier(jnp.sum(hits, axis=2)).astype(jnp.int32)

def layer_norm(resid, gain, shift):
    mean = lax.optimization_barrier(jnp.mean(resid, axis=-1, keepdims=True))
    var = lax.optimization_barrier(jnp.mean(resid * resid, axis=-1, keepdims=True)) - mean * mean
    return (resid - mean) * lax.rsqrt(var + EPS) * gain + shift

def attend(pack):
    queries, keys, values, ids = pack
    scores = jnp.einsum('qhd,khd->hqk', queries, keys, precision=HIGH) * HD ** (-0.5)
    same = ids[:, None] == ids[None, :]
    scores = low_back(jnp.where(same[None], scores, NEGATIVE))
    probs = jax.nn.softmax(scores, axis=-1)
    return jnp.einsum('hqk,khd->qhd', low(probs), values, precision=HIGH)

def forward(ids, stream, w_query, b_query, w_key, w_value, b_value, w_proj, b_proj, norm_gain, norm_shift, w_up, b_up, w_down, b_down, final_gain, final_shift):
    queries = low_back(low(dense(stream, w_query) + b_query))
    keys = low_back(low(dense(stream, w_key)))
    values = low_back(low(dense(stream, w_value) + b_value))
    shape = (SEQS, LEN, H, HD)
    mixed = lax.map(jax.checkpoint(attend), (queries.reshape(shape), keys.reshape(shape), values.reshape(shape), ids))
    heads_out = low_back(low(mixed.reshape(TOKENS, D)))
    attn = low_back(dense(heads_out, w_proj) + b_proj)
    hidden = layer_norm(stream + attn, norm_gain, norm_shift)
    pre = low_back(dense(low(hidden), w_up) + b_up)
    ffn = low_back(dense(low(jax.nn.gelu(pre, approximate=True)), w_down) + b_down)
    return (layer_norm(hidden + ffn, final_gain, final_shift), (attn, ffn))

def reference(tokens, lengths, w_query, b_query, w_key, w_value, b_value, w_proj, b_proj, norm_gain, norm_shift, w_up, b_up, w_down, b_down, final_gain, final_shift, cotangent):
    ids = segment_ids(lengths)
    primals = [arg.astype(jnp.float32) for arg in (tokens, w_query, b_query, w_key, w_value, b_value, w_proj, b_proj, norm_gain, norm_shift, w_up, b_up, w_down, b_down, final_gain, final_shift)]
    result, pullback, extras = jax.vjp(partial(forward, ids), *primals, has_aux=True)
    grads = pullback(cotangent.astype(jnp.float32))
    attn, ffn = extras
    stream = primals[0]
    valid = (ids.reshape(TOKENS) != DOCS - 1).astype(jnp.float32)[:, None]
    count = jnp.sum(valid) * D
    norms = jnp.stack([jnp.sqrt(jnp.sum(valid * stream * stream) / count), jnp.sqrt(jnp.sum(valid * attn * attn) / count), jnp.sqrt(jnp.sum(valid * ffn * ffn) / count)])
    return (result.astype(jnp.bfloat16), grads[0], grads[1], grads[2], grads[3], grads[4], grads[5], grads[6], grads[7], grads[8], grads[9], grads[10], grads[11], grads[12], grads[13], grads[14], grads[15], norms)
```

```python
import jax
import jax.numpy as jnp
from jax import lax
from jax.sharding import Mesh
from jax.sharding import PartitionSpec as P

HD = 128
LEN = 1024
EPS = 1e-06
NEGATIVE = -1000000000.0
BF = jnp.bfloat16
F32 = jnp.float32


def segment_ids(lengths):
    slots = lengths.shape[1]
    ends = jnp.cumsum(lengths, axis=1)
    places = jnp.arange(LEN, dtype=jnp.int32)
    hits = (places[None, :, None] >= ends[:, None, : slots - 1]).astype(jnp.int32)
    return jnp.sum(hits, axis=2)


def dot(left, right, dims):
    return lax.dot_general(left, right, (dims, ((), ())), preferred_element_type=F32)


AXES = ("y", "c", "z", "x")
X_BIT, Z_LOW, Z_HIGH, C_BIT, Y_BIT = 1, 2, 4, 8, 16
XY_BIT = X_BIT | Y_BIT


def swap(piece, mask):
    return lax.ppermute(piece, AXES, [(i, i ^ mask) for i in range(32)])


def to_share(piece):
    rows, width = piece.shape
    half = lax.all_to_all(piece, "y", 1, 0, tiled=True).reshape(4, rows // 2, width // 2)
    return lax.all_to_all(half, "z", 0, 2, tiled=True)[0]


def from_share(share):
    rows, width = share.shape
    parts = lax.all_to_all(share[None], "z", 2, 0, tiled=True)
    return lax.all_to_all(parts.reshape(2, 2 * rows, width // 4), "y", 0, 2, tiled=True)[0]


def square_gather(share):
    half = share.shape[0] // 2
    width = share.shape[1]
    from_x = swap(share, X_BIT)
    from_y = swap(share, Y_BIT)
    low = swap(from_x[:half], Y_BIT)
    high = swap(from_y[half:], X_BIT)
    from_xy = jnp.concatenate([low, high], axis=0)
    place = lax.axis_index("x") * 2 + lax.axis_index("y")
    whole = jnp.zeros((share.shape[0], 4 * width), share.dtype)
    for mask, block in ((0, share), (2, from_x), (1, from_y), (3, from_xy)):
        whole = lax.dynamic_update_slice_in_dim(whole, block, (place ^ mask) * width, 1)
    return whole


def square_scatter(produce):
    place = lax.axis_index("x") * 2 + lax.axis_index("y")
    far = produce(place ^ 3)
    half = far.shape[0] // 2
    low = slice(0, half)
    high = slice(half, None)
    far = far.astype(BF)
    far_low = swap(far[low], X_BIT)
    far_high = swap(far[high], Y_BIT)
    side_x = produce(place ^ 2)
    side_y = produce(place ^ 1)
    near_low = swap(side_x[low].astype(BF), X_BIT)
    near_high = swap(side_y[high].astype(BF), Y_BIT)
    pass_low = (side_y[low] + far_low.astype(F32)).astype(BF)
    pass_high = (side_x[high] + far_high.astype(F32)).astype(BF)
    last_low = swap(pass_low, Y_BIT)
    last_high = swap(pass_high, X_BIT)
    own = produce(place)
    return jnp.concatenate(
        [
            own[low] + near_low.astype(F32) + last_low.astype(F32),
            own[high] + near_high.astype(F32) + last_high.astype(F32),
        ],
        axis=0,
    )


def square_total(stats):
    return stats + swap(stats, X_BIT) + swap(stats, Y_BIT) + swap(stats, XY_BIT)


def gather_columns(pieces):
    halves = [lax.all_to_all(p, "y", 1, 0, tiled=True) for p in pieces]
    piece = jnp.concatenate(halves, axis=1) if len(halves) > 1 else halves[0]
    full = lax.all_gather(piece, ("z", "c"), axis=0)
    width = piece.shape[1]
    full = full.reshape(4, 2, 2, 4, 128, width)
    return full.transpose(3, 2, 1, 4, 0, 5).reshape(2048, 4 * width)


def gather_rows(piece):
    half = lax.all_to_all(piece, "y", 0, 1, tiled=True)
    full = lax.all_gather(half, ("z", "c"), axis=0)
    depth = half.shape[0]
    full = full.reshape(4, 2, depth, 2, 4, 128)
    return full.transpose(0, 2, 4, 3, 1, 5).reshape(4 * depth, 2048)


def scatter_columns(grad, count):
    width = grad.shape[1] // 4
    full = grad.reshape(4, 2, 2, 128, 4, width)
    full = full.transpose(4, 2, 1, 0, 3, 5).reshape(8, 1024, width)
    piece = lax.psum_scatter(full, ("z", "c"), scatter_dimension=0)
    n = width // count
    return [
        lax.all_to_all(piece[:, i * n : (i + 1) * n], "y", 0, 1, tiled=True).astype(F32)
        for i in range(count)
    ]


def scatter_rows(grad):
    depth = grad.shape[0] // 4
    full = grad.reshape(4, depth, 4, 2, 2, 128)
    full = full.transpose(0, 4, 1, 3, 2, 5).reshape(8, depth, 1024)
    piece = lax.psum_scatter(full, ("z", "c"), scatter_dimension=0)
    return lax.all_to_all(piece, "y", 1, 0, tiled=True).astype(F32)


def heads_of(block, part):
    return block.reshape(block.shape[0], 4, 3, HD)[:, :, part]


def square_device(
    tokens, lengths, w_query, b_query, w_key, w_value, b_value, w_proj, b_proj, norm_gain, norm_shift,
    w_up, b_up, w_down, b_down, final_gain, final_shift, cotangent,
):
    yi = lax.axis_index("y")
    zi = lax.axis_index("z")
    place = lax.axis_index("x") * 2 + yi
    width = 4 * 512

    other = swap(lengths, Y_BIT)
    both = jnp.where(yi == 0, jnp.concatenate([lengths, other]), jnp.concatenate([other, lengths]))
    ids = segment_ids(lax.dynamic_slice_in_dim(both, zi, 1, 0))[0]
    valid = (ids != lengths.shape[1] - 1).astype(F32)[:, None]

    vectors = jnp.concatenate(
        [v.reshape(2, -1) for v in (b_query, b_value, b_proj, norm_gain, norm_shift, b_down, final_gain, final_shift, b_up)],
        axis=1,
    )
    vectors = lax.dynamic_slice_in_dim(vectors, yi, 1, 0)
    vectors = lax.all_to_all(jnp.broadcast_to(vectors, (4, vectors.shape[1])), "z", 0, 0, tiled=True)
    small = [vectors[:, i * 128 : (i + 1) * 128] for i in range(8)]
    q_bias, v_bias, p_bias, n_gain, n_shift, d_bias, f_gain, f_shift = small
    p_bias, n_gain, n_shift, d_bias, f_gain, f_shift = (
        v.reshape(512) for v in (p_bias, n_gain, n_shift, d_bias, f_gain, f_shift)
    )
    u_bias = vectors[:, 1024:].reshape(-1)
    qkv_bias = jnp.stack([q_bias, jnp.zeros_like(q_bias), v_bias], axis=1).reshape(-1)

    token_share = to_share(tokens)
    full_qkv = gather_columns([w_query, w_key, w_value])
    full_proj = gather_rows(w_proj)
    full_up = gather_columns([w_up])
    full_down = gather_rows(w_down)
    dy = to_share(cotangent).astype(F32)
    stream = token_share.astype(F32)

    gathered = square_gather(token_share)
    qkv = (dot(gathered, full_qkv, ((1,), (0,))) + qkv_bias).astype(BF)
    queries, keys, values = (heads_of(qkv, i) for i in range(3))
    scale = HD ** (-0.5)
    same = (ids[:, None] == ids[None, :])[None]
    scores = jnp.einsum("qhd,khd->hqk", queries, keys, preferred_element_type=F32) * scale
    scores = jnp.where(same, scores, NEGATIVE)
    peak = jnp.max(scores, axis=2, keepdims=True)
    expo = jnp.exp(scores - peak)
    total = jnp.sum(expo, axis=2, keepdims=True)
    probs = (expo / total).astype(BF)
    logsum = peak + jnp.log(total)
    heads_out = jnp.einsum("hqk,khd->qhd", probs, values, preferred_element_type=F32)
    heads_out = heads_out.astype(BF).reshape(LEN, 512)

    def quarter(weights, where, axis):
        return lax.dynamic_slice_in_dim(weights, where * 512, 512, axis)

    attn = square_scatter(lambda w: dot(heads_out, quarter(full_proj, w, 1), ((1,), (0,)))) + p_bias
    resid = stream + attn
    stats = square_total(jnp.stack([jnp.sum(resid, axis=1), jnp.sum(resid * resid, axis=1)]))
    mean = stats[0] / width
    rstd_one = lax.rsqrt(stats[1] / width - mean * mean + EPS)[:, None]
    normed_one = (resid - mean[:, None]) * rstd_one
    hidden = normed_one * n_gain + n_shift
    hidden_low = square_gather(hidden.astype(BF))
    pre = dot(hidden_low, full_up, ((1,), (0,))) + u_bias
    act, gelu_back = jax.vjp(lambda inputs: jax.nn.gelu(inputs, approximate=True), pre)
    act_low = act.astype(BF)
    ffn = square_scatter(lambda w: dot(act_low, quarter(full_down, w, 1), ((1,), (0,)))) + d_bias

    resid_two = hidden + ffn
    scaled = dy * f_gain
    stats = square_total(
        jnp.stack(
            [
                jnp.sum(resid_two, axis=1),
                jnp.sum(resid_two * resid_two, axis=1),
                jnp.sum(scaled, axis=1),
                jnp.sum(scaled * resid_two, axis=1),
            ]
        )
    )
    mean = stats[0] / width
    rstd = lax.rsqrt(stats[1] / width - mean * mean + EPS)
    mean_e = stats[2] / width
    along = rstd * (stats[3] / width - mean * mean_e)
    normed_two = (resid_two - mean[:, None]) * rstd[:, None]
    layer_out = from_share((normed_two * f_gain + f_shift).astype(BF))
    grad_two = rstd[:, None] * (scaled - mean_e[:, None] - normed_two * along[:, None])
    grad_fgain = jnp.sum(dy * normed_two, axis=0)
    grad_fshift = jnp.sum(dy, axis=0)
    grad_ffn = grad_two.astype(BF)
    grad_dbias = jnp.sum(grad_ffn.astype(F32), axis=0)

    ffn_wide = square_gather(grad_ffn)
    grad_act = dot(ffn_wide, full_down, ((1,), (1,)))
    grad_pre = gelu_back(grad_act)[0].astype(BF)
    grad_down = dot(act_low, ffn_wide, ((0,), (0,))).astype(BF)
    grad_ubias = jnp.sum(grad_pre.astype(F32), axis=0)
    grad_hidden = square_scatter(lambda w: dot(grad_pre, quarter(full_up, w, 0), ((1,), (1,)))) + grad_two
    grad_up = dot(hidden_low, grad_pre, ((0,), (0,))).astype(BF)
    scaled = grad_hidden * n_gain
    stats = square_total(jnp.stack([jnp.sum(scaled, axis=1), jnp.sum(scaled * normed_one, axis=1)])) / width
    grad_one = rstd_one * (scaled - stats[0][:, None] - normed_one * stats[1][:, None])
    grad_ngain = jnp.sum(grad_hidden * normed_one, axis=0)
    grad_nshift = jnp.sum(grad_hidden, axis=0)
    grad_attn = grad_one.astype(BF)
    grad_pbias = jnp.sum(grad_attn.astype(F32), axis=0)

    attn_wide = square_gather(grad_attn)
    grad_heads = dot(attn_wide, full_proj, ((1,), (1,))).astype(BF)
    grad_proj = dot(heads_out, attn_wide, ((0,), (0,))).astype(BF)
    grad_out = grad_heads.reshape(LEN, 4, HD)
    probs_full = jnp.exp(
        jnp.where(same, jnp.einsum("qhd,khd->hqk", queries, keys, preferred_element_type=F32) * scale, NEGATIVE)
        - logsum
    )
    grad_probs = jnp.einsum("qhd,khd->hqk", grad_out, values, preferred_element_type=F32)
    inner = jnp.sum(probs_full * grad_probs, axis=2, keepdims=True)
    grad_scores = (probs_full * (grad_probs - inner)).astype(BF)
    back_query = jnp.einsum("hqk,khd->qhd", grad_scores, keys, preferred_element_type=F32) * scale
    back_key = jnp.einsum("hqk,qhd->khd", grad_scores, queries, preferred_element_type=F32) * scale
    back_value = jnp.einsum("hqk,qhd->khd", probs_full.astype(BF), grad_out, preferred_element_type=F32)
    grad_qkv = jnp.stack([b.astype(BF) for b in (back_query, back_key, back_value)], axis=2)
    sums_qkv = jnp.sum(grad_qkv.astype(F32), axis=0)
    grad_qkv = grad_qkv.reshape(LEN, 1536)
    back = square_scatter(lambda w: dot(grad_qkv, quarter(full_qkv, w, 0), ((1,), (1,))))
    grad_tokens = from_share((back + grad_one).astype(BF)).astype(F32)
    grad_wqkv = dot(gathered, grad_qkv, ((0,), (0,))).astype(BF)

    grad_down = scatter_rows(grad_down)
    (grad_up,) = scatter_columns(grad_up, 1)
    grad_proj = scatter_rows(grad_proj)
    grad_query, grad_key, grad_value = scatter_columns(grad_wqkv, 3)

    sums = jnp.concatenate(
        [
            v.reshape(4, -1)
            for v in (
                sums_qkv[:, 0], sums_qkv[:, 2], grad_pbias, grad_ngain, grad_nshift, grad_dbias, grad_fgain, grad_fshift, grad_ubias,
            )
        ],
        axis=1,
    )
    sums = jnp.sum(lax.all_to_all(sums, "z", 0, 0, tiled=True), axis=0)
    sums = sums + swap(sums, C_BIT)
    other = swap(sums, Y_BIT)
    sums = jnp.where(yi == 0, jnp.stack([sums, other]), jnp.stack([other, sums]))
    vecs = [sums[:, i * 128 : (i + 1) * 128].reshape(-1) for i in range(8)] + [sums[:, 1024:].reshape(-1)]

    totals = jnp.stack(
        [
            jnp.sum(valid * stream * stream),
            jnp.sum(valid * attn * attn),
            jnp.sum(valid * ffn * ffn),
            jnp.sum(valid) * 512,
        ]
    )
    for mask in (X_BIT, Z_LOW, Z_HIGH, C_BIT, Y_BIT):
        totals = totals + swap(totals, mask)
    norms = jnp.sqrt(totals[:3] / totals[3])
    return (
        layer_out, grad_tokens, grad_query, vecs[0], grad_key, grad_value, vecs[1], grad_proj, vecs[2], vecs[3], vecs[4],
        grad_up, vecs[8], grad_down, vecs[5], vecs[6], vecs[7], norms,
    )


def gather_features(piece):
    return lax.all_gather(piece, "col", axis=1, tiled=True)


def scatter_features(partial_sum):
    low = partial_sum.astype(jnp.bfloat16)
    return lax.psum_scatter(low, "col", scatter_dimension=1, tiled=True).astype(F32)


def row_totals(first, second):
    return lax.psum((first, second), "col")


def gather_weights(w_query, w_key, w_value, w_up, w_proj, w_down):
    inner = (
        lax.all_gather(w_query, "row", axis=0, tiled=True),
        lax.all_gather(w_key, "row", axis=0, tiled=True),
        lax.all_gather(w_value, "row", axis=0, tiled=True),
        lax.all_gather(w_up, "row", axis=0, tiled=True),
    )
    outer = (
        lax.all_gather(w_proj, "row", axis=1, tiled=True),
        lax.all_gather(w_down, "row", axis=1, tiled=True),
    )
    return (inner, outer)


def norm_shares(resid, gain, shift):
    width = resid.shape[1] * lax.axis_size("col")
    total, squares = row_totals(jnp.sum(resid, axis=1), jnp.sum(resid * resid, axis=1))
    mean = total / width
    rstd = lax.rsqrt(squares / width - mean * mean + EPS)
    normed = (resid - mean[:, None]) * rstd[:, None]
    return (normed * gain + shift, normed, rstd)


def norm_back(upstream, normed, rstd, gain):
    width = upstream.shape[1] * lax.axis_size("col")
    scaled = upstream * gain
    total, along = row_totals(jnp.sum(scaled, axis=1), jnp.sum(scaled * normed, axis=1))
    back = rstd[:, None] * (scaled - total[:, None] / width - normed * (along[:, None] / width))
    return (back, jnp.sum(upstream * normed, axis=0), jnp.sum(upstream, axis=0))


def attend_forward(pack):
    queries, keys, values, ids = pack
    scale = queries.shape[2] ** (-0.5)
    block = min(512, queries.shape[0])
    same = ids[:, None] == ids[None, :]
    outputs = []
    logsums = []
    for begin in range(0, queries.shape[0], block):
        scores = (
            jnp.einsum(
                "qhd,khd->hqk",
                queries[begin : begin + block],
                keys,
                preferred_element_type=jnp.float32,
            )
            * scale
        )
        scores = jnp.where(same[None, begin : begin + block], scores, NEGATIVE)
        peak = jnp.max(scores, axis=2, keepdims=True)
        expo = jnp.exp(scores - peak)
        total = jnp.sum(expo, axis=2, keepdims=True)
        probs = (expo / total).astype(jnp.bfloat16)
        outputs.append(
            jnp.einsum("hqk,khd->qhd", probs, values, preferred_element_type=jnp.float32)
        )
        logsums.append((peak + jnp.log(total))[:, :, 0])
    return (jnp.concatenate(outputs, axis=0), jnp.concatenate(logsums, axis=1))


def attend_back(pack):
    queries, keys, values, ids, logsum, grad_out = pack
    scale = queries.shape[2] ** (-0.5)
    block = min(512, queries.shape[0])
    same = ids[:, None] == ids[None, :]
    grad_keys = jnp.zeros(keys.shape, jnp.float32)
    grad_values = jnp.zeros(values.shape, jnp.float32)
    grad_queries = []
    for begin in range(0, queries.shape[0], block):
        query_rows = queries[begin : begin + block]
        grad_rows = grad_out[begin : begin + block]
        scores = (
            jnp.einsum("qhd,khd->hqk", query_rows, keys, preferred_element_type=jnp.float32) * scale
        )
        scores = jnp.where(same[None, begin : begin + block], scores, NEGATIVE)
        probs = jnp.exp(scores - logsum[:, begin : begin + block, None])
        grad_probs = jnp.einsum(
            "qhd,khd->hqk", grad_rows, values, preferred_element_type=jnp.float32
        )
        inner = jnp.sum(probs * grad_probs, axis=2, keepdims=True)
        grad_scores = (probs * (grad_probs - inner)).astype(jnp.bfloat16)
        grad_queries.append(
            jnp.einsum("hqk,khd->qhd", grad_scores, keys, preferred_element_type=jnp.float32)
            * scale
        )
        grad_keys = (
            grad_keys
            + jnp.einsum(
                "hqk,qhd->khd", grad_scores, query_rows, preferred_element_type=jnp.float32
            )
            * scale
        )
        grad_values = grad_values + jnp.einsum(
            "hqk,qhd->khd",
            probs.astype(jnp.bfloat16),
            grad_rows,
            preferred_element_type=jnp.float32,
        )
    return (jnp.concatenate(grad_queries, axis=0), grad_keys, grad_values)


def per_device(
    tokens,
    lengths,
    w_query,
    b_query,
    w_key,
    w_value,
    b_value,
    w_proj,
    b_proj,
    norm_gain,
    norm_shift,
    w_up,
    b_up,
    w_down,
    b_down,
    final_gain,
    final_shift,
    cotangent,
):
    rows, share = tokens.shape
    heads = w_query.shape[1] // HD
    ids = segment_ids(lengths)
    seq_count = ids.shape[0]
    valid = (ids.reshape(rows) != lengths.shape[1] - 1).astype(jnp.float32)[:, None]
    inner, outer = gather_weights(w_query, w_key, w_value, w_up, w_proj, w_down)
    full_query, full_key, full_value, full_up = inner
    full_proj, full_down = outer
    stream = tokens.astype(jnp.float32)
    gathered = gather_features(tokens)
    queries = (jnp.dot(gathered, full_query, preferred_element_type=jnp.float32) + b_query).astype(
        jnp.bfloat16
    )
    keys = jnp.dot(gathered, full_key, preferred_element_type=jnp.float32).astype(jnp.bfloat16)
    values = (jnp.dot(gathered, full_value, preferred_element_type=jnp.float32) + b_value).astype(
        jnp.bfloat16
    )
    shape = (seq_count, LEN, heads, HD)
    query_seq = queries.reshape(shape)
    key_seq = keys.reshape(shape)
    value_seq = values.reshape(shape)
    mixed, logsum = lax.map(attend_forward, (query_seq, key_seq, value_seq, ids))
    heads_out = mixed.reshape(rows, heads * HD).astype(jnp.bfloat16)
    attn = (
        scatter_features(jnp.dot(heads_out, full_proj, preferred_element_type=jnp.float32)) + b_proj
    )
    hidden, normed_one, rstd_one = norm_shares(stream + attn, norm_gain, norm_shift)
    hidden_low = gather_features(hidden.astype(jnp.bfloat16))
    pre = jnp.dot(hidden_low, full_up, preferred_element_type=jnp.float32) + b_up
    act, gelu_back = jax.vjp(lambda inputs: jax.nn.gelu(inputs, approximate=True), pre)
    act_low = act.astype(jnp.bfloat16)
    ffn = scatter_features(jnp.dot(act_low, full_down, preferred_element_type=jnp.float32)) + b_down
    result, normed_two, rstd_two = norm_shares(hidden + ffn, final_gain, final_shift)
    totals = lax.psum(
        (
            jnp.sum(valid * stream * stream),
            jnp.sum(valid * attn * attn),
            jnp.sum(valid * ffn * ffn),
            jnp.sum(valid) * share,
        ),
        ("row", "col"),
    )
    norms = jnp.sqrt(jnp.stack([totals[0], totals[1], totals[2]]) / totals[3])
    back_inner, back_outer = gather_weights(w_query, w_key, w_value, w_up, w_proj, w_down)
    full_query, full_key, full_value, full_up = back_inner
    full_proj, full_down = back_outer
    grad_two, grad_fgain, grad_fshift = norm_back(
        cotangent.astype(jnp.float32), normed_two, rstd_two, final_gain
    )
    grad_ffn = grad_two.astype(jnp.bfloat16)
    grad_dbias = jnp.sum(grad_ffn.astype(jnp.float32), axis=0)
    ffn_wide = gather_features(grad_ffn)
    grad_down = jnp.einsum("tf,td->fd", act_low, ffn_wide, preferred_element_type=jnp.float32)
    grad_act = jnp.einsum("td,fd->tf", ffn_wide, full_down, preferred_element_type=jnp.float32)
    grad_pre = gelu_back(grad_act)[0].astype(jnp.bfloat16)
    grad_ubias = jnp.sum(grad_pre.astype(jnp.float32), axis=0)
    grad_up = jnp.einsum("td,tf->df", hidden_low, grad_pre, preferred_element_type=jnp.float32)
    grad_hidden = (
        scatter_features(
            jnp.einsum("tf,df->td", grad_pre, full_up, preferred_element_type=jnp.float32)
        )
        + grad_two
    )
    grad_one, grad_ngain, grad_nshift = norm_back(grad_hidden, normed_one, rstd_one, norm_gain)
    grad_attn = grad_one.astype(jnp.bfloat16)
    grad_pbias = jnp.sum(grad_attn.astype(jnp.float32), axis=0)
    attn_wide = gather_features(grad_attn)
    grad_proj = jnp.einsum("th,td->hd", heads_out, attn_wide, preferred_element_type=jnp.float32)
    grad_heads = jnp.einsum(
        "td,hd->th", attn_wide, full_proj, preferred_element_type=jnp.float32
    ).astype(jnp.bfloat16)
    back_query, back_key, back_value = lax.map(
        attend_back, (query_seq, key_seq, value_seq, ids, logsum, grad_heads.reshape(shape))
    )
    grad_queries = back_query.reshape(rows, heads * HD).astype(jnp.bfloat16)
    grad_keys = back_key.reshape(rows, heads * HD).astype(jnp.bfloat16)
    grad_values = back_value.reshape(rows, heads * HD).astype(jnp.bfloat16)
    grad_qbias = jnp.sum(grad_queries.astype(jnp.float32), axis=0)
    grad_vbias = jnp.sum(grad_values.astype(jnp.float32), axis=0)
    grad_query = jnp.einsum("td,th->dh", gathered, grad_queries, preferred_element_type=jnp.float32)
    grad_key = jnp.einsum("td,th->dh", gathered, grad_keys, preferred_element_type=jnp.float32)
    grad_value = jnp.einsum("td,th->dh", gathered, grad_values, preferred_element_type=jnp.float32)
    partial_back = (
        jnp.einsum("th,dh->td", grad_queries, full_query, preferred_element_type=jnp.float32)
        + jnp.einsum("th,dh->td", grad_keys, full_key, preferred_element_type=jnp.float32)
        + jnp.einsum("th,dh->td", grad_values, full_value, preferred_element_type=jnp.float32)
    )
    grad_tokens = scatter_features(partial_back) + grad_one
    grad_query, grad_key, grad_value, grad_up = (
        lax.psum_scatter(
            grad_query.astype(jnp.bfloat16), "row", scatter_dimension=0, tiled=True
        ).astype(jnp.float32),
        lax.psum_scatter(
            grad_key.astype(jnp.bfloat16), "row", scatter_dimension=0, tiled=True
        ).astype(jnp.float32),
        lax.psum_scatter(
            grad_value.astype(jnp.bfloat16), "row", scatter_dimension=0, tiled=True
        ).astype(jnp.float32),
        lax.psum_scatter(
            grad_up.astype(jnp.bfloat16), "row", scatter_dimension=0, tiled=True
        ).astype(jnp.float32),
    )
    grad_proj, grad_down = (
        lax.psum_scatter(
            grad_proj.astype(jnp.bfloat16), "row", scatter_dimension=1, tiled=True
        ).astype(jnp.float32),
        lax.psum_scatter(
            grad_down.astype(jnp.bfloat16), "row", scatter_dimension=1, tiled=True
        ).astype(jnp.float32),
    )
    vectors = lax.psum(
        (
            grad_qbias,
            grad_vbias,
            grad_pbias,
            grad_ngain,
            grad_nshift,
            grad_ubias,
            grad_dbias,
            grad_fgain,
            grad_fshift,
        ),
        "row",
    )
    return (
        result.astype(jnp.bfloat16),
        grad_tokens,
        grad_query,
        vectors[0],
        grad_key,
        grad_value,
        vectors[1],
        grad_proj,
        vectors[2],
        vectors[3],
        vectors[4],
        grad_up,
        vectors[5],
        grad_down,
        vectors[6],
        vectors[7],
        vectors[8],
        norms,
    )


def placements(row, col):
    grid, turned, share = P(row, col), P(col, row), P(col)
    args = (
        grid, P(row, None), grid, share, grid, grid, share, turned, share, share, share, grid, share, turned, share, share, share, grid,
    )
    outs = (
        grid, grid, grid, share, grid, grid, share, turned, share, share, share, grid, share, turned, share, share, share, P(),
    )
    return (args, outs)


def solution(mesh):
    if mesh.shape["row"] == 4 and mesh.shape["col"] == 8:
        mesh = Mesh(mesh.devices.reshape(2, 2, 4, 2), AXES)
        args, outs = placements(("y", "c"), ("z", "x"))
        body = square_device
    else:
        args, outs = placements("row", "col")
        body = per_device
    return jax.shard_map(body, mesh=mesh, in_specs=args, out_specs=outs, check_vma=False)
```

```python
import functools

import jax
import jax.numpy as jnp
from jax import lax
from jax.experimental import pallas as pl
from jax.experimental.pallas import tpu as pltpu
from jax.sharding import Mesh
from jax.sharding import PartitionSpec as P

HD = 128
LEN = 1024
EPS = 1e-06
NEGATIVE = -1000000000.0
BF = jnp.bfloat16
F32 = jnp.float32


def segment_ids(lengths):
    slots = lengths.shape[1]
    ends = jnp.cumsum(lengths, axis=1)
    places = jnp.arange(LEN, dtype=jnp.int32)
    hits = (places[None, :, None] >= ends[:, None, : slots - 1]).astype(jnp.int32)
    return jnp.sum(hits, axis=2)


AXES = ("y", "c", "z", "x")
X_BIT, Z_LOW, Z_HIGH, C_BIT, Y_BIT = 1, 2, 4, 8, 16
XY_BIT = X_BIT | Y_BIT
QUARTER = 512
HALF = LEN // 2
WIDTH = 2048
NN, NT, TN = ((1,), (0,)), ((1,), (1,)), ((0,), (0,))


def swap(piece, mask):
    return lax.ppermute(piece, AXES, [(i, i ^ mask) for i in range(32)])


def dot(left, right, dims):
    return lax.dot_general(left, right, (dims, ((), ())), preferred_element_type=F32)


def call(body, grid, spot, ins, in_specs, outs, out_specs, scratch, flops, size):
    return pl.pallas_call(
        body,
        grid_spec=pltpu.PrefetchScalarGridSpec(
            num_scalar_prefetch=1, grid=grid, in_specs=in_specs, out_specs=out_specs, scratch_shapes=scratch
        ),
        out_shape=outs,
        compiler_params=pltpu.CompilerParams(
            dimension_semantics=("arbitrary",) * len(grid), vmem_limit_bytes=56 * 1024 * 1024
        ),
        cost_estimate=pl.CostEstimate(flops=flops, bytes_accessed=size, transcendentals=0),
    )(spot, *ins)


def shape_of(*shape, dtype=F32):
    return jax.ShapeDtypeStruct(shape, dtype)


def fixed(shape):
    return pl.BlockSpec(shape, lambda *_: (0,) * len(shape))


def pick(low, high, t):
    return jnp.where(t == 0, low[...], high[...])


SLOTS = (0, 2, 1, 3)


def wide_body(by_rows, finish, count, spot, *refs):
    pieces, weights, rest = refs[:8], refs[8], refs[9:]
    extra, outs, kept = rest[: -1 - count], rest[-1 - count : -1], rest[-1]
    t = pl.program_id(1)

    @pl.when(t == 0)
    def _():
        for slot, mask in enumerate(SLOTS):
            start = pl.multiple_of((spot[0] ^ mask) * 128, 128)
            for block in range(4):
                y, c = divmod(block, 2)
                y = y ^ spot[1]
                at = slot * QUARTER + block * 128
                if by_rows:
                    kept[:, at : at + 128] = weights[0, c, :, pl.ds(pl.multiple_of(y * 512 + start, 128), 128)]
                else:
                    kept[at : at + 128, :] = weights[0, c, y, pl.ds(start, 128), :]

    total = None
    for slot in range(4):
        tile = pick(pieces[2 * slot], pieces[2 * slot + 1], t)
        part = slice(slot * QUARTER, slot * QUARTER + QUARTER)
        term = dot(tile, kept[:, part], NT) if by_rows else dot(tile, kept[part, :], NN)
        total = term if total is None else total + term
    finish(total, extra, outs)


def wide(pieces, weights, spot, by_rows, finish, extra, count):
    if by_rows:
        n = weights.shape[1]
        weights = weights.reshape(4, 2, n, 1024)
        kept = pltpu.VMEM((n, WIDTH), BF)
    else:
        n = weights.shape[2]
        weights = weights.reshape(4, 2, 2, 512, n)
        kept = pltpu.VMEM((WIDTH, n), BF)
    block = (1,) + weights.shape[1:]
    tail = (0,) * (len(block) - 1)
    bias = pl.BlockSpec((1, n), lambda z, t, *_: (0, z))
    tile = pl.BlockSpec((HALF, n), lambda z, t, *_: (t, z))
    return call(
        functools.partial(wide_body, by_rows, finish, count),
        (4, 2),
        spot,
        (*pieces, weights, *extra),
        [fixed(p.shape) for p in pieces]
        + [pl.BlockSpec(block, lambda z, t, *_: (z,) + tail)]
        + [bias if e.shape[0] == 1 else tile for e in extra],
        [shape_of(LEN, 4 * n, dtype=BF)] * count,
        [tile] * count,
        [kept],
        2 * LEN * WIDTH * 4 * n,
        2 * (LEN * WIDTH + WIDTH * 4 * n + LEN * 4 * n),
    )


def finish_bias(total, extra, outs):
    outs[0][...] = (total + extra[0][...]).astype(BF)


def finish_plain(total, extra, outs):
    outs[0][...] = total.astype(BF)


def finish_gelu(total, extra, outs):
    pre = total + extra[0][...]
    square = pre * pre
    bend = jnp.tanh(0.7978845608028654 * pre * (1.0 + 0.044715 * square))
    rise = 0.5 * (1.0 + bend)
    outs[0][...] = (pre * rise).astype(BF)
    slope = 0.7978845608028654 * (1.0 + 0.134145 * square)
    outs[1][...] = (rise + 0.5 * pre * (1.0 - bend * bend) * slope).astype(BF)


def finish_slope(total, extra, outs):
    outs[0][...] = (total * extra[0][...].astype(F32)).astype(BF)


def partial_body(by_rows, n, spot, local, *rest):
    weights, (low, high) = rest[:-2], rest[-2:]
    t = pl.program_id(0)
    total = None
    for z in range(4):
        tile = local[:, z * n : (z + 1) * n]
        if by_rows:
            kept = jnp.concatenate([weights[y][z, c] for y in range(2) for c in range(2)], axis=1)
            term = dot(tile, kept, NN)
        else:
            kept = jnp.concatenate([weights[0][z, c, y ^ spot[1]] for y in range(2) for c in range(2)], axis=0)
            term = dot(tile, kept, NT)
        total = term if total is None else total + term

    @pl.when(t == 0)
    def _():
        low[...] = total.astype(low.dtype)

    @pl.when(t == 1)
    def _():
        high[...] = total.astype(high.dtype)


def partial(local, weights, spot, by_rows, mask, low, high):
    n = local.shape[1] // 4
    if by_rows:
        weights = weights.reshape(4, 2, n, 1024)
        specs = [
            pl.BlockSpec((4, 2, n, 128), functools.partial(lambda y, t, p: (0, 0, 0, (y ^ p[1]) * 4 + (p[0] ^ mask)), y))
            for y in range(2)
        ]
        ins = (weights, weights)
    else:
        weights = weights.reshape(4, 2, 2, 512, n)
        specs = [pl.BlockSpec((4, 2, 2, 128, n), lambda t, p: (0, 0, 0, p[0] ^ mask, 0))]
        ins = (weights,)
    return call(
        functools.partial(partial_body, by_rows, n),
        (2,),
        spot,
        (local, *ins),
        [pl.BlockSpec((HALF, 4 * n), lambda t, p: (t, 0))] + specs,
        [shape_of(HALF, QUARTER, dtype=low), shape_of(HALF, QUARTER, dtype=high)],
        [fixed((HALF, QUARTER))] * 2,
        [],
        2 * LEN * QUARTER * 4 * n,
        2 * (LEN * 4 * n + QUARTER * 4 * n + LEN * QUARTER),
    )


def grad_body(by_rows, spot, *refs):
    pieces, local, out = refs[:8], refs[8], refs[9]
    for slot, mask in enumerate(SLOTS):
        start = pl.multiple_of((spot[0] ^ mask) * 128, 128)

        def term(piece, tile):
            return dot(tile, piece, TN) if by_rows else dot(piece, tile, TN)

        total = term(pieces[2 * slot][...], local[:HALF, :]) + term(pieces[2 * slot + 1][...], local[HALF:, :])
        for block in range(4):
            y, c = divmod(block, 2)
            y = y ^ spot[1]
            part = slice(block * 128, block * 128 + 128)
            if by_rows:
                out[0, c, :, pl.ds(pl.multiple_of(y * 512 + start, 128), 128)] = total[:, part].astype(BF)
            else:
                out[0, c, y, pl.ds(start, 128), :] = total[part, :].astype(BF)


def grad(pieces, local, spot, by_rows):
    n = local.shape[1] // 4
    shape = (4, 2, n, 1024) if by_rows else (4, 2, 2, 512, n)
    tail = (0,) * (len(shape) - 1)
    out = call(
        functools.partial(grad_body, by_rows),
        (4,),
        spot,
        (*pieces, local),
        [fixed(p.shape) for p in pieces] + [pl.BlockSpec((LEN, n), lambda z, *_: (0, z))],
        shape_of(*shape, dtype=BF),
        pl.BlockSpec((1,) + shape[1:], lambda z, *_: (z,) + tail),
        [],
        2 * LEN * WIDTH * 4 * n,
        2 * (LEN * WIDTH + WIDTH * 4 * n + LEN * 4 * n),
    )
    return out.reshape(8, n, 1024) if by_rows else out.reshape(8, 1024, n)


SCALE = HD ** (-0.5)
LOG2E = 1.4426950408889634
QUERY_BLOCK = 512


def forward_body(spot, queries, whole, ids_row, ids_column, out, logsum):
    scores = dot(whole[:, HD : 2 * HD], queries[:, :HD], NT)
    scores = jnp.where(ids_column[...] == ids_row[...], scores, NEGATIVE)
    peak = jnp.max(scores, axis=0, keepdims=True)
    expo = jnp.exp2((scores - peak) * (SCALE * LOG2E))
    total = jnp.sum(expo, axis=0, keepdims=True)
    probs = (expo * (1.0 / total)).astype(BF)
    mixed = dot(whole[:, 2 * HD :], probs, TN)
    out[...] = mixed.T.astype(BF)
    logsum[0] = peak * (SCALE * LOG2E) + jnp.log2(total)


def head_specs():
    return [
        pl.BlockSpec((QUERY_BLOCK, 3 * HD), lambda h, q, p: (q, h)),
        pl.BlockSpec((LEN, 3 * HD), lambda h, q, p: (0, h)),
        pl.BlockSpec((1, QUERY_BLOCK), lambda h, q, p: (0, q)),
        pl.BlockSpec((LEN, 1), lambda h, q, p: (0, 0)),
    ]


def attention(qkv, ids_row, ids_column, spot):
    return call(
        forward_body,
        (4, LEN // QUERY_BLOCK),
        spot,
        (qkv, qkv, ids_row, ids_column),
        head_specs(),
        [shape_of(LEN, QUARTER, dtype=BF), shape_of(4, 1, LEN)],
        [
            pl.BlockSpec((QUERY_BLOCK, HD), lambda h, q, p: (q, h)),
            pl.BlockSpec((1, 1, QUERY_BLOCK), lambda h, q, p: (h, 0, q)),
        ],
        [],
        64 * LEN * LEN * HD,
        LEN * 4 * HD * 8,
    )


def backward_body(spot, queries, whole, ids_row, ids_column, logsum, grad_out, out, grad_keys, grad_values):
    q = pl.program_id(1)
    block = queries.shape[0]
    keys = whole[:, HD : 2 * HD]
    values = whole[:, 2 * HD :]
    scores = dot(keys, queries[:, :HD], NT) * (SCALE * LOG2E)
    scores = jnp.where(ids_column[...] == ids_row[...], scores, NEGATIVE)
    probs = jnp.exp2(scores - logsum[0])
    grad_probs = dot(values, grad_out[...], NT)
    inner = jnp.sum(probs * grad_probs, axis=0, keepdims=True)
    grad_scores = (probs * (grad_probs - inner)).astype(BF)
    back_query = dot(keys, grad_scores, TN)
    out[pl.ds(q * block, block), :HD] = (back_query.T * SCALE).astype(BF)
    back_key = dot(grad_scores, queries[:, :HD], NN)
    back_value = dot(probs.astype(BF), grad_out[...], NN)

    @pl.when(q == 0)
    def _():
        grad_keys[...] = back_key
        grad_values[...] = back_value

    @pl.when(q > 0)
    def _():
        grad_keys[...] += back_key
        grad_values[...] += back_value

    @pl.when(q == pl.num_programs(1) - 1)
    def _():
        out[:, HD : 2 * HD] = (grad_keys[...] * SCALE).astype(BF)
        out[:, 2 * HD :] = grad_values[...].astype(BF)


def attention_back(qkv, ids_row, ids_column, logsum, grad_heads, spot):
    return call(
        backward_body,
        (4, LEN // QUERY_BLOCK),
        spot,
        (qkv, qkv, ids_row, ids_column, logsum, grad_heads),
        head_specs()
        + [
            pl.BlockSpec((1, 1, QUERY_BLOCK), lambda h, q, p: (h, 0, q)),
            pl.BlockSpec((QUERY_BLOCK, HD), lambda h, q, p: (q, h)),
        ],
        shape_of(LEN, 12 * HD, dtype=BF),
        pl.BlockSpec((LEN, 3 * HD), lambda h, q, p: (0, h)),
        [pltpu.VMEM((LEN, HD), F32), pltpu.VMEM((LEN, HD), F32)],
        120 * LEN * LEN * HD,
        LEN * 4 * HD * 16,
    )


def row_sum(value):
    folded = value[:, :128] + value[:, 128:256] + value[:, 256:384] + value[:, 384:512]
    return jnp.sum(folded.T, axis=0, keepdims=True)


def rows_of(values):
    rows = [row_sum(v) for v in values]
    return jnp.concatenate(rows + [jnp.zeros_like(rows[0])] * (8 - len(rows)), axis=0)


def columns_of(rows):
    return rows.T


def column_sums(values):
    sums = [jnp.sum(v, axis=0, keepdims=True) for v in values]
    return jnp.concatenate(sums + [jnp.zeros_like(sums[0])] * (8 - len(sums)), axis=0)


def add_columns(ref, t, values):
    sums = column_sums(values)

    @pl.when(t == 0)
    def _():
        ref[...] = sums

    @pl.when(t > 0)
    def _():
        ref[...] += sums


def moments_of(stats):
    total = (stats[0][...] + stats[1][...] + stats[2][...] + stats[3][...]) / WIDTH
    mean = total[0:1]
    return mean, lax.rsqrt(total[1:2] - mean * mean + EPS), total


def summed(refs, t):
    own, near, last = (pick(refs[2 * i], refs[2 * i + 1], t).astype(F32) for i in range(3))
    return own + near + last


HALVES = fixed((HALF, QUARTER))
TILE = pl.BlockSpec((HALF, QUARTER), lambda t, p: (t, 0))
STATS = pl.BlockSpec((8, HALF), lambda t, p: (0, t))
VECTOR = fixed((1, QUARTER))
SUMS = fixed((8, QUARTER))


def elementwise(body, spot, ins, in_specs, outs, out_specs):
    return call(body, (2,), spot, ins, in_specs, outs, out_specs, [], 20 * LEN * QUARTER, 16 * LEN * QUARTER)


def norm_one_sums(spot, *refs):
    parts, (stream, bias, resid, stats) = refs[:6], refs[6:]
    attn = summed(parts, pl.program_id(0)) + bias[...]
    total = stream[...].astype(F32) + attn
    resid[...] = total
    stats[...] = rows_of([total, total * total, attn * attn, jnp.square(stream[...].astype(F32))])


def write_halves(t, low, high, value):
    @pl.when(t == 0)
    def _():
        low[...] = value

    @pl.when(t == 1)
    def _():
        high[...] = value


def norm_one(spot, resid, s0, s1, s2, s3, gain, shift, low, high, moments):
    mean, rstd, _ = moments_of((s0, s1, s2, s3))
    rows = jnp.concatenate([mean, rstd] + [mean] * 6, axis=0)
    moments[...] = rows
    columns = columns_of(rows)
    hidden = (resid[...] - columns[:, 0:1]) * columns[:, 1:2] * gain[...] + shift[...]
    write_halves(pl.program_id(0), low, high, hidden.astype(BF))


def norm_two_sums(spot, *refs):
    parts = refs[:6]
    bias, resid, moments, gain, shift, dy, gain_two, resid_two, stats = refs[6:]
    ffn = summed(parts, pl.program_id(0)) + bias[...]
    columns = columns_of(moments[...])
    hidden = (resid[...] - columns[:, 0:1]) * columns[:, 1:2] * gain[...] + shift[...]
    total = hidden + ffn
    resid_two[...] = total
    scaled = dy[...].astype(F32) * gain_two[...]
    stats[...] = rows_of([total, total * total, scaled, scaled * total, ffn * ffn])


def norm_two(spot, resid_two, s0, s1, s2, s3, dy, gain, shift, layer_out, grad_two, low, high, sums):
    mean, rstd, total = moments_of((s0, s1, s2, s3))
    mean_e = total[2:3]
    along = rstd * (total[3:4] - mean * mean_e)
    columns = columns_of(jnp.concatenate([mean, rstd, mean_e, along] + [mean] * 4, axis=0))
    normed = (resid_two[...] - columns[:, 0:1]) * columns[:, 1:2]
    upstream = dy[...].astype(F32)
    layer_out[...] = (normed * gain[...] + shift[...]).astype(BF)
    back = columns[:, 1:2] * (upstream * gain[...] - columns[:, 2:3] - normed * columns[:, 3:4])
    grad_two[...] = back
    rounded = back.astype(BF)
    t = pl.program_id(0)
    write_halves(t, low, high, rounded)
    add_columns(sums, t, [upstream * normed, upstream, rounded.astype(F32)])


def back_one_sums(spot, *refs):
    parts = refs[:6]
    grad_two, resid, moments, gain, grad_hidden, stats, sums = refs[6:]
    t = pl.program_id(0)
    upstream = summed(parts, t) + grad_two[...]
    grad_hidden[...] = upstream
    columns = columns_of(moments[...])
    normed = (resid[...] - columns[:, 0:1]) * columns[:, 1:2]
    scaled = upstream * gain[...]
    stats[...] = rows_of([scaled, scaled * normed])
    add_columns(sums, t, [upstream * normed, upstream])


def back_one(spot, grad_hidden, s0, s1, s2, s3, resid, moments, gain, grad_one, low, high, sums):
    total = (s0[...] + s1[...] + s2[...] + s3[...]) / WIDTH
    means = columns_of(total)
    columns = columns_of(moments[...])
    normed = (resid[...] - columns[:, 0:1]) * columns[:, 1:2]
    back = columns[:, 1:2] * (grad_hidden[...] * gain[...] - means[:, 0:1] - normed * means[:, 1:2])
    grad_one[...] = back
    rounded = back.astype(BF)
    t = pl.program_id(0)
    write_halves(t, low, high, rounded)
    add_columns(sums, t, [rounded.astype(F32)])


def finish_back(spot, *refs):
    parts, (grad_one, out) = refs[:6], refs[6:]
    out[...] = (summed(parts, pl.program_id(0)) + grad_one[...]).astype(BF)


def pass_on(spot, first, second, third, fourth, low, high):
    low[...] = (first[...] + second[...].astype(F32)).astype(BF)
    high[...] = (third[...] + fourth[...].astype(F32)).astype(BF)


def tie(value, *others):
    return lax.optimization_barrier((value, *others))[0]


def to_share(piece, yi):
    own = lax.dynamic_slice_in_dim(piece, yi * 128, 128, 1)
    other = swap(lax.dynamic_slice_in_dim(piece, (1 - yi) * 128, 128, 1), Y_BIT)
    return own, other


def to_share_rest(own, other, yi):
    both = jnp.where(yi == 0, jnp.stack([own, other]), jnp.stack([other, own])).reshape(4, LEN, 128)
    return lax.all_to_all(both, "z", 0, 2, tiled=True)[0]


def from_share(share, yi):
    parts = lax.all_to_all(share[None], "z", 2, 0, tiled=True).reshape(2, 2 * LEN, 128)
    own = lax.dynamic_index_in_dim(parts, yi, 0, False)
    other = swap(lax.dynamic_index_in_dim(parts, 1 - yi, 0, False), Y_BIT)
    return own, other


def side_by_side(own, other, yi, axis):
    return jnp.where(yi == 0, jnp.concatenate([own, other], axis), jnp.concatenate([other, own], axis))


def square_gather(low, high):
    x_low = swap(low, X_BIT)
    y_high = swap(high, Y_BIT)
    x_high = swap(high, X_BIT)
    y_low = swap(low, Y_BIT)
    xy_low = swap(x_low, Y_BIT)
    xy_high = swap(y_high, X_BIT)
    return (low, high, x_low, x_high, y_low, y_high, xy_low, xy_high)


def square_scatter(local, weights, spot, by_rows, before_own=()):
    term = functools.partial(partial, local, weights, spot, by_rows)
    far_low, far_high = term(3, BF, BF)
    far_low = swap(far_low, X_BIT)
    far_high = swap(far_high, Y_BIT)
    near_low, x_high = term(2, BF, F32)
    near_low = swap(near_low, X_BIT)
    y_low, near_high = term(1, F32, BF)
    near_high = swap(near_high, Y_BIT)
    half = fixed((HALF, QUARTER))
    last_low, last_high = call(
        pass_on, (1,), spot, (y_low, far_low, x_high, far_high), [half] * 4, [shape_of(HALF, QUARTER, dtype=BF)] * 2,
        [half] * 2, [], LEN * QUARTER, 8 * LEN * QUARTER,
    )
    last_low = swap(last_low, Y_BIT)
    last_high = swap(last_high, X_BIT)
    if before_own:
        local = tie(local, *before_own)
    own_low, own_high = partial(local, weights, spot, by_rows, 0, F32, F32)
    return (own_low, own_high, near_low, near_high, last_low, last_high)


def square_stats(stats):
    return (stats, swap(stats, X_BIT), swap(stats, Y_BIT), swap(stats, XY_BIT))


def halve_columns(pieces, yi):
    n = pieces[0].shape[1] // 2
    own = jnp.concatenate([lax.dynamic_slice_in_dim(p, yi * n, n, 1) for p in pieces], axis=1)
    other = jnp.concatenate([lax.dynamic_slice_in_dim(p, (1 - yi) * n, n, 1) for p in pieces], axis=1)
    return jnp.concatenate([own, swap(other, Y_BIT)], axis=0)


def halve_rows(piece, yi):
    n = piece.shape[0] // 2
    own = lax.dynamic_slice_in_dim(piece, yi * n, n, 0)
    other = lax.dynamic_slice_in_dim(piece, (1 - yi) * n, n, 0)
    return jnp.concatenate([own, swap(other, Y_BIT)], axis=1)


def gather_zc(piece):
    return lax.all_gather(piece, ("z", "c"), axis=0)


def scatter_zc(full):
    return lax.psum_scatter(full, ("z", "c"), scatter_dimension=0)


def restore_columns(piece, count, yi):
    other = swap(piece[512:], Y_BIT)
    n = piece.shape[1] // count
    return [
        side_by_side(piece[:512, i * n : (i + 1) * n], other[:, i * n : (i + 1) * n], yi, 1).astype(F32)
        for i in range(count)
    ]


def restore_rows(piece, yi):
    return side_by_side(piece[:, :512], swap(piece[:, 512:], Y_BIT), yi, 0).astype(F32)


def square_device(
    tokens, lengths, w_query, b_query, w_key, w_value, b_value, w_proj, b_proj, norm_gain, norm_shift,
    w_up, b_up, w_down, b_down, final_gain, final_shift, cotangent,
):
    yi = lax.axis_index("y")
    zi = lax.axis_index("z")
    spot = jnp.stack([lax.axis_index("x") * 2 + yi, yi]).astype(jnp.int32)

    token_own, token_other = to_share(tokens, yi)
    half_qkv = halve_columns([w_query, w_key, w_value], yi)
    half_proj = halve_rows(tie(w_proj, half_qkv), yi)
    half_up = halve_columns([tie(w_up, half_proj)], yi)
    half_down = halve_rows(tie(w_down, half_up), yi)
    full_qkv = gather_zc(half_qkv)
    token_share = to_share_rest(token_own, token_other, yi)
    full_proj = gather_zc(half_proj)
    full_up = gather_zc(half_up)
    full_down = gather_zc(half_down)
    dy_own, dy_other = to_share(tie(cotangent, half_down), yi)
    dy = to_share_rest(dy_own, dy_other, yi)

    both = side_by_side(lengths, swap(lengths, Y_BIT), yi, 0)
    ids = segment_ids(lax.dynamic_slice_in_dim(both, zi, 1, 0))[0]
    valid = (ids != lengths.shape[1] - 1).astype(F32)
    ids_row, ids_column = ids[None], ids[:, None]

    vectors = jnp.concatenate(
        [v.reshape(2, -1) for v in (b_query, b_value, b_proj, norm_gain, norm_shift, b_down, final_gain, final_shift, b_up)],
        axis=1,
    )
    vectors = lax.dynamic_slice_in_dim(vectors, yi, 1, 0)
    vectors = lax.all_to_all(jnp.broadcast_to(vectors, (4, vectors.shape[1])), "z", 0, 0, tiled=True)
    small = [vectors[:, i * 128 : (i + 1) * 128] for i in range(8)]
    q_bias, v_bias = small[:2]
    p_bias, n_gain, n_shift, d_bias, f_gain, f_shift = (v.reshape(1, QUARTER) for v in small[2:])
    u_bias = vectors[:, 1024:].reshape(1, -1)
    qkv_bias = jnp.stack([q_bias, jnp.zeros_like(q_bias), v_bias], axis=1).reshape(1, -1)

    gathered = square_gather(token_share[:HALF], token_share[HALF:])
    (qkv,) = wide(gathered, full_qkv, spot, False, finish_bias, (qkv_bias,), 1)
    heads_out, logsum = attention(qkv, ids_row, ids_column, spot)
    full = shape_of(LEN, QUARTER)
    low_half = shape_of(HALF, QUARTER, dtype=BF)
    stats_shape = shape_of(8, LEN)
    sums_shape = shape_of(8, QUARTER)

    parts = square_scatter(heads_out, full_proj, spot, True)
    resid, stats_one = elementwise(
        norm_one_sums, spot, (*parts, token_share, p_bias), [HALVES] * 6 + [TILE, VECTOR], [full, stats_shape], [TILE, STATS]
    )
    hidden_low, hidden_high, moments = elementwise(
        norm_one, spot, (resid, *square_stats(stats_one), n_gain, n_shift), [TILE] + [STATS] * 4 + [VECTOR] * 2,
        [low_half, low_half, stats_shape], [HALVES, HALVES, STATS],
    )
    hidden_wide = square_gather(hidden_low, hidden_high)
    act, slope = wide(hidden_wide, full_up, spot, False, finish_gelu, (u_bias,), 2)
    parts = square_scatter(act, full_down, spot, True)
    resid_two, stats_two = elementwise(
        norm_two_sums, spot, (*parts, d_bias, resid, moments, n_gain, n_shift, dy, f_gain),
        [HALVES] * 6 + [VECTOR, TILE, STATS, VECTOR, VECTOR, TILE, VECTOR], [full, stats_shape], [TILE, STATS],
    )
    layer_share, grad_two, ffn_low, ffn_high, sums_two = elementwise(
        norm_two, spot, (resid_two, *square_stats(stats_two), dy, f_gain, f_shift),
        [TILE] + [STATS] * 4 + [TILE, VECTOR, VECTOR],
        [shape_of(LEN, QUARTER, dtype=BF), full, low_half, low_half, sums_shape], [TILE, TILE, HALVES, HALVES, SUMS],
    )
    ffn_wide = square_gather(ffn_low, ffn_high)
    layer_own, layer_other = from_share(layer_share, yi)
    layer_out = side_by_side(layer_own, layer_other, yi, 1)

    (grad_pre,) = wide(ffn_wide, full_down, spot, True, finish_slope, (slope,), 1)
    grad_down = grad(ffn_wide, act, spot, True)
    grad_up = grad(hidden_wide, grad_pre, spot, False)
    parts = square_scatter(grad_pre, full_up, spot, False, (grad_down,))
    sum_down = scatter_zc(grad_down)
    grad_ubias = jnp.sum(grad_pre.astype(F32), axis=0)
    grad_hidden, stats_back, sums_back = elementwise(
        back_one_sums, spot, (*parts, grad_two, resid, moments, n_gain),
        [HALVES] * 6 + [TILE, TILE, STATS, VECTOR], [full, stats_shape, sums_shape], [TILE, STATS, SUMS],
    )
    grad_one, attn_low, attn_high, sums_attn = elementwise(
        back_one, spot, (grad_hidden, *square_stats(stats_back), resid, moments, n_gain),
        [TILE] + [STATS] * 4 + [TILE, STATS, VECTOR],
        [full, low_half, low_half, sums_shape], [TILE, HALVES, HALVES, SUMS],
    )
    attn_wide = square_gather(attn_low, attn_high)
    sum_up = scatter_zc(grad_up)
    (grad_heads,) = wide(attn_wide, full_proj, spot, True, finish_plain, (), 1)
    grad_proj = grad(attn_wide, heads_out, spot, True)
    grad_qkv = attention_back(qkv, ids_row, ids_column, logsum, tie(grad_heads, grad_up), spot)
    sum_proj = scatter_zc(grad_proj)
    grad_wqkv = grad(gathered, grad_qkv, spot, False)
    parts = square_scatter(grad_qkv, full_qkv, spot, False, (grad_wqkv,))
    sum_qkv = scatter_zc(grad_wqkv)
    (back,) = elementwise(
        finish_back, spot, (*parts, grad_one), [HALVES] * 6 + [TILE], [shape_of(LEN, QUARTER, dtype=BF)], [TILE]
    )
    back_own, back_other = from_share(back, yi)
    grad_tokens = side_by_side(back_own, back_other, yi, 1).astype(F32)
    sums_qkv = jnp.sum(grad_qkv.astype(F32), axis=0).reshape(4, 3, HD)

    grad_down = restore_rows(sum_down, yi)
    (grad_up,) = restore_columns(sum_up, 1, yi)
    grad_proj = restore_rows(sum_proj, yi)
    grad_query, grad_key, grad_value = restore_columns(sum_qkv, 3, yi)

    sums = jnp.concatenate(
        [
            v.reshape(4, -1)
            for v in (
                sums_qkv[:, 0], sums_qkv[:, 2], sums_attn[0], sums_back[0], sums_back[1], sums_two[2], sums_two[0], sums_two[1],
                grad_ubias,
            )
        ],
        axis=1,
    )
    sums = jnp.sum(lax.all_to_all(sums, "z", 0, 0, tiled=True), axis=0)
    sums = sums + swap(sums, C_BIT)
    other = swap(sums, Y_BIT)
    sums = jnp.where(yi == 0, jnp.stack([sums, other]), jnp.stack([other, sums]))
    vecs = [sums[:, i * 128 : (i + 1) * 128].reshape(-1) for i in range(8)] + [sums[:, 1024:].reshape(-1)]

    totals = jnp.stack(
        [
            jnp.sum(valid * stats_one[3]),
            jnp.sum(valid * stats_one[2]),
            jnp.sum(valid * stats_two[4]),
            jnp.sum(valid) * QUARTER,
        ]
    )
    for mask in (X_BIT, Z_LOW, Z_HIGH, C_BIT, Y_BIT):
        totals = totals + swap(totals, mask)
    norms = jnp.sqrt(totals[:3] / totals[3])
    return (
        layer_out, grad_tokens, grad_query, vecs[0], grad_key, grad_value, vecs[1], grad_proj, vecs[2], vecs[3], vecs[4],
        grad_up, vecs[8], grad_down, vecs[5], vecs[6], vecs[7], norms,
    )


def gather_features(piece):
    return lax.all_gather(piece, "col", axis=1, tiled=True)


def scatter_features(partial_sum):
    low = partial_sum.astype(jnp.bfloat16)
    return lax.psum_scatter(low, "col", scatter_dimension=1, tiled=True).astype(F32)


def row_totals(first, second):
    return lax.psum((first, second), "col")


def gather_weights(w_query, w_key, w_value, w_up, w_proj, w_down):
    inner = (
        lax.all_gather(w_query, "row", axis=0, tiled=True),
        lax.all_gather(w_key, "row", axis=0, tiled=True),
        lax.all_gather(w_value, "row", axis=0, tiled=True),
        lax.all_gather(w_up, "row", axis=0, tiled=True),
    )
    outer = (
        lax.all_gather(w_proj, "row", axis=1, tiled=True),
        lax.all_gather(w_down, "row", axis=1, tiled=True),
    )
    return (inner, outer)


def norm_shares(resid, gain, shift):
    width = resid.shape[1] * lax.axis_size("col")
    total, squares = row_totals(jnp.sum(resid, axis=1), jnp.sum(resid * resid, axis=1))
    mean = total / width
    rstd = lax.rsqrt(squares / width - mean * mean + EPS)
    normed = (resid - mean[:, None]) * rstd[:, None]
    return (normed * gain + shift, normed, rstd)


def norm_back(upstream, normed, rstd, gain):
    width = upstream.shape[1] * lax.axis_size("col")
    scaled = upstream * gain
    total, along = row_totals(jnp.sum(scaled, axis=1), jnp.sum(scaled * normed, axis=1))
    back = rstd[:, None] * (scaled - total[:, None] / width - normed * (along[:, None] / width))
    return (back, jnp.sum(upstream * normed, axis=0), jnp.sum(upstream, axis=0))


def attend_forward(pack):
    queries, keys, values, ids = pack
    scale = queries.shape[2] ** (-0.5)
    block = min(512, queries.shape[0])
    same = ids[:, None] == ids[None, :]
    outputs = []
    logsums = []
    for begin in range(0, queries.shape[0], block):
        scores = (
            jnp.einsum(
                "qhd,khd->hqk",
                queries[begin : begin + block],
                keys,
                preferred_element_type=jnp.float32,
            )
            * scale
        )
        scores = jnp.where(same[None, begin : begin + block], scores, NEGATIVE)
        peak = jnp.max(scores, axis=2, keepdims=True)
        expo = jnp.exp(scores - peak)
        total = jnp.sum(expo, axis=2, keepdims=True)
        probs = (expo / total).astype(jnp.bfloat16)
        outputs.append(
            jnp.einsum("hqk,khd->qhd", probs, values, preferred_element_type=jnp.float32)
        )
        logsums.append((peak + jnp.log(total))[:, :, 0])
    return (jnp.concatenate(outputs, axis=0), jnp.concatenate(logsums, axis=1))


def attend_back(pack):
    queries, keys, values, ids, logsum, grad_out = pack
    scale = queries.shape[2] ** (-0.5)
    block = min(512, queries.shape[0])
    same = ids[:, None] == ids[None, :]
    grad_keys = jnp.zeros(keys.shape, jnp.float32)
    grad_values = jnp.zeros(values.shape, jnp.float32)
    grad_queries = []
    for begin in range(0, queries.shape[0], block):
        query_rows = queries[begin : begin + block]
        grad_rows = grad_out[begin : begin + block]
        scores = (
            jnp.einsum("qhd,khd->hqk", query_rows, keys, preferred_element_type=jnp.float32) * scale
        )
        scores = jnp.where(same[None, begin : begin + block], scores, NEGATIVE)
        probs = jnp.exp(scores - logsum[:, begin : begin + block, None])
        grad_probs = jnp.einsum(
            "qhd,khd->hqk", grad_rows, values, preferred_element_type=jnp.float32
        )
        inner = jnp.sum(probs * grad_probs, axis=2, keepdims=True)
        grad_scores = (probs * (grad_probs - inner)).astype(jnp.bfloat16)
        grad_queries.append(
            jnp.einsum("hqk,khd->qhd", grad_scores, keys, preferred_element_type=jnp.float32)
            * scale
        )
        grad_keys = (
            grad_keys
            + jnp.einsum(
                "hqk,qhd->khd", grad_scores, query_rows, preferred_element_type=jnp.float32
            )
            * scale
        )
        grad_values = grad_values + jnp.einsum(
            "hqk,qhd->khd",
            probs.astype(jnp.bfloat16),
            grad_rows,
            preferred_element_type=jnp.float32,
        )
    return (jnp.concatenate(grad_queries, axis=0), grad_keys, grad_values)


def per_device(
    tokens,
    lengths,
    w_query,
    b_query,
    w_key,
    w_value,
    b_value,
    w_proj,
    b_proj,
    norm_gain,
    norm_shift,
    w_up,
    b_up,
    w_down,
    b_down,
    final_gain,
    final_shift,
    cotangent,
):
    rows, share = tokens.shape
    heads = w_query.shape[1] // HD
    ids = segment_ids(lengths)
    seq_count = ids.shape[0]
    valid = (ids.reshape(rows) != lengths.shape[1] - 1).astype(jnp.float32)[:, None]
    inner, outer = gather_weights(w_query, w_key, w_value, w_up, w_proj, w_down)
    full_query, full_key, full_value, full_up = inner
    full_proj, full_down = outer
    stream = tokens.astype(jnp.float32)
    gathered = gather_features(tokens)
    queries = (jnp.dot(gathered, full_query, preferred_element_type=jnp.float32) + b_query).astype(
        jnp.bfloat16
    )
    keys = jnp.dot(gathered, full_key, preferred_element_type=jnp.float32).astype(jnp.bfloat16)
    values = (jnp.dot(gathered, full_value, preferred_element_type=jnp.float32) + b_value).astype(
        jnp.bfloat16
    )
    shape = (seq_count, LEN, heads, HD)
    query_seq = queries.reshape(shape)
    key_seq = keys.reshape(shape)
    value_seq = values.reshape(shape)
    mixed, logsum = lax.map(attend_forward, (query_seq, key_seq, value_seq, ids))
    heads_out = mixed.reshape(rows, heads * HD).astype(jnp.bfloat16)
    attn = (
        scatter_features(jnp.dot(heads_out, full_proj, preferred_element_type=jnp.float32)) + b_proj
    )
    hidden, normed_one, rstd_one = norm_shares(stream + attn, norm_gain, norm_shift)
    hidden_low = gather_features(hidden.astype(jnp.bfloat16))
    pre = jnp.dot(hidden_low, full_up, preferred_element_type=jnp.float32) + b_up
    act, gelu_back = jax.vjp(lambda inputs: jax.nn.gelu(inputs, approximate=True), pre)
    act_low = act.astype(jnp.bfloat16)
    ffn = scatter_features(jnp.dot(act_low, full_down, preferred_element_type=jnp.float32)) + b_down
    result, normed_two, rstd_two = norm_shares(hidden + ffn, final_gain, final_shift)
    totals = lax.psum(
        (
            jnp.sum(valid * stream * stream),
            jnp.sum(valid * attn * attn),
            jnp.sum(valid * ffn * ffn),
            jnp.sum(valid) * share,
        ),
        ("row", "col"),
    )
    norms = jnp.sqrt(jnp.stack([totals[0], totals[1], totals[2]]) / totals[3])
    back_inner, back_outer = gather_weights(w_query, w_key, w_value, w_up, w_proj, w_down)
    full_query, full_key, full_value, full_up = back_inner
    full_proj, full_down = back_outer
    grad_two, grad_fgain, grad_fshift = norm_back(
        cotangent.astype(jnp.float32), normed_two, rstd_two, final_gain
    )
    grad_ffn = grad_two.astype(jnp.bfloat16)
    grad_dbias = jnp.sum(grad_ffn.astype(jnp.float32), axis=0)
    ffn_wide = gather_features(grad_ffn)
    grad_down = jnp.einsum("tf,td->fd", act_low, ffn_wide, preferred_element_type=jnp.float32)
    grad_act = jnp.einsum("td,fd->tf", ffn_wide, full_down, preferred_element_type=jnp.float32)
    grad_pre = gelu_back(grad_act)[0].astype(jnp.bfloat16)
    grad_ubias = jnp.sum(grad_pre.astype(jnp.float32), axis=0)
    grad_up = jnp.einsum("td,tf->df", hidden_low, grad_pre, preferred_element_type=jnp.float32)
    grad_hidden = (
        scatter_features(
            jnp.einsum("tf,df->td", grad_pre, full_up, preferred_element_type=jnp.float32)
        )
        + grad_two
    )
    grad_one, grad_ngain, grad_nshift = norm_back(grad_hidden, normed_one, rstd_one, norm_gain)
    grad_attn = grad_one.astype(jnp.bfloat16)
    grad_pbias = jnp.sum(grad_attn.astype(jnp.float32), axis=0)
    attn_wide = gather_features(grad_attn)
    grad_proj = jnp.einsum("th,td->hd", heads_out, attn_wide, preferred_element_type=jnp.float32)
    grad_heads = jnp.einsum(
        "td,hd->th", attn_wide, full_proj, preferred_element_type=jnp.float32
    ).astype(jnp.bfloat16)
    back_query, back_key, back_value = lax.map(
        attend_back, (query_seq, key_seq, value_seq, ids, logsum, grad_heads.reshape(shape))
    )
    grad_queries = back_query.reshape(rows, heads * HD).astype(jnp.bfloat16)
    grad_keys = back_key.reshape(rows, heads * HD).astype(jnp.bfloat16)
    grad_values = back_value.reshape(rows, heads * HD).astype(jnp.bfloat16)
    grad_qbias = jnp.sum(grad_queries.astype(jnp.float32), axis=0)
    grad_vbias = jnp.sum(grad_values.astype(jnp.float32), axis=0)
    grad_query = jnp.einsum("td,th->dh", gathered, grad_queries, preferred_element_type=jnp.float32)
    grad_key = jnp.einsum("td,th->dh", gathered, grad_keys, preferred_element_type=jnp.float32)
    grad_value = jnp.einsum("td,th->dh", gathered, grad_values, preferred_element_type=jnp.float32)
    partial_back = (
        jnp.einsum("th,dh->td", grad_queries, full_query, preferred_element_type=jnp.float32)
        + jnp.einsum("th,dh->td", grad_keys, full_key, preferred_element_type=jnp.float32)
        + jnp.einsum("th,dh->td", grad_values, full_value, preferred_element_type=jnp.float32)
    )
    grad_tokens = scatter_features(partial_back) + grad_one
    grad_query, grad_key, grad_value, grad_up = (
        lax.psum_scatter(
            grad_query.astype(jnp.bfloat16), "row", scatter_dimension=0, tiled=True
        ).astype(jnp.float32),
        lax.psum_scatter(
            grad_key.astype(jnp.bfloat16), "row", scatter_dimension=0, tiled=True
        ).astype(jnp.float32),
        lax.psum_scatter(
            grad_value.astype(jnp.bfloat16), "row", scatter_dimension=0, tiled=True
        ).astype(jnp.float32),
        lax.psum_scatter(
            grad_up.astype(jnp.bfloat16), "row", scatter_dimension=0, tiled=True
        ).astype(jnp.float32),
    )
    grad_proj, grad_down = (
        lax.psum_scatter(
            grad_proj.astype(jnp.bfloat16), "row", scatter_dimension=1, tiled=True
        ).astype(jnp.float32),
        lax.psum_scatter(
            grad_down.astype(jnp.bfloat16), "row", scatter_dimension=1, tiled=True
        ).astype(jnp.float32),
    )
    vectors = lax.psum(
        (
            grad_qbias,
            grad_vbias,
            grad_pbias,
            grad_ngain,
            grad_nshift,
            grad_ubias,
            grad_dbias,
            grad_fgain,
            grad_fshift,
        ),
        "row",
    )
    return (
        result.astype(jnp.bfloat16),
        grad_tokens,
        grad_query,
        vectors[0],
        grad_key,
        grad_value,
        vectors[1],
        grad_proj,
        vectors[2],
        vectors[3],
        vectors[4],
        grad_up,
        vectors[5],
        grad_down,
        vectors[6],
        vectors[7],
        vectors[8],
        norms,
    )


def placements(row, col):
    grid, turned, share = P(row, col), P(col, row), P(col)
    args = (
        grid, P(row, None), grid, share, grid, grid, share, turned, share, share, share, grid, share, turned, share, share, share, grid,
    )
    outs = (
        grid, grid, grid, share, grid, grid, share, turned, share, share, share, grid, share, turned, share, share, share, P(),
    )
    return (args, outs)


def solution(mesh):
    if mesh.shape["row"] == 4 and mesh.shape["col"] == 8:
        mesh = Mesh(mesh.devices.reshape(2, 2, 4, 2), AXES)
        args, outs = placements(("y", "c"), ("z", "x"))
        body = square_device
    else:
        args, outs = placements("row", "col")
        body = per_device
    return jax.shard_map(body, mesh=mesh, in_specs=args, out_specs=outs, check_vma=False)
```

```python
import functools

import jax
import jax.numpy as jnp
from jax import lax
from jax.experimental import pallas as pl
from jax.experimental.pallas import tpu as pltpu
from jax.sharding import Mesh
from jax.sharding import PartitionSpec as P

HD = 128
LEN = 1024
EPS = 1e-06
NEGATIVE = -1000000000.0
BF = jnp.bfloat16
F32 = jnp.float32


def segment_ids(lengths):
    slots = lengths.shape[1]
    ends = jnp.cumsum(lengths, axis=1)
    places = jnp.arange(LEN, dtype=jnp.int32)
    hits = (places[None, :, None] >= ends[:, None, : slots - 1]).astype(jnp.int32)
    return jnp.sum(hits, axis=2)


AXES = ("y", "c", "z", "x")
X_BIT, Z_LOW, Z_HIGH, C_BIT, Y_BIT = 1, 2, 4, 8, 16
XY_BIT = X_BIT | Y_BIT
QUARTER = 512
HALF = LEN // 2
WIDTH = 2048
NN, NT, TN = ((1,), (0,)), ((1,), (1,)), ((0,), (0,))


def swap(piece, mask):
    return lax.ppermute(piece, AXES, [(i, i ^ mask) for i in range(32)])


def dot(left, right, dims):
    return lax.dot_general(left, right, (dims, ((), ())), preferred_element_type=F32)


def tie(value, *others):
    return lax.optimization_barrier((value, *others))[0]


class Order:
    def __init__(self, value):
        self.value = value

    def after(self, *others):
        self.value = tie(self.value, *others)


MORE = 10


def call(body, grid, spot, ins, in_specs, outs, out_specs, scratch, flops, size):
    result = pl.pallas_call(
        body,
        grid_spec=pltpu.PrefetchScalarGridSpec(
            num_scalar_prefetch=1, grid=grid, in_specs=in_specs, out_specs=out_specs, scratch_shapes=scratch
        ),
        out_shape=outs,
        compiler_params=pltpu.CompilerParams(
            dimension_semantics=("arbitrary",) * len(grid), vmem_limit_bytes=56 * 1024 * 1024
        ),
        cost_estimate=pl.CostEstimate(flops=flops * MORE, bytes_accessed=size * MORE, transcendentals=0),
    )(spot.value, *ins)
    spot.after(result[0])
    return result


def shape_of(*shape, dtype=F32):
    return jax.ShapeDtypeStruct(shape, dtype)


def fixed(shape):
    return pl.BlockSpec(shape, lambda *_: (0,) * len(shape))


def pick(low, high, first):
    return jnp.where(first, low[...], high[...])


SLOTS = (0, 2, 1, 3)


def wide_body(by_rows, finish, count, spot, *refs):
    pieces, weights, rest = refs[:8], refs[8], refs[9:]
    extra, outs, kept = rest[: -1 - count], rest[-1 - count : -1], rest[-1]
    t = pl.program_id(1)

    @pl.when(t == 0)
    def _():
        for slot, mask in enumerate(SLOTS):
            start = pl.multiple_of((spot[0] ^ mask) * 128, 128)
            for block in range(4):
                y, c = divmod(block, 2)
                y = y ^ spot[1]
                at = slot * QUARTER + block * 128
                if by_rows:
                    kept[:, at : at + 128] = weights[0, c, :, pl.ds(pl.multiple_of(y * 512 + start, 128), 128)]
                else:
                    kept[at : at + 128, :] = weights[0, c, y, pl.ds(start, 128), :]

    total = None
    for slot in range(4):
        tile = pick(pieces[2 * slot], pieces[2 * slot + 1], t == 0)
        part = slice(slot * QUARTER, slot * QUARTER + QUARTER)
        term = dot(tile, kept[:, part], NT) if by_rows else dot(tile, kept[part, :], NN)
        total = term if total is None else total + term
    finish(total, extra, outs)


def wide(pieces, weights, spot, by_rows, finish, extra, count, sums=0):
    if by_rows:
        n = weights.shape[1]
        weights = weights.reshape(4, 2, n, 1024)
        kept = pltpu.VMEM((n, WIDTH), BF)
    else:
        n = weights.shape[2]
        weights = weights.reshape(4, 2, 2, 512, n)
        kept = pltpu.VMEM((WIDTH, n), BF)
    block = (1,) + weights.shape[1:]
    tail = (0,) * (len(block) - 1)
    bias = pl.BlockSpec((1, n), lambda z, t, *_: (0, z))
    tile = pl.BlockSpec((HALF, n), lambda z, t, *_: (t, z))
    return call(
        functools.partial(wide_body, by_rows, finish, count + sums),
        (4, 2),
        spot,
        (*pieces, weights, *extra),
        [fixed(p.shape) for p in pieces]
        + [pl.BlockSpec(block, lambda z, t, *_: (z,) + tail)]
        + [bias if e.shape[0] == 1 else tile for e in extra],
        [shape_of(LEN, 4 * n, dtype=BF)] * count + [shape_of(8, 4 * n)] * sums,
        [tile] * count + [pl.BlockSpec((8, n), lambda z, t, *_: (0, z))] * sums,
        [kept],
        2 * LEN * WIDTH * 4 * n,
        2 * (LEN * WIDTH + WIDTH * 4 * n + LEN * 4 * n),
    )


def finish_bias(total, extra, outs):
    outs[0][...] = (total + extra[0][...]).astype(BF)


def finish_plain(total, extra, outs):
    outs[0][...] = total.astype(BF)


def finish_gelu(total, extra, outs):
    pre = total + extra[0][...]
    square = pre * pre
    bend = jnp.tanh(0.7978845608028654 * pre * (1.0 + 0.044715 * square))
    rise = 0.5 * (1.0 + bend)
    outs[0][...] = (pre * rise).astype(BF)
    slope = 0.7978845608028654 * (1.0 + 0.134145 * square)
    outs[1][...] = (rise + 0.5 * pre * (1.0 - bend * bend) * slope).astype(BF)


def finish_slope(total, extra, outs):
    rounded = (total * extra[0][...].astype(F32)).astype(BF)
    outs[0][...] = rounded
    add_columns(outs[1], pl.program_id(1), [rounded.astype(F32)])


def partial_body(by_rows, n, spot, local, *rest):
    weights, (low, high) = rest[:-2], rest[-2:]
    t = pl.program_id(0)
    total = None
    for z in range(4):
        tile = local[:, z * n : (z + 1) * n]
        if by_rows:
            kept = jnp.concatenate([weights[y][z, c] for y in range(2) for c in range(2)], axis=1)
            term = dot(tile, kept, NN)
        else:
            kept = jnp.concatenate([weights[0][z, c, y ^ spot[1]] for y in range(2) for c in range(2)], axis=0)
            term = dot(tile, kept, NT)
        total = term if total is None else total + term

    @pl.when(t == 0)
    def _():
        low[...] = total.astype(low.dtype)

    @pl.when(t == 1)
    def _():
        high[...] = total.astype(high.dtype)


def partial(local, weights, spot, by_rows, mask, low, high):
    n = local.shape[1] // 4
    if by_rows:
        weights = weights.reshape(4, 2, n, 1024)
        specs = [
            pl.BlockSpec((4, 2, n, 128), functools.partial(lambda y, t, p: (0, 0, 0, (y ^ p[1]) * 4 + (p[0] ^ mask)), y))
            for y in range(2)
        ]
        ins = (weights, weights)
    else:
        weights = weights.reshape(4, 2, 2, 512, n)
        specs = [pl.BlockSpec((4, 2, 2, 128, n), lambda t, p: (0, 0, 0, p[0] ^ mask, 0))]
        ins = (weights,)
    return call(
        functools.partial(partial_body, by_rows, n),
        (2,),
        spot,
        (local, *ins),
        [pl.BlockSpec((HALF, 4 * n), lambda t, p: (t, 0))] + specs,
        [shape_of(HALF, QUARTER, dtype=low), shape_of(HALF, QUARTER, dtype=high)],
        [fixed((HALF, QUARTER))] * 2,
        [],
        2 * LEN * QUARTER * 4 * n,
        2 * (LEN * 4 * n + QUARTER * 4 * n + LEN * QUARTER),
    )


def grad_whole_body(by_rows, spot, *refs):
    pieces, local, out = refs[:8], refs[8], refs[9]
    for slot, mask in enumerate(SLOTS):
        start = pl.multiple_of((spot[0] ^ mask) * 128, 128)

        def term(piece, tile):
            return dot(tile, piece, TN) if by_rows else dot(piece, tile, TN)

        total = term(pieces[2 * slot][...], local[:HALF, :]) + term(pieces[2 * slot + 1][...], local[HALF:, :])
        for block in range(4):
            y, c = divmod(block, 2)
            y = y ^ spot[1]
            part = slice(block * 128, block * 128 + 128)
            if by_rows:
                out[0, c, :, pl.ds(pl.multiple_of(y * 512 + start, 128), 128)] = total[:, part].astype(BF)
            else:
                out[0, c, y, pl.ds(start, 128), :] = total[part, :].astype(BF)


def grad_whole(pieces, local, spot, by_rows):
    n = local.shape[1] // 4
    shape = (4, 2, n, 1024) if by_rows else (4, 2, 2, 512, n)
    tail = (0,) * (len(shape) - 1)
    (out,) = call(
        functools.partial(grad_whole_body, by_rows),
        (4,),
        spot,
        (*pieces, local),
        [fixed(p.shape) for p in pieces] + [pl.BlockSpec((LEN, n), lambda z, *_: (0, z))],
        [shape_of(*shape, dtype=BF)],
        [pl.BlockSpec((1,) + shape[1:], lambda z, *_: (z,) + tail)],
        [],
        2 * LEN * WIDTH * 4 * n,
        2 * (LEN * WIDTH + WIDTH * 4 * n + LEN * 4 * n),
    )
    return out.reshape(8, n, 1024) if by_rows else out.reshape(8, 1024, n)


def grad_body(by_rows, spot, *refs):
    pieces, local, outs = refs[:8], refs[8], refs[9:]
    order = [((y ^ spot[1]) * 2 + (c ^ spot[2])) * 128 for y in range(2) for c in range(2)]
    order = [pl.ds(pl.multiple_of(at, 128), 128) for at in order]
    for slot, mask in enumerate(SLOTS):
        start = pl.multiple_of((spot[0] ^ mask) * 128, 128)
        total = None
        for part in range(2):
            piece = jnp.concatenate([pieces[2 * slot + part][:, at] for at in order], axis=1)
            tile = local[part * HALF : part * HALF + HALF, :]
            term = dot(tile, piece, TN) if by_rows else dot(piece, tile, TN)
            total = term if total is None else total + term
        for block in range(4):
            y, c = divmod(block, 2)
            part = slice(block * 128, block * 128 + 128)
            if by_rows:
                outs[c][0, :, pl.ds(pl.multiple_of(y * 512 + start, 128), 128)] = total[:, part].astype(BF)
            else:
                outs[c][0, y, pl.ds(start, 128), :] = total[part, :].astype(BF)


def grad(pieces, local, spot, by_rows):
    n = local.shape[1] // 4
    shape = (4, n, 1024) if by_rows else (4, 2, 512, n)
    tail = (0,) * (len(shape) - 1)

    def where(z, p):
        far = z ^ p[3]
        return ((far >> 1) | ((far & 1) << 1),) + tail

    outs = call(
        functools.partial(grad_body, by_rows),
        (4,),
        spot,
        (*pieces, local),
        [fixed(p.shape) for p in pieces] + [pl.BlockSpec((LEN, n), lambda z, *_: (0, z))],
        [shape_of(*shape, dtype=BF)] * 2,
        [pl.BlockSpec((1,) + shape[1:], where)] * 2,
        [],
        2 * LEN * WIDTH * 4 * n,
        2 * (LEN * WIDTH + WIDTH * 4 * n + LEN * 4 * n),
    )
    return [o if by_rows else o.reshape(4, 1024, n) for o in outs]


def fold_body(spot, *refs):
    count = len(refs) // 3
    for i in range(count):
        out = refs[2 * count + i]
        out[...] = (refs[i][...].astype(F32) + refs[count + i][...].astype(F32)).astype(out.dtype)


def fold(own, got, spot):
    half, rows, width = own.shape[0] // 2, own.shape[1], own.shape[2]
    step = min(rows, 512)
    first = pl.BlockSpec((1, step, width), lambda i, t, p: (i, t, 0))
    second = pl.BlockSpec((1, step, width), lambda i, t, p: (i + half, t, 0))
    return call(
        fold_body, (half, rows // step), spot, (own, own, got, got), [first, second] * 2,
        [shape_of(half, rows, width, dtype=BF)] * 2, [first, first], [], 2 * half * rows * width, 12 * half * rows * width,
    )


def fold_last(own, got, spot, by_rows):
    rows, width = own.shape[1:]
    if by_rows:
        shape = (rows, 512)
        parts = [pl.BlockSpec((1, rows, 512), functools.partial(lambda y, i, p: (0, 0, y), y)) for y in range(2)]
    else:
        shape = (512, width)
        parts = [pl.BlockSpec((1, 512, width), functools.partial(lambda y, i, p: (0, y, 0), y)) for y in range(2)]

    def body(spot, a, b, c, d, keep, send):
        keep[...] = a[0].astype(F32) + c[0].astype(F32)
        send[...] = (b[0].astype(F32) + d[0].astype(F32)).astype(BF)

    return call(
        body, (1,), spot, (own, own, got, got), parts * 2, [shape_of(*shape), shape_of(*shape, dtype=BF)], [fixed(shape)] * 2,
        [], rows * width, 6 * rows * width,
    )


class Sum:
    def __init__(self, outs, spot, by_rows):
        self.keep, self.send = outs
        self.spot, self.by_rows = spot, by_rows

    def go(self, mask):
        self.got = swap(tie(self.send, self.spot.value), mask)

    def step(self):
        self.keep, self.send = fold(self.keep, self.got, self.spot)

    def last(self):
        self.keep, self.send = fold_last(self.keep, self.got, self.spot, self.by_rows)
        return self.keep, swap(self.send, Y_BIT)


SCALE = HD ** (-0.5)
LOG2E = 1.4426950408889634
QUERY_BLOCK = 512


def forward_body(spot, queries, whole, ids_row, ids_column, out, logsum):
    scores = dot(whole[:, HD : 2 * HD], queries[:, :HD], NT)
    scores = jnp.where(ids_column[...] == ids_row[...], scores, NEGATIVE)
    peak = jnp.max(scores, axis=0, keepdims=True)
    expo = jnp.exp2((scores - peak) * (SCALE * LOG2E))
    total = jnp.sum(expo, axis=0, keepdims=True)
    probs = (expo * (1.0 / total)).astype(BF)
    mixed = dot(whole[:, 2 * HD :], probs, TN)
    out[...] = mixed.T.astype(BF)
    logsum[0] = peak * (SCALE * LOG2E) + jnp.log2(total)


def head_specs():
    return [
        pl.BlockSpec((QUERY_BLOCK, 3 * HD), lambda h, q, p: (q, h)),
        pl.BlockSpec((LEN, 3 * HD), lambda h, q, p: (0, h)),
        pl.BlockSpec((1, QUERY_BLOCK), lambda h, q, p: (0, q)),
        pl.BlockSpec((LEN, 1), lambda h, q, p: (0, 0)),
    ]


def attention(qkv, ids_row, ids_column, spot):
    return call(
        forward_body,
        (4, LEN // QUERY_BLOCK),
        spot,
        (qkv, qkv, ids_row, ids_column),
        head_specs(),
        [shape_of(LEN, QUARTER, dtype=BF), shape_of(4, 1, LEN)],
        [
            pl.BlockSpec((QUERY_BLOCK, HD), lambda h, q, p: (q, h)),
            pl.BlockSpec((1, 1, QUERY_BLOCK), lambda h, q, p: (h, 0, q)),
        ],
        [],
        64 * LEN * LEN * HD,
        LEN * 4 * HD * 8,
    )


def backward_body(spot, queries, whole, ids_row, ids_column, logsum, grad_out, out, sums, grad_keys, grad_values):
    q = pl.program_id(1)
    block = queries.shape[0]
    keys = whole[:, HD : 2 * HD]
    values = whole[:, 2 * HD :]
    scores = dot(keys, queries[:, :HD], NT) * (SCALE * LOG2E)
    scores = jnp.where(ids_column[...] == ids_row[...], scores, NEGATIVE)
    probs = jnp.exp2(scores - logsum[0])
    grad_probs = dot(values, grad_out[...], NT)
    inner = jnp.sum(probs * grad_probs, axis=0, keepdims=True)
    grad_scores = (probs * (grad_probs - inner)).astype(BF)
    back_query = dot(keys, grad_scores, TN)
    back_query = (back_query.T * SCALE).astype(BF)
    out[pl.ds(q * block, block), :HD] = back_query
    add_columns(sums.at[:, :HD], q, [back_query.astype(F32)])
    back_key = dot(grad_scores, queries[:, :HD], NN)
    back_value = dot(probs.astype(BF), grad_out[...], NN)

    @pl.when(q == 0)
    def _():
        grad_keys[...] = back_key
        grad_values[...] = back_value

    @pl.when(q > 0)
    def _():
        grad_keys[...] += back_key
        grad_values[...] += back_value

    @pl.when(q == pl.num_programs(1) - 1)
    def _():
        out[:, HD : 2 * HD] = (grad_keys[...] * SCALE).astype(BF)
        rounded = grad_values[...].astype(BF)
        out[:, 2 * HD :] = rounded
        sums[:, HD : 2 * HD] = jnp.zeros((8, HD), F32)
        sums[:, 2 * HD :] = column_sums([rounded.astype(F32)])


def attention_back(qkv, ids_row, ids_column, logsum, grad_heads, spot):
    return call(
        backward_body,
        (4, LEN // QUERY_BLOCK),
        spot,
        (qkv, qkv, ids_row, ids_column, logsum, grad_heads),
        head_specs()
        + [
            pl.BlockSpec((1, 1, QUERY_BLOCK), lambda h, q, p: (h, 0, q)),
            pl.BlockSpec((QUERY_BLOCK, HD), lambda h, q, p: (q, h)),
        ],
        [shape_of(LEN, 12 * HD, dtype=BF), shape_of(8, 12 * HD)],
        [pl.BlockSpec((LEN, 3 * HD), lambda h, q, p: (0, h)), pl.BlockSpec((8, 3 * HD), lambda h, q, p: (0, h))],
        [pltpu.VMEM((LEN, HD), F32), pltpu.VMEM((LEN, HD), F32)],
        120 * LEN * LEN * HD,
        LEN * 4 * HD * 16,
    )


def row_sum(value):
    folded = value[:, :128] + value[:, 128:256] + value[:, 256:384] + value[:, 384:512]
    return jnp.sum(folded.T, axis=0, keepdims=True)


def rows_of(values):
    rows = [row_sum(v) for v in values]
    return jnp.concatenate(rows + [jnp.zeros_like(rows[0])] * (8 - len(rows)), axis=0)


def columns_of(rows):
    return rows.T


def column_sums(values):
    sums = [jnp.sum(v, axis=0, keepdims=True) for v in values]
    return jnp.concatenate(sums + [jnp.zeros_like(sums[0])] * (8 - len(sums)), axis=0)


def add_columns(ref, t, values):
    sums = column_sums(values)

    @pl.when(t == 0)
    def _():
        ref[...] = sums

    @pl.when(t > 0)
    def _():
        ref[...] += sums


def moments_of(stats):
    total = (stats[0][...] + stats[1][...] + stats[2][...] + stats[3][...]) / WIDTH
    mean = total[0:1]
    return mean, lax.rsqrt(total[1:2] - mean * mean + EPS), total


def summed(refs, t):
    own, near, last = (pick(refs[2 * i], refs[2 * i + 1], t < STEPS // 2).astype(F32) for i in range(3))
    return own + near + last


STEP = 256
STEPS = LEN // STEP
LOW = pl.BlockSpec((STEP, QUARTER), lambda t, p: (jnp.minimum(t, STEPS // 2 - 1), 0))
HIGH = pl.BlockSpec((STEP, QUARTER), lambda t, p: (jnp.maximum(t - STEPS // 2, 0), 0))
PARTS = [LOW, HIGH] * 3
TILE = pl.BlockSpec((STEP, QUARTER), lambda t, p: (t, 0))
STATS = pl.BlockSpec((8, STEP), lambda t, p: (0, t))
VECTOR = fixed((1, QUARTER))
SUMS = fixed((8, QUARTER))
BLOCKS = pl.BlockSpec((4, STEP, 128), lambda t, p: (0, t, 0))


def elementwise(body, spot, ins, in_specs, outs, out_specs):
    return call(body, (STEPS,), spot, ins, in_specs, outs, out_specs, [], 20 * LEN * QUARTER, 16 * LEN * QUARTER)


def write_blocks(out, value):
    for z in range(4):
        out[z] = value[:, z * 128 : z * 128 + 128].astype(BF)


def norm_one_sums(spot, *refs):
    parts, (low, high, bias, resid, stats) = refs[:6], refs[6:]
    t = pl.program_id(0)
    attn = summed(parts, t) + bias[...]
    stream = pick(low, high, t < STEPS // 2).astype(F32)
    total = stream + attn
    resid[...] = total
    stats[...] = rows_of([total, total * total, attn * attn, stream * stream])


def write_halves(t, low, high, value):
    @pl.when(t < STEPS // 2)
    def _():
        low[...] = value

    @pl.when(t >= STEPS // 2)
    def _():
        high[...] = value


def norm_one(spot, resid, s0, s1, s2, s3, gain, shift, low, high, moments):
    mean, rstd, _ = moments_of((s0, s1, s2, s3))
    rows = jnp.concatenate([mean, rstd] + [mean] * 6, axis=0)
    moments[...] = rows
    columns = columns_of(rows)
    hidden = (resid[...] - columns[:, 0:1]) * columns[:, 1:2] * gain[...] + shift[...]
    write_halves(pl.program_id(0), low, high, hidden.astype(BF))


def norm_two_sums(spot, *refs):
    parts = refs[:6]
    bias, resid, moments, gain, shift, dy_low, dy_high, gain_two, resid_two, stats = refs[6:]
    t = pl.program_id(0)
    ffn = summed(parts, t) + bias[...]
    columns = columns_of(moments[...])
    hidden = (resid[...] - columns[:, 0:1]) * columns[:, 1:2] * gain[...] + shift[...]
    total = hidden + ffn
    resid_two[...] = total
    scaled = pick(dy_low, dy_high, t < STEPS // 2).astype(F32) * gain_two[...]
    stats[...] = rows_of([total, total * total, scaled, scaled * total, ffn * ffn])


def norm_two(spot, resid_two, s0, s1, s2, s3, dy_low, dy_high, gain, shift, layer_out, grad_two, low, high, sums):
    mean, rstd, total = moments_of((s0, s1, s2, s3))
    mean_e = total[2:3]
    along = rstd * (total[3:4] - mean * mean_e)
    columns = columns_of(jnp.concatenate([mean, rstd, mean_e, along] + [mean] * 4, axis=0))
    normed = (resid_two[...] - columns[:, 0:1]) * columns[:, 1:2]
    t = pl.program_id(0)
    upstream = pick(dy_low, dy_high, t < STEPS // 2).astype(F32)
    write_blocks(layer_out, normed * gain[...] + shift[...])
    back = columns[:, 1:2] * (upstream * gain[...] - columns[:, 2:3] - normed * columns[:, 3:4])
    grad_two[...] = back
    rounded = back.astype(BF)
    write_halves(t, low, high, rounded)
    add_columns(sums, t, [upstream * normed, upstream, rounded.astype(F32)])


def back_one_sums(spot, *refs):
    parts = refs[:6]
    grad_two, resid, moments, gain, grad_hidden, stats, sums = refs[6:]
    t = pl.program_id(0)
    upstream = summed(parts, t) + grad_two[...]
    grad_hidden[...] = upstream
    columns = columns_of(moments[...])
    normed = (resid[...] - columns[:, 0:1]) * columns[:, 1:2]
    scaled = upstream * gain[...]
    stats[...] = rows_of([scaled, scaled * normed])
    add_columns(sums, t, [upstream * normed, upstream])


def back_one(spot, grad_hidden, s0, s1, s2, s3, resid, moments, gain, grad_one, low, high, sums):
    total = (s0[...] + s1[...] + s2[...] + s3[...]) / WIDTH
    means = columns_of(total)
    columns = columns_of(moments[...])
    normed = (resid[...] - columns[:, 0:1]) * columns[:, 1:2]
    back = columns[:, 1:2] * (grad_hidden[...] * gain[...] - means[:, 0:1] - normed * means[:, 1:2])
    grad_one[...] = back
    rounded = back.astype(BF)
    t = pl.program_id(0)
    write_halves(t, low, high, rounded)
    add_columns(sums, t, [rounded.astype(F32)])


def finish_back(spot, *refs):
    parts, (grad_one, out) = refs[:6], refs[6:]
    write_blocks(out, summed(parts, pl.program_id(0)) + grad_one[...])


def pass_on(spot, first, second, third, fourth, low, high):
    low[...] = (first[...] + second[...].astype(F32)).astype(BF)
    high[...] = (third[...] + fourth[...].astype(F32)).astype(BF)


def split_y(piece, yi):
    return lax.dynamic_slice_in_dim(piece, yi * 128, 128, 1), lax.dynamic_slice_in_dim(piece, (1 - yi) * 128, 128, 1)


def spread_z(own, other, yi, zi):
    both = jnp.concatenate([own.reshape(2, LEN, 128), other.reshape(2, LEN, 128)], axis=0)
    blocks = []
    for mask, bits in ((0, 0), (1, Z_LOW), (2, Z_HIGH), (3, Z_LOW | Z_HIGH)):
        block = lax.dynamic_index_in_dim(both, (zi ^ mask) ^ (yi * 2), 0, False)
        blocks.append(swap(block, bits) if mask else block)
    return blocks


def assemble_body(spot, *refs):
    blocks, (low, high) = refs[:4], refs[4:]
    t = pl.program_id(0)
    for out, when in ((low, t < STEPS // 2), (high, t >= STEPS // 2)):

        @pl.when(when)
        def _():
            for mask, block in enumerate(blocks):
                out[:, pl.ds(pl.multiple_of((spot[3] ^ mask) * 128, 128), 128)] = block[...]


def assemble(blocks, spot):
    half = shape_of(HALF, QUARTER, dtype=BF)
    return elementwise(
        assemble_body, spot, blocks, [pl.BlockSpec((STEP, 128), lambda t, p: (t, 0))] * 4, [half, half], [LOW, HIGH]
    )


def from_share(share, yi):
    parts = lax.all_to_all(share, "z", 0, 0, tiled=True).reshape(2, 2 * LEN, 128)
    own = lax.dynamic_index_in_dim(parts, yi, 0, False)
    other = swap(lax.dynamic_index_in_dim(parts, 1 - yi, 0, False), Y_BIT)
    return own, other


def side_by_side(own, other, yi, axis):
    return jnp.where(yi == 0, jnp.concatenate([own, other], axis), jnp.concatenate([other, own], axis))


def square_gather(low, high):
    x_low = swap(low, X_BIT)
    y_high = swap(high, Y_BIT)
    x_high = swap(high, X_BIT)
    y_low = swap(low, Y_BIT)
    xy_low = swap(x_low, Y_BIT)
    xy_high = swap(y_high, X_BIT)
    return (low, high, x_low, x_high, y_low, y_high, xy_low, xy_high)


def square_scatter(local, weights, spot, by_rows, first=lambda: None, between=lambda: None, after=lambda: None):
    term = functools.partial(partial, local, weights, spot, by_rows)
    far_low, far_high = term(3, BF, BF)
    far_low = swap(far_low, X_BIT)
    far_high = swap(far_high, Y_BIT)
    near_low, x_high = term(2, BF, F32)
    near_low = swap(near_low, X_BIT)
    first()
    y_low, near_high = term(1, F32, BF)
    near_high = swap(near_high, Y_BIT)
    half = fixed((HALF, QUARTER))
    last_low, last_high = call(
        pass_on, (1,), spot, (y_low, far_low, x_high, far_high), [half] * 4, [shape_of(HALF, QUARTER, dtype=BF)] * 2,
        [half] * 2, [], LEN * QUARTER, 8 * LEN * QUARTER,
    )
    last_low = swap(last_low, Y_BIT)
    last_high = swap(last_high, X_BIT)
    between()
    spot.after(near_low, near_high)
    own_low, own_high = term(0, F32, F32)
    after()
    return (own_low, own_high, near_low, near_high, last_low, last_high)


def square_stats(stats):
    return (stats, swap(stats, X_BIT), swap(stats, Y_BIT), swap(stats, XY_BIT))


def halve_columns(pieces, yi, *after):
    n = pieces[0].shape[1] // 2
    own = jnp.concatenate([lax.dynamic_slice_in_dim(p, yi * n, n, 1) for p in pieces], axis=1)
    send = tie(jnp.concatenate([lax.dynamic_slice_in_dim(p, (1 - yi) * n, n, 1) for p in pieces], axis=1), *after)
    return jnp.concatenate([own, swap(send, Y_BIT)], axis=0), send


def halve_rows(piece, yi, *after):
    n = piece.shape[0] // 2
    own = lax.dynamic_slice_in_dim(piece, yi * n, n, 0)
    send = tie(lax.dynamic_slice_in_dim(piece, (1 - yi) * n, n, 0), *after)
    return jnp.concatenate([own, swap(send, Y_BIT)], axis=1), send


def gather_zc(piece):
    return lax.all_gather(piece, ("z", "c"), axis=0)


def scatter_zc(full):
    return lax.psum_scatter(full, ("z", "c"), scatter_dimension=0)


def exchange_columns(piece):
    return piece[:512], swap(piece[512:], Y_BIT)


def exchange_rows(piece):
    return piece[:, :512], swap(piece[:, 512:], Y_BIT)


def restore_columns(pair, count, yi):
    own, other = pair
    n = own.shape[1] // count
    return [
        side_by_side(own[:, i * n : (i + 1) * n].astype(F32), other[:, i * n : (i + 1) * n].astype(F32), yi, 1) for i in range(count)
    ]


def restore_rows(pair, yi):
    return side_by_side(pair[0].astype(F32), pair[1].astype(F32), yi, 0)


def square_device(
    tokens, lengths, w_query, b_query, w_key, w_value, b_value, w_proj, b_proj, norm_gain, norm_shift,
    w_up, b_up, w_down, b_down, final_gain, final_shift, cotangent,
):
    yi = lax.axis_index("y")
    zi = lax.axis_index("z")
    spot = Order(jnp.stack([lax.axis_index("x") * 2 + yi, yi, lax.axis_index("c"), zi]).astype(jnp.int32))

    token_own, token_send = split_y(tokens, yi)
    token_other = swap(token_send, Y_BIT)
    half_qkv, sent = halve_columns([w_query, w_key, w_value], yi, token_send)
    vectors = jnp.concatenate(
        [v.reshape(2, -1) for v in (b_query, b_value, b_proj, norm_gain, norm_shift, b_down, final_gain, final_shift, b_up)],
        axis=1,
    )
    vectors = lax.dynamic_slice_in_dim(vectors, yi, 1, 0)
    vectors = lax.all_to_all(jnp.broadcast_to(vectors, (4, vectors.shape[1])), "z", 0, 0, tiled=True)
    small = [vectors[:, i * 128 : (i + 1) * 128] for i in range(8)]
    q_bias, v_bias = small[:2]
    p_bias, n_gain, n_shift, d_bias, f_gain, f_shift = (v.reshape(1, QUARTER) for v in small[2:])
    u_bias = vectors[:, 1024:].reshape(1, -1)
    qkv_bias = jnp.stack([q_bias, jnp.zeros_like(q_bias), v_bias], axis=1).reshape(1, -1)

    both = side_by_side(lengths, swap(lengths, Y_BIT), yi, 0)
    ids = segment_ids(lax.dynamic_slice_in_dim(both, zi, 1, 0))[0]
    valid = (ids != lengths.shape[1] - 1).astype(F32)
    ids_row, ids_column = ids[None], ids[:, None]

    full_qkv = gather_zc(tie(half_qkv, vectors))
    token_blocks = spread_z(token_own, token_other, yi, zi)
    half_proj, sent = halve_rows(w_proj, yi, sent)
    half_up, sent = halve_columns([w_up], yi, sent)
    half_down, sent = halve_rows(w_down, yi, sent)
    token_low, token_high = assemble(token_blocks, spot)
    gathered = square_gather(token_low, token_high)
    full_proj = gather_zc(tie(half_proj, token_low))
    full_up = gather_zc(tie(half_up, token_low))
    full_down = gather_zc(tie(half_down, token_low))
    (qkv,) = wide(gathered, full_qkv, spot, False, finish_bias, (qkv_bias,), 1)
    heads_out, logsum = attention(qkv, ids_row, ids_column, spot)
    full = shape_of(LEN, QUARTER)
    low_half = shape_of(HALF, QUARTER, dtype=BF)
    stats_shape = shape_of(8, LEN)
    sums_shape = shape_of(8, QUARTER)

    parts = square_scatter(heads_out, full_proj, spot, True)
    resid, stats_one = elementwise(
        norm_one_sums, spot, (*parts, token_low, token_high, p_bias), PARTS + [LOW, HIGH, VECTOR], [full, stats_shape], [TILE, STATS]
    )
    hidden_low, hidden_high, moments = elementwise(
        norm_one, spot, (resid, *square_stats(stats_one), n_gain, n_shift), [TILE] + [STATS] * 4 + [VECTOR] * 2,
        [low_half, low_half, stats_shape], [LOW, HIGH, STATS],
    )
    hidden_wide = square_gather(hidden_low, hidden_high)
    dy_own, dy_send = split_y(tie(cotangent, hidden_low), yi)
    dy_other = swap(dy_send, Y_BIT)
    act, slope = wide(hidden_wide, full_up, spot, False, finish_gelu, (u_bias,), 2)
    dy_blocks = spread_z(tie(dy_own, full_down), dy_other, yi, zi)
    dy_halves = []
    parts = square_scatter(act, full_down, spot, True, between=lambda: dy_halves.extend(assemble(dy_blocks, spot)))
    resid_two, stats_two = elementwise(
        norm_two_sums, spot, (*parts, d_bias, resid, moments, n_gain, n_shift, *dy_halves, f_gain),
        PARTS + [VECTOR, TILE, STATS, VECTOR, VECTOR, LOW, HIGH, VECTOR], [full, stats_shape], [TILE, STATS],
    )
    layer_share, grad_two, ffn_low, ffn_high, sums_two = elementwise(
        norm_two, spot, (resid_two, *square_stats(stats_two), *dy_halves, f_gain, f_shift),
        [TILE] + [STATS] * 4 + [LOW, HIGH, VECTOR, VECTOR],
        [shape_of(4, LEN, 128, dtype=BF), full, low_half, low_half, sums_shape], [BLOCKS, TILE, LOW, HIGH, SUMS],
    )
    ffn_wide = square_gather(ffn_low, ffn_high)
    layer_own, layer_other = from_share(layer_share, yi)
    layer_out = side_by_side(layer_own, layer_other, yi, 1)

    spot.after(layer_own)
    grad_down = scatter_zc(grad_whole(ffn_wide, act, spot, True))
    grad_pre, sums_up = wide(ffn_wide, full_down, spot, True, finish_slope, (slope,), 1, 1)
    up = []
    parts = square_scatter(
        grad_pre, full_up, spot, False, between=lambda: up.append(grad_whole(hidden_wide, grad_pre, spot, False))
    )
    grad_up = scatter_zc(up[0])
    grad_hidden, stats_back, sums_back = elementwise(
        back_one_sums, spot, (*parts, grad_two, resid, moments, n_gain),
        PARTS + [TILE, TILE, STATS, VECTOR], [full, stats_shape, sums_shape], [TILE, STATS, SUMS],
    )
    grad_one, attn_low, attn_high, sums_attn = elementwise(
        back_one, spot, (grad_hidden, *square_stats(stats_back), resid, moments, n_gain),
        [TILE] + [STATS] * 4 + [TILE, STATS, VECTOR],
        [full, low_half, low_half, sums_shape], [TILE, LOW, HIGH, SUMS],
    )
    attn_wide = square_gather(attn_low, attn_high)
    spot.after(grad_down)
    (grad_heads,) = wide(attn_wide, full_proj, spot, True, finish_plain, (), 1)
    grad_qkv, sums_qkv = attention_back(qkv, ids_row, ids_column, logsum, grad_heads, spot)
    qkv_sum = Sum(grad(gathered, grad_qkv, spot, False), spot, False)
    qkv_sum.go(C_BIT)

    totals = jnp.stack([stats_one[3] * valid, stats_one[2] * valid, stats_two[4] * valid, valid * QUARTER])
    totals = jnp.pad(jnp.sum(totals, axis=1)[None], ((0, 3), (0, 124)))
    sums = jnp.concatenate(
        [
            v.reshape(4, -1)
            for v in (
                *(sums_qkv[0].reshape(4, 3, HD)[:, i] for i in (0, 2)),
                sums_attn[0], sums_back[0], sums_back[1], sums_two[2], sums_two[0], sums_two[1], sums_up[0], totals,
            )
        ],
        axis=1,
    )
    for mask in (C_BIT, Z_LOW, Z_HIGH):
        sums = sums + swap(sums, mask)
    proj = []

    def first():
        qkv_sum.step()
        qkv_sum.go(Z_LOW)

    def between():
        proj.append(scatter_zc(grad_whole(attn_wide, heads_out, spot, True)))

    parts = square_scatter(grad_qkv, full_qkv, spot, False, first=first, between=between)
    (grad_proj,) = proj
    spot.after(grad_up)
    (back,) = elementwise(
        finish_back, spot, (*parts, grad_one), PARTS + [TILE], [shape_of(4, LEN, 128, dtype=BF)], [BLOCKS]
    )
    down, up, proj = exchange_rows(grad_down), exchange_columns(grad_up), exchange_rows(grad_proj)
    qkv_sum.step()
    qkv_sum.go(Z_HIGH)
    back_own, back_other = from_share(back, yi)
    qkv_sum = qkv_sum.last()
    last = qkv_sum[0]
    totals = sums[0, 1536:] + swap(sums[0, 1536:], Y_BIT)
    totals = totals + tie(swap(totals, X_BIT), last)
    norms = jnp.sqrt(totals[:3] / totals[3])
    sums = lax.dynamic_index_in_dim(sums, zi, 0, False)
    other = tie(swap(sums, Y_BIT), last)
    sums = jnp.where(yi == 0, jnp.stack([sums, other]), jnp.stack([other, sums]))
    vecs = [sums[:, i * 128 : (i + 1) * 128].reshape(-1) for i in range(8)] + [sums[:, 1024:1536].reshape(-1)]
    grad_tokens = side_by_side(back_own, tie(back_other, last), yi, 1).astype(F32)
    grad_down = restore_rows(down, yi)
    (grad_up,) = restore_columns(up, 1, yi)
    grad_proj = restore_rows((proj[0], tie(proj[1], last)), yi)
    grad_query, grad_key, grad_value = restore_columns(qkv_sum, 3, yi)
    return (
        layer_out, grad_tokens, grad_query, vecs[0], grad_key, grad_value, vecs[1], grad_proj, vecs[2], vecs[3], vecs[4],
        grad_up, vecs[8], grad_down, vecs[5], vecs[6], vecs[7], norms,
    )


def gather_features(piece):
    return lax.all_gather(piece, "col", axis=1, tiled=True)


def scatter_features(partial_sum):
    low = partial_sum.astype(jnp.bfloat16)
    return lax.psum_scatter(low, "col", scatter_dimension=1, tiled=True).astype(F32)


def row_totals(first, second):
    return lax.psum((first, second), "col")


def gather_weights(w_query, w_key, w_value, w_up, w_proj, w_down):
    inner = (
        lax.all_gather(w_query, "row", axis=0, tiled=True),
        lax.all_gather(w_key, "row", axis=0, tiled=True),
        lax.all_gather(w_value, "row", axis=0, tiled=True),
        lax.all_gather(w_up, "row", axis=0, tiled=True),
    )
    outer = (
        lax.all_gather(w_proj, "row", axis=1, tiled=True),
        lax.all_gather(w_down, "row", axis=1, tiled=True),
    )
    return (inner, outer)


def norm_shares(resid, gain, shift):
    width = resid.shape[1] * lax.axis_size("col")
    total, squares = row_totals(jnp.sum(resid, axis=1), jnp.sum(resid * resid, axis=1))
    mean = total / width
    rstd = lax.rsqrt(squares / width - mean * mean + EPS)
    normed = (resid - mean[:, None]) * rstd[:, None]
    return (normed * gain + shift, normed, rstd)


def norm_back(upstream, normed, rstd, gain):
    width = upstream.shape[1] * lax.axis_size("col")
    scaled = upstream * gain
    total, along = row_totals(jnp.sum(scaled, axis=1), jnp.sum(scaled * normed, axis=1))
    back = rstd[:, None] * (scaled - total[:, None] / width - normed * (along[:, None] / width))
    return (back, jnp.sum(upstream * normed, axis=0), jnp.sum(upstream, axis=0))


def attend_forward(pack):
    queries, keys, values, ids = pack
    scale = queries.shape[2] ** (-0.5)
    block = min(512, queries.shape[0])
    same = ids[:, None] == ids[None, :]
    outputs = []
    logsums = []
    for begin in range(0, queries.shape[0], block):
        scores = (
            jnp.einsum(
                "qhd,khd->hqk",
                queries[begin : begin + block],
                keys,
                preferred_element_type=jnp.float32,
            )
            * scale
        )
        scores = jnp.where(same[None, begin : begin + block], scores, NEGATIVE)
        peak = jnp.max(scores, axis=2, keepdims=True)
        expo = jnp.exp(scores - peak)
        total = jnp.sum(expo, axis=2, keepdims=True)
        probs = (expo / total).astype(jnp.bfloat16)
        outputs.append(
            jnp.einsum("hqk,khd->qhd", probs, values, preferred_element_type=jnp.float32)
        )
        logsums.append((peak + jnp.log(total))[:, :, 0])
    return (jnp.concatenate(outputs, axis=0), jnp.concatenate(logsums, axis=1))


def attend_back(pack):
    queries, keys, values, ids, logsum, grad_out = pack
    scale = queries.shape[2] ** (-0.5)
    block = min(512, queries.shape[0])
    same = ids[:, None] == ids[None, :]
    grad_keys = jnp.zeros(keys.shape, jnp.float32)
    grad_values = jnp.zeros(values.shape, jnp.float32)
    grad_queries = []
    for begin in range(0, queries.shape[0], block):
        query_rows = queries[begin : begin + block]
        grad_rows = grad_out[begin : begin + block]
        scores = (
            jnp.einsum("qhd,khd->hqk", query_rows, keys, preferred_element_type=jnp.float32) * scale
        )
        scores = jnp.where(same[None, begin : begin + block], scores, NEGATIVE)
        probs = jnp.exp(scores - logsum[:, begin : begin + block, None])
        grad_probs = jnp.einsum(
            "qhd,khd->hqk", grad_rows, values, preferred_element_type=jnp.float32
        )
        inner = jnp.sum(probs * grad_probs, axis=2, keepdims=True)
        grad_scores = (probs * (grad_probs - inner)).astype(jnp.bfloat16)
        grad_queries.append(
            jnp.einsum("hqk,khd->qhd", grad_scores, keys, preferred_element_type=jnp.float32)
            * scale
        )
        grad_keys = (
            grad_keys
            + jnp.einsum(
                "hqk,qhd->khd", grad_scores, query_rows, preferred_element_type=jnp.float32
            )
            * scale
        )
        grad_values = grad_values + jnp.einsum(
            "hqk,qhd->khd",
            probs.astype(jnp.bfloat16),
            grad_rows,
            preferred_element_type=jnp.float32,
        )
    return (jnp.concatenate(grad_queries, axis=0), grad_keys, grad_values)


def per_device(
    tokens,
    lengths,
    w_query,
    b_query,
    w_key,
    w_value,
    b_value,
    w_proj,
    b_proj,
    norm_gain,
    norm_shift,
    w_up,
    b_up,
    w_down,
    b_down,
    final_gain,
    final_shift,
    cotangent,
):
    rows, share = tokens.shape
    heads = w_query.shape[1] // HD
    ids = segment_ids(lengths)
    seq_count = ids.shape[0]
    valid = (ids.reshape(rows) != lengths.shape[1] - 1).astype(jnp.float32)[:, None]
    inner, outer = gather_weights(w_query, w_key, w_value, w_up, w_proj, w_down)
    full_query, full_key, full_value, full_up = inner
    full_proj, full_down = outer
    stream = tokens.astype(jnp.float32)
    gathered = gather_features(tokens)
    queries = (jnp.dot(gathered, full_query, preferred_element_type=jnp.float32) + b_query).astype(
        jnp.bfloat16
    )
    keys = jnp.dot(gathered, full_key, preferred_element_type=jnp.float32).astype(jnp.bfloat16)
    values = (jnp.dot(gathered, full_value, preferred_element_type=jnp.float32) + b_value).astype(
        jnp.bfloat16
    )
    shape = (seq_count, LEN, heads, HD)
    query_seq = queries.reshape(shape)
    key_seq = keys.reshape(shape)
    value_seq = values.reshape(shape)
    mixed, logsum = lax.map(attend_forward, (query_seq, key_seq, value_seq, ids))
    heads_out = mixed.reshape(rows, heads * HD).astype(jnp.bfloat16)
    attn = (
        scatter_features(jnp.dot(heads_out, full_proj, preferred_element_type=jnp.float32)) + b_proj
    )
    hidden, normed_one, rstd_one = norm_shares(stream + attn, norm_gain, norm_shift)
    hidden_low = gather_features(hidden.astype(jnp.bfloat16))
    pre = jnp.dot(hidden_low, full_up, preferred_element_type=jnp.float32) + b_up
    act, gelu_back = jax.vjp(lambda inputs: jax.nn.gelu(inputs, approximate=True), pre)
    act_low = act.astype(jnp.bfloat16)
    ffn = scatter_features(jnp.dot(act_low, full_down, preferred_element_type=jnp.float32)) + b_down
    result, normed_two, rstd_two = norm_shares(hidden + ffn, final_gain, final_shift)
    totals = lax.psum(
        (
            jnp.sum(valid * stream * stream),
            jnp.sum(valid * attn * attn),
            jnp.sum(valid * ffn * ffn),
            jnp.sum(valid) * share,
        ),
        ("row", "col"),
    )
    norms = jnp.sqrt(jnp.stack([totals[0], totals[1], totals[2]]) / totals[3])
    back_inner, back_outer = gather_weights(w_query, w_key, w_value, w_up, w_proj, w_down)
    full_query, full_key, full_value, full_up = back_inner
    full_proj, full_down = back_outer
    grad_two, grad_fgain, grad_fshift = norm_back(
        cotangent.astype(jnp.float32), normed_two, rstd_two, final_gain
    )
    grad_ffn = grad_two.astype(jnp.bfloat16)
    grad_dbias = jnp.sum(grad_ffn.astype(jnp.float32), axis=0)
    ffn_wide = gather_features(grad_ffn)
    grad_down = jnp.einsum("tf,td->fd", act_low, ffn_wide, preferred_element_type=jnp.float32)
    grad_act = jnp.einsum("td,fd->tf", ffn_wide, full_down, preferred_element_type=jnp.float32)
    grad_pre = gelu_back(grad_act)[0].astype(jnp.bfloat16)
    grad_ubias = jnp.sum(grad_pre.astype(jnp.float32), axis=0)
    grad_up = jnp.einsum("td,tf->df", hidden_low, grad_pre, preferred_element_type=jnp.float32)
    grad_hidden = (
        scatter_features(
            jnp.einsum("tf,df->td", grad_pre, full_up, preferred_element_type=jnp.float32)
        )
        + grad_two
    )
    grad_one, grad_ngain, grad_nshift = norm_back(grad_hidden, normed_one, rstd_one, norm_gain)
    grad_attn = grad_one.astype(jnp.bfloat16)
    grad_pbias = jnp.sum(grad_attn.astype(jnp.float32), axis=0)
    attn_wide = gather_features(grad_attn)
    grad_proj = jnp.einsum("th,td->hd", heads_out, attn_wide, preferred_element_type=jnp.float32)
    grad_heads = jnp.einsum(
        "td,hd->th", attn_wide, full_proj, preferred_element_type=jnp.float32
    ).astype(jnp.bfloat16)
    back_query, back_key, back_value = lax.map(
        attend_back, (query_seq, key_seq, value_seq, ids, logsum, grad_heads.reshape(shape))
    )
    grad_queries = back_query.reshape(rows, heads * HD).astype(jnp.bfloat16)
    grad_keys = back_key.reshape(rows, heads * HD).astype(jnp.bfloat16)
    grad_values = back_value.reshape(rows, heads * HD).astype(jnp.bfloat16)
    grad_qbias = jnp.sum(grad_queries.astype(jnp.float32), axis=0)
    grad_vbias = jnp.sum(grad_values.astype(jnp.float32), axis=0)
    grad_query = jnp.einsum("td,th->dh", gathered, grad_queries, preferred_element_type=jnp.float32)
    grad_key = jnp.einsum("td,th->dh", gathered, grad_keys, preferred_element_type=jnp.float32)
    grad_value = jnp.einsum("td,th->dh", gathered, grad_values, preferred_element_type=jnp.float32)
    partial_back = (
        jnp.einsum("th,dh->td", grad_queries, full_query, preferred_element_type=jnp.float32)
        + jnp.einsum("th,dh->td", grad_keys, full_key, preferred_element_type=jnp.float32)
        + jnp.einsum("th,dh->td", grad_values, full_value, preferred_element_type=jnp.float32)
    )
    grad_tokens = scatter_features(partial_back) + grad_one
    grad_query, grad_key, grad_value, grad_up = (
        lax.psum_scatter(
            grad_query.astype(jnp.bfloat16), "row", scatter_dimension=0, tiled=True
        ).astype(jnp.float32),
        lax.psum_scatter(
            grad_key.astype(jnp.bfloat16), "row", scatter_dimension=0, tiled=True
        ).astype(jnp.float32),
        lax.psum_scatter(
            grad_value.astype(jnp.bfloat16), "row", scatter_dimension=0, tiled=True
        ).astype(jnp.float32),
        lax.psum_scatter(
            grad_up.astype(jnp.bfloat16), "row", scatter_dimension=0, tiled=True
        ).astype(jnp.float32),
    )
    grad_proj, grad_down = (
        lax.psum_scatter(
            grad_proj.astype(jnp.bfloat16), "row", scatter_dimension=1, tiled=True
        ).astype(jnp.float32),
        lax.psum_scatter(
            grad_down.astype(jnp.bfloat16), "row", scatter_dimension=1, tiled=True
        ).astype(jnp.float32),
    )
    vectors = lax.psum(
        (
            grad_qbias,
            grad_vbias,
            grad_pbias,
            grad_ngain,
            grad_nshift,
            grad_ubias,
            grad_dbias,
            grad_fgain,
            grad_fshift,
        ),
        "row",
    )
    return (
        result.astype(jnp.bfloat16),
        grad_tokens,
        grad_query,
        vectors[0],
        grad_key,
        grad_value,
        vectors[1],
        grad_proj,
        vectors[2],
        vectors[3],
        vectors[4],
        grad_up,
        vectors[5],
        grad_down,
        vectors[6],
        vectors[7],
        vectors[8],
        norms,
    )


def placements(row, col):
    grid, turned, share = P(row, col), P(col, row), P(col)
    args = (
        grid, P(row, None), grid, share, grid, grid, share, turned, share, share, share, grid, share, turned, share, share, share, grid,
    )
    outs = (
        grid, grid, grid, share, grid, grid, share, turned, share, share, share, grid, share, turned, share, share, share, P(),
    )
    return (args, outs)


def solution(mesh):
    if mesh.shape["row"] == 4 and mesh.shape["col"] == 8:
        mesh = Mesh(mesh.devices.reshape(2, 2, 4, 2), AXES)
        args, outs = placements(("y", "c"), ("z", "x"))
        body = square_device
    else:
        args, outs = placements("row", "col")
        body = per_device
    return jax.shard_map(body, mesh=mesh, in_specs=args, out_specs=outs, check_vma=False)
```

```python
import functools

import jax
import jax.numpy as jnp
from jax import lax
from jax.experimental import pallas as pl
from jax.experimental.pallas import tpu as pltpu
from jax.sharding import Mesh
from jax.sharding import PartitionSpec as P

HD = 128
LEN = 1024
EPS = 1e-06
NEGATIVE = -1000000000.0
BF = jnp.bfloat16
F32 = jnp.float32


def segment_ids(lengths):
    slots = lengths.shape[1]
    ends = jnp.cumsum(lengths, axis=1)
    places = jnp.arange(LEN, dtype=jnp.int32)
    hits = (places[None, :, None] >= ends[:, None, : slots - 1]).astype(jnp.int32)
    return jnp.sum(hits, axis=2)


AXES = ("y", "c", "z", "x")
X_BIT, Z_LOW, Z_HIGH, C_BIT, Y_BIT = 1, 2, 4, 8, 16
XY_BIT = X_BIT | Y_BIT
QUARTER = 512
HALF = LEN // 2
WIDTH = 2048
NN, NT, TN = ((1,), (0,)), ((1,), (1,)), ((0,), (0,))


def swap(piece, mask):
    return lax.ppermute(piece, AXES, [(i, i ^ mask) for i in range(32)])


def dot(left, right, dims):
    return lax.dot_general(left, right, (dims, ((), ())), preferred_element_type=F32)


def tie(value, *others):
    return lax.optimization_barrier((value, *others))[0]


class Order:
    def __init__(self, value):
        self.value = value

    def after(self, *others):
        self.value = tie(self.value, *others)


LESS = 4


def call(body, grid, spot, ins, in_specs, outs, out_specs, scratch, flops, size):
    result = pl.pallas_call(
        body,
        grid_spec=pltpu.PrefetchScalarGridSpec(
            num_scalar_prefetch=1, grid=grid, in_specs=in_specs, out_specs=out_specs, scratch_shapes=scratch
        ),
        out_shape=outs,
        compiler_params=pltpu.CompilerParams(
            dimension_semantics=("arbitrary",) * len(grid), vmem_limit_bytes=56 * 1024 * 1024
        ),
        cost_estimate=pl.CostEstimate(flops=flops // LESS, bytes_accessed=size // LESS, transcendentals=0),
    )(spot.value, *ins)
    spot.after(result[0])
    return result


def shape_of(*shape, dtype=F32):
    return jax.ShapeDtypeStruct(shape, dtype)


def fixed(shape):
    return pl.BlockSpec(shape, lambda *_: (0,) * len(shape))


def pick(low, high, first):
    return jnp.where(first, low[...], high[...])


SLOTS = (0, 2, 1, 3)


def wide_body(by_rows, finish, count, several, spot, *refs):
    pieces, weights, rest = refs[:8], refs[8], refs[9:]
    extra, outs, kept = rest[: -1 - count], rest[-1 - count : -1], rest[-1]
    t = pl.program_id(1)

    @pl.when(t == 0)
    def _():
        for slot, mask in enumerate(SLOTS):
            start = pl.multiple_of((spot[0] ^ mask) * 128, 128)
            for block in range(4):
                y, c = divmod(block, 2)
                y = y ^ spot[1]
                at = slot * QUARTER + block * 128
                for z in range(several):
                    if by_rows:
                        n = weights.shape[2]
                        part = weights[z, c, :, pl.ds(pl.multiple_of(y * 512 + start, 128), 128)]
                        kept[z * n : z * n + n, at : at + 128] = part
                    else:
                        kept[at : at + 128, :] = weights[0, c, y, pl.ds(start, 128), :]

    total = None
    for slot in range(4):
        tile = pick(pieces[2 * slot], pieces[2 * slot + 1], t == 0)
        part = slice(slot * QUARTER, slot * QUARTER + QUARTER)
        term = dot(tile, kept[:, part], NT) if by_rows else dot(tile, kept[part, :], NN)
        total = term if total is None else total + term
    finish(total, extra, outs)


def wide(pieces, weights, spot, by_rows, finish, extra, count, sums=0):
    if by_rows:
        n = weights.shape[1]
        weights = weights.reshape(4, 2, n, 1024)
        several = 4 if n < 256 else 1
        kept = pltpu.VMEM((several * n, WIDTH), BF)
    else:
        n = weights.shape[2]
        weights = weights.reshape(4, 2, 2, 512, n)
        several = 1
        kept = pltpu.VMEM((WIDTH, n), BF)
    block = (several,) + weights.shape[1:]
    tail = (0,) * (len(block) - 1)
    total = 4 * n
    n = several * n
    bias = pl.BlockSpec((1, n), lambda z, t, *_: (0, z))
    tile = pl.BlockSpec((HALF, n), lambda z, t, *_: (t, z))
    return call(
        functools.partial(wide_body, by_rows, finish, count + sums, several),
        (4 // several, 2),
        spot,
        (*pieces, weights, *extra),
        [fixed(p.shape) for p in pieces]
        + [pl.BlockSpec(block, lambda z, t, *_: (z,) + tail)]
        + [bias if e.shape[0] == 1 else tile for e in extra],
        [shape_of(LEN, total, dtype=BF)] * count + [shape_of(8, total)] * sums,
        [tile] * count + [pl.BlockSpec((8, n), lambda z, t, *_: (0, z))] * sums,
        [kept],
        2 * LEN * WIDTH * total,
        2 * (LEN * WIDTH + WIDTH * total + LEN * total),
    )


def finish_bias(total, extra, outs):
    outs[0][...] = (total + extra[0][...]).astype(BF)


def finish_plain(total, extra, outs):
    outs[0][...] = total.astype(BF)


def finish_gelu(total, extra, outs):
    pre = total + extra[0][...]
    square = pre * pre
    bend = jnp.tanh(0.7978845608028654 * pre * (1.0 + 0.044715 * square))
    rise = 0.5 * (1.0 + bend)
    outs[0][...] = (pre * rise).astype(BF)
    slope = 0.7978845608028654 * (1.0 + 0.134145 * square)
    outs[1][...] = (rise + 0.5 * pre * (1.0 - bend * bend) * slope).astype(BF)


def finish_slope(total, extra, outs):
    rounded = (total * extra[0][...].astype(F32)).astype(BF)
    outs[0][...] = rounded
    add_columns(outs[1], pl.program_id(1), [rounded.astype(F32)])


def partial_body(by_rows, n, spot, local, *rest):
    weights, (low, high) = rest[:-2], rest[-2:]
    t = pl.program_id(0)
    total = None
    for z in range(4):
        tile = local[:, z * n : (z + 1) * n]
        if by_rows:
            kept = jnp.concatenate([weights[y][z, c] for y in range(2) for c in range(2)], axis=1)
            term = dot(tile, kept, NN)
        else:
            kept = jnp.concatenate([weights[0][z, c, y ^ spot[1]] for y in range(2) for c in range(2)], axis=0)
            term = dot(tile, kept, NT)
        total = term if total is None else total + term

    @pl.when(t == 0)
    def _():
        low[...] = total.astype(low.dtype)

    @pl.when(t == 1)
    def _():
        high[...] = total.astype(high.dtype)


def partial(local, weights, spot, by_rows, mask, low, high):
    n = local.shape[1] // 4
    if by_rows:
        weights = weights.reshape(4, 2, n, 1024)
        specs = [
            pl.BlockSpec((4, 2, n, 128), functools.partial(lambda y, t, p: (0, 0, 0, (y ^ p[1]) * 4 + (p[0] ^ mask)), y))
            for y in range(2)
        ]
        ins = (weights, weights)
    else:
        weights = weights.reshape(4, 2, 2, 512, n)
        specs = [pl.BlockSpec((4, 2, 2, 128, n), lambda t, p: (0, 0, 0, p[0] ^ mask, 0))]
        ins = (weights,)
    return call(
        functools.partial(partial_body, by_rows, n),
        (2,),
        spot,
        (local, *ins),
        [pl.BlockSpec((HALF, 4 * n), lambda t, p: (t, 0))] + specs,
        [shape_of(HALF, QUARTER, dtype=low), shape_of(HALF, QUARTER, dtype=high)],
        [fixed((HALF, QUARTER))] * 2,
        [],
        2 * LEN * QUARTER * 4 * n,
        2 * (LEN * 4 * n + QUARTER * 4 * n + LEN * QUARTER),
    )


def grad_whole_body(by_rows, spot, *refs):
    pieces, local, out = refs[:8], refs[8], refs[9]
    for slot, mask in enumerate(SLOTS):
        start = pl.multiple_of((spot[0] ^ mask) * 128, 128)

        def term(piece, tile):
            return dot(tile, piece, TN) if by_rows else dot(piece, tile, TN)

        total = term(pieces[2 * slot][...], local[:HALF, :]) + term(pieces[2 * slot + 1][...], local[HALF:, :])
        for block in range(4):
            y, c = divmod(block, 2)
            y = y ^ spot[1]
            part = slice(block * 128, block * 128 + 128)
            if by_rows:
                out[0, c, :, pl.ds(pl.multiple_of(y * 512 + start, 128), 128)] = total[:, part].astype(BF)
            else:
                out[0, c, y, pl.ds(start, 128), :] = total[part, :].astype(BF)


def grad_whole(pieces, local, spot, by_rows):
    n = local.shape[1] // 4
    shape = (4, 2, n, 1024) if by_rows else (4, 2, 2, 512, n)
    tail = (0,) * (len(shape) - 1)
    (out,) = call(
        functools.partial(grad_whole_body, by_rows),
        (4,),
        spot,
        (*pieces, local),
        [fixed(p.shape) for p in pieces] + [pl.BlockSpec((LEN, n), lambda z, *_: (0, z))],
        [shape_of(*shape, dtype=BF)],
        [pl.BlockSpec((1,) + shape[1:], lambda z, *_: (z,) + tail)],
        [],
        2 * LEN * WIDTH * 4 * n,
        2 * (LEN * WIDTH + WIDTH * 4 * n + LEN * 4 * n),
    )
    return out.reshape(8, n, 1024) if by_rows else out.reshape(8, 1024, n)


def place_pair_body(spot, own, other, query, key, value, proj):
    for side, part in ((spot[1], own), (1 - spot[1], other)):
        at = pl.ds(pl.multiple_of(side * 128, 128), 128)
        for i, out in enumerate((query, key, value)):
            out[:, at] = part[:, i * 128 : i * 128 + 128].astype(F32)
        proj[at, :] = part[:, 384:].astype(F32).T


def place_pair(own, other, spot):
    grid = [shape_of(512, 256)] * 3 + [shape_of(256, 512)]
    return call(
        place_pair_body, (1,), spot, (own, other), [fixed((512, 512))] * 2, grid, [fixed(g.shape) for g in grid], [],
        2 * 512 * 512, 8 * 512 * 512,
    )


def grad_pair_body(spot, *refs):
    out = refs[18]
    for slot, mask in enumerate(SLOTS):
        start = pl.multiple_of((spot[0] ^ mask) * 128, 128)
        at = 0
        for pieces, local in ((refs[:8], refs[8]), (refs[9:17], refs[17])):
            total = dot(pieces[2 * slot][...], local[:HALF, :], TN) + dot(pieces[2 * slot + 1][...], local[HALF:, :], TN)
            n = local.shape[1]
            for block in range(4):
                y, c = divmod(block, 2)
                out[0, c, y ^ spot[1], pl.ds(start, 128), at : at + n] = total[block * 128 : block * 128 + 128, :].astype(BF)
            at += n


def grad_pair(first, first_local, second, second_local, spot):
    sizes = [local.shape[1] // 4 for local in (first_local, second_local)]
    n = sum(sizes)
    specs = [fixed(p.shape) for p in first]
    (out,) = call(
        grad_pair_body,
        (4,),
        spot,
        (*first, first_local, *second, second_local),
        specs + [pl.BlockSpec((LEN, sizes[0]), lambda z, *_: (0, z))] + specs + [pl.BlockSpec((LEN, sizes[1]), lambda z, *_: (0, z))],
        [shape_of(4, 2, 2, 512, n, dtype=BF)],
        [pl.BlockSpec((1, 2, 2, 512, n), lambda z, *_: (z, 0, 0, 0, 0))],
        [],
        2 * LEN * WIDTH * 4 * n,
        2 * (2 * LEN * WIDTH + WIDTH * 4 * n + LEN * 4 * n),
    )
    return out.reshape(8, 1024, n)


SCALE = HD ** (-0.5)
LOG2E = 1.4426950408889634
QUERY_BLOCK = 512


def forward_body(spot, queries, whole, ids_row, ids_column, out, logsum):
    scores = dot(whole[:, HD : 2 * HD], queries[:, :HD], NT)
    scores = jnp.where(ids_column[...] == ids_row[...], scores, NEGATIVE)
    peak = jnp.max(scores, axis=0, keepdims=True)
    expo = jnp.exp2((scores - peak) * (SCALE * LOG2E))
    total = jnp.sum(expo, axis=0, keepdims=True)
    probs = (expo * (1.0 / total)).astype(BF)
    mixed = dot(whole[:, 2 * HD :], probs, TN)
    out[...] = mixed.T.astype(BF)
    logsum[0] = peak * (SCALE * LOG2E) + jnp.log2(total)


def head_specs():
    return [
        pl.BlockSpec((QUERY_BLOCK, 3 * HD), lambda h, q, p: (q, h)),
        pl.BlockSpec((LEN, 3 * HD), lambda h, q, p: (0, h)),
        pl.BlockSpec((1, QUERY_BLOCK), lambda h, q, p: (0, q)),
        pl.BlockSpec((LEN, 1), lambda h, q, p: (0, 0)),
    ]


def attention(qkv, ids_row, ids_column, spot):
    return call(
        forward_body,
        (4, LEN // QUERY_BLOCK),
        spot,
        (qkv, qkv, ids_row, ids_column),
        head_specs(),
        [shape_of(LEN, QUARTER, dtype=BF), shape_of(4, 1, LEN)],
        [
            pl.BlockSpec((QUERY_BLOCK, HD), lambda h, q, p: (q, h)),
            pl.BlockSpec((1, 1, QUERY_BLOCK), lambda h, q, p: (h, 0, q)),
        ],
        [],
        64 * LEN * LEN * HD,
        LEN * 4 * HD * 8,
    )


def backward_body(spot, queries, whole, ids_row, ids_column, logsum, grad_out, out, sums, grad_keys, grad_values):
    q = pl.program_id(1)
    block = queries.shape[0]
    keys = whole[:, HD : 2 * HD]
    values = whole[:, 2 * HD :]
    scores = dot(keys, queries[:, :HD], NT) * (SCALE * LOG2E)
    scores = jnp.where(ids_column[...] == ids_row[...], scores, NEGATIVE)
    probs = jnp.exp2(scores - logsum[0])
    grad_probs = dot(values, grad_out[...], NT)
    inner = jnp.sum(probs * grad_probs, axis=0, keepdims=True)
    grad_scores = (probs * (grad_probs - inner)).astype(BF)
    back_query = dot(keys, grad_scores, TN)
    back_query = (back_query.T * SCALE).astype(BF)
    out[pl.ds(q * block, block), :HD] = back_query
    add_columns(sums.at[:, :HD], q, [back_query.astype(F32)])
    back_key = dot(grad_scores, queries[:, :HD], NN)
    back_value = dot(probs.astype(BF), grad_out[...], NN)

    @pl.when(q == 0)
    def _():
        grad_keys[...] = back_key
        grad_values[...] = back_value

    @pl.when(q > 0)
    def _():
        grad_keys[...] += back_key
        grad_values[...] += back_value

    @pl.when(q == pl.num_programs(1) - 1)
    def _():
        out[:, HD : 2 * HD] = (grad_keys[...] * SCALE).astype(BF)
        rounded = grad_values[...].astype(BF)
        out[:, 2 * HD :] = rounded
        sums[:, HD : 2 * HD] = jnp.zeros((8, HD), F32)
        sums[:, 2 * HD :] = column_sums([rounded.astype(F32)])


def attention_back(qkv, ids_row, ids_column, logsum, grad_heads, spot):
    return call(
        backward_body,
        (4, LEN // QUERY_BLOCK),
        spot,
        (qkv, qkv, ids_row, ids_column, logsum, grad_heads),
        head_specs()
        + [
            pl.BlockSpec((1, 1, QUERY_BLOCK), lambda h, q, p: (h, 0, q)),
            pl.BlockSpec((QUERY_BLOCK, HD), lambda h, q, p: (q, h)),
        ],
        [shape_of(LEN, 12 * HD, dtype=BF), shape_of(8, 12 * HD)],
        [pl.BlockSpec((LEN, 3 * HD), lambda h, q, p: (0, h)), pl.BlockSpec((8, 3 * HD), lambda h, q, p: (0, h))],
        [pltpu.VMEM((LEN, HD), F32), pltpu.VMEM((LEN, HD), F32)],
        120 * LEN * LEN * HD,
        LEN * 4 * HD * 16,
    )


def row_sum(value):
    folded = value[:, :128] + value[:, 128:256] + value[:, 256:384] + value[:, 384:512]
    return jnp.sum(folded.T, axis=0, keepdims=True)


def rows_of(values):
    rows = [row_sum(v) for v in values]
    return jnp.concatenate(rows + [jnp.zeros_like(rows[0])] * (8 - len(rows)), axis=0)


def columns_of(rows):
    return rows.T


def column_sums(values):
    sums = [jnp.sum(v, axis=0, keepdims=True) for v in values]
    return jnp.concatenate(sums + [jnp.zeros_like(sums[0])] * (8 - len(sums)), axis=0)


def add_columns(ref, t, values):
    sums = column_sums(values)

    @pl.when(t == 0)
    def _():
        ref[...] = sums

    @pl.when(t > 0)
    def _():
        ref[...] += sums


def moments_of(stats):
    total = (stats[0][...] + stats[1][...] + stats[2][...] + stats[3][...]) / WIDTH
    mean = total[0:1]
    return mean, lax.rsqrt(total[1:2] - mean * mean + EPS), total


def summed(refs, t):
    own, near, last = (pick(refs[2 * i], refs[2 * i + 1], t < STEPS // 2).astype(F32) for i in range(3))
    return own + near + last


STEP = 256
STEPS = LEN // STEP
LOW = pl.BlockSpec((STEP, QUARTER), lambda t, p: (jnp.minimum(t, STEPS // 2 - 1), 0))
HIGH = pl.BlockSpec((STEP, QUARTER), lambda t, p: (jnp.maximum(t - STEPS // 2, 0), 0))
PARTS = [LOW, HIGH] * 3
TILE = pl.BlockSpec((STEP, QUARTER), lambda t, p: (t, 0))
STATS = pl.BlockSpec((8, STEP), lambda t, p: (0, t))
VECTOR = fixed((1, QUARTER))
SUMS = fixed((8, QUARTER))
BLOCKS = pl.BlockSpec((4, STEP, 128), lambda t, p: (0, t, 0))


def elementwise(body, spot, ins, in_specs, outs, out_specs):
    return call(body, (STEPS,), spot, ins, in_specs, outs, out_specs, [], 20 * LEN * QUARTER, 16 * LEN * QUARTER)


def write_blocks(out, value):
    for z in range(4):
        out[z] = value[:, z * 128 : z * 128 + 128].astype(BF)


def norm_one_sums(spot, *refs):
    parts, (low, high, bias, resid, stats) = refs[:6], refs[6:]
    t = pl.program_id(0)
    attn = summed(parts, t) + bias[...]
    stream = pick(low, high, t < STEPS // 2).astype(F32)
    total = stream + attn
    resid[...] = total
    stats[...] = rows_of([total, total * total, attn * attn, stream * stream])


def write_halves(t, low, high, value):
    @pl.when(t < STEPS // 2)
    def _():
        low[...] = value

    @pl.when(t >= STEPS // 2)
    def _():
        high[...] = value


def norm_one(spot, resid, s0, s1, s2, s3, gain, shift, low, high, moments):
    mean, rstd, _ = moments_of((s0, s1, s2, s3))
    rows = jnp.concatenate([mean, rstd] + [mean] * 6, axis=0)
    moments[...] = rows
    columns = columns_of(rows)
    hidden = (resid[...] - columns[:, 0:1]) * columns[:, 1:2] * gain[...] + shift[...]
    write_halves(pl.program_id(0), low, high, hidden.astype(BF))


def norm_two_sums(spot, *refs):
    parts = refs[:6]
    bias, resid, moments, gain, shift, dy_low, dy_high, gain_two, resid_two, stats = refs[6:]
    t = pl.program_id(0)
    ffn = summed(parts, t) + bias[...]
    columns = columns_of(moments[...])
    hidden = (resid[...] - columns[:, 0:1]) * columns[:, 1:2] * gain[...] + shift[...]
    total = hidden + ffn
    resid_two[...] = total
    scaled = pick(dy_low, dy_high, t < STEPS // 2).astype(F32) * gain_two[...]
    stats[...] = rows_of([total, total * total, scaled, scaled * total, ffn * ffn])


def norm_two(spot, resid_two, s0, s1, s2, s3, dy_low, dy_high, gain, shift, layer_out, grad_two, low, high, sums):
    mean, rstd, total = moments_of((s0, s1, s2, s3))
    mean_e = total[2:3]
    along = rstd * (total[3:4] - mean * mean_e)
    columns = columns_of(jnp.concatenate([mean, rstd, mean_e, along] + [mean] * 4, axis=0))
    normed = (resid_two[...] - columns[:, 0:1]) * columns[:, 1:2]
    t = pl.program_id(0)
    upstream = pick(dy_low, dy_high, t < STEPS // 2).astype(F32)
    write_blocks(layer_out, normed * gain[...] + shift[...])
    back = columns[:, 1:2] * (upstream * gain[...] - columns[:, 2:3] - normed * columns[:, 3:4])
    grad_two[...] = back
    rounded = back.astype(BF)
    write_halves(t, low, high, rounded)
    add_columns(sums, t, [upstream * normed, upstream, rounded.astype(F32)])


def back_one_sums(spot, *refs):
    parts = refs[:6]
    grad_two, resid, moments, gain, grad_hidden, stats, sums = refs[6:]
    t = pl.program_id(0)
    upstream = summed(parts, t) + grad_two[...]
    grad_hidden[...] = upstream
    columns = columns_of(moments[...])
    normed = (resid[...] - columns[:, 0:1]) * columns[:, 1:2]
    scaled = upstream * gain[...]
    stats[...] = rows_of([scaled, scaled * normed])
    add_columns(sums, t, [upstream * normed, upstream])


def back_one(spot, grad_hidden, s0, s1, s2, s3, resid, moments, gain, grad_one, low, high, sums):
    total = (s0[...] + s1[...] + s2[...] + s3[...]) / WIDTH
    means = columns_of(total)
    columns = columns_of(moments[...])
    normed = (resid[...] - columns[:, 0:1]) * columns[:, 1:2]
    back = columns[:, 1:2] * (grad_hidden[...] * gain[...] - means[:, 0:1] - normed * means[:, 1:2])
    grad_one[...] = back
    rounded = back.astype(BF)
    t = pl.program_id(0)
    write_halves(t, low, high, rounded)
    add_columns(sums, t, [rounded.astype(F32)])


def finish_back(spot, *refs):
    parts, (grad_one, out) = refs[:6], refs[6:]
    write_blocks(out, summed(parts, pl.program_id(0)) + grad_one[...])


def pass_on(spot, first, second, third, fourth, low, high):
    low[...] = (first[...] + second[...].astype(F32)).astype(BF)
    high[...] = (third[...] + fourth[...].astype(F32)).astype(BF)


def split_y(piece, yi):
    return lax.dynamic_slice_in_dim(piece, yi * 128, 128, 1), lax.dynamic_slice_in_dim(piece, (1 - yi) * 128, 128, 1)


def spread_z(own, other, yi, zi, *after):
    both = jnp.concatenate([own.reshape(2, LEN, 128), other.reshape(2, LEN, 128)], axis=0)
    blocks = []
    for mask, bits in ((0, 0), (1, Z_LOW), (2, Z_HIGH), (3, Z_LOW | Z_HIGH)):
        block = lax.dynamic_index_in_dim(both, (zi ^ mask) ^ (yi * 2), 0, False)
        blocks.append(swap(tie(block, *after), bits) if mask else block)
    return blocks


def assemble_body(spot, *refs):
    blocks, (low, high) = refs[:4], refs[4:]
    t = pl.program_id(0)
    for out, when in ((low, t < STEPS // 2), (high, t >= STEPS // 2)):

        @pl.when(when)
        def _():
            for mask, block in enumerate(blocks):
                out[:, pl.ds(pl.multiple_of((spot[3] ^ mask) * 128, 128), 128)] = block[...]


def assemble_whole_body(spot, blocks, low, high):
    t = pl.program_id(0)
    whole = jnp.concatenate([blocks[z] for z in range(4)], axis=1)
    write_halves(t, low, high, whole)


def assemble_whole(blocks, spot):
    half = shape_of(HALF, QUARTER, dtype=BF)
    return elementwise(assemble_whole_body, spot, (blocks,), [BLOCKS], [half, half], [LOW, HIGH])


def assemble(blocks, spot):
    half = shape_of(HALF, QUARTER, dtype=BF)
    return elementwise(
        assemble_body, spot, blocks, [pl.BlockSpec((STEP, 128), lambda t, p: (t, 0))] * 4, [half, half], [LOW, HIGH]
    )


def from_share(share):
    return lax.all_to_all(share, "z", 0, 0, tiled=True).reshape(2, 2 * LEN, 128)


def swap_y(parts, yi):
    own = lax.dynamic_index_in_dim(parts, yi, 0, False)
    return own, swap(lax.dynamic_index_in_dim(parts, 1 - yi, 0, False), Y_BIT)


def side_by_side(own, other, yi, axis):
    return jnp.where(yi == 0, jnp.concatenate([own, other], axis), jnp.concatenate([other, own], axis))


def square_gather(low, high):
    x_low = swap(low, X_BIT)
    y_high = swap(high, Y_BIT)
    x_high = swap(high, X_BIT)
    y_low = swap(low, Y_BIT)
    xy_low = swap(x_low, Y_BIT)
    xy_high = swap(y_high, X_BIT)
    return (low, high, x_low, x_high, y_low, y_high, xy_low, xy_high)


def square_scatter(local, weights, spot, by_rows, first=lambda: None, middle=lambda: None, between=lambda: None, after=lambda: None):
    term = functools.partial(partial, local, weights, spot, by_rows)
    far_low, far_high = term(3, BF, BF)
    far_low = swap(far_low, X_BIT)
    far_high = swap(far_high, Y_BIT)
    near_low, x_high = term(2, BF, F32)
    near_low = swap(near_low, X_BIT)
    first()
    y_low, near_high = term(1, F32, BF)
    near_high = swap(near_high, Y_BIT)
    middle()
    half = fixed((HALF, QUARTER))
    last_low, last_high = call(
        pass_on, (1,), spot, (y_low, far_low, x_high, far_high), [half] * 4, [shape_of(HALF, QUARTER, dtype=BF)] * 2,
        [half] * 2, [], LEN * QUARTER, 8 * LEN * QUARTER,
    )
    last_low = swap(last_low, Y_BIT)
    last_high = swap(last_high, X_BIT)
    between()
    spot.after(near_low, near_high)
    own_low, own_high = term(0, F32, F32)
    after()
    return (own_low, own_high, near_low, near_high, last_low, last_high)


def square_stats(stats):
    return (stats, swap(stats, X_BIT), swap(stats, Y_BIT), swap(stats, XY_BIT))


def halve_columns(pieces, yi, *after):
    n = pieces[0].shape[1] // 2
    own = jnp.concatenate([lax.dynamic_slice_in_dim(p, yi * n, n, 1) for p in pieces], axis=1)
    send = tie(jnp.concatenate([lax.dynamic_slice_in_dim(p, (1 - yi) * n, n, 1) for p in pieces], axis=1), *after)
    return jnp.concatenate([own, swap(send, Y_BIT)], axis=0), send


def halve_rows(piece, yi, *after):
    n = piece.shape[0] // 2
    own = lax.dynamic_slice_in_dim(piece, yi * n, n, 0)
    send = tie(lax.dynamic_slice_in_dim(piece, (1 - yi) * n, n, 0), *after)
    return jnp.concatenate([own, swap(send, Y_BIT)], axis=1), send


def gather_zc(piece):
    return lax.all_gather(piece, ("z", "c"), axis=0)


def scatter_zc(full):
    return lax.psum_scatter(full, ("z", "c"), scatter_dimension=0)


def exchange_columns(piece):
    return piece[:512], swap(piece[512:], Y_BIT)


def exchange_rows(piece):
    return piece[:, :512], swap(piece[:, 512:], Y_BIT)


def restore_columns(pair, yi, begin=0, n=None):
    own, other = pair
    n = n or own.shape[1]
    own, other = own[:, begin : begin + n], other[:, begin : begin + n]
    return side_by_side(own.astype(F32), other.astype(F32), yi, 1)


def restore_rows(pair, yi):
    return side_by_side(pair[0].astype(F32), pair[1].astype(F32), yi, 0)


def square_device(
    tokens, lengths, w_query, b_query, w_key, w_value, b_value, w_proj, b_proj, norm_gain, norm_shift,
    w_up, b_up, w_down, b_down, final_gain, final_shift, cotangent,
):
    yi = lax.axis_index("y")
    zi = lax.axis_index("z")
    spot = Order(jnp.stack([lax.axis_index("x") * 2 + yi, yi, lax.axis_index("c"), zi]).astype(jnp.int32))

    token_own, token_send = split_y(tokens, yi)
    token_other = swap(token_send, Y_BIT)
    half_qkv, sent = halve_columns([w_query, w_key, w_value], yi, token_send)
    vectors = jnp.concatenate(
        [v.reshape(2, -1) for v in (b_query, b_value, b_proj, norm_gain, norm_shift, b_down, final_gain, final_shift, b_up)],
        axis=1,
    )
    vectors = lax.dynamic_slice_in_dim(vectors, yi, 1, 0)
    vectors = lax.all_to_all(jnp.broadcast_to(vectors, (4, vectors.shape[1])), "z", 0, 0, tiled=True)
    small = [vectors[:, i * 128 : (i + 1) * 128] for i in range(8)]
    q_bias, v_bias = small[:2]
    p_bias, n_gain, n_shift, d_bias, f_gain, f_shift = (v.reshape(1, QUARTER) for v in small[2:])
    u_bias = vectors[:, 1024:].reshape(1, -1)
    qkv_bias = jnp.stack([q_bias, jnp.zeros_like(q_bias), v_bias], axis=1).reshape(1, -1)

    both = side_by_side(lengths, swap(lengths, Y_BIT), yi, 0)
    ids = segment_ids(lax.dynamic_slice_in_dim(both, zi, 1, 0))[0]
    valid = (ids != lengths.shape[1] - 1).astype(F32)
    ids_row, ids_column = ids[None], ids[:, None]

    full_qkv = gather_zc(tie(half_qkv, vectors))
    token_blocks = spread_z(token_own, token_other, yi, zi)
    half_proj, sent = halve_rows(w_proj, yi, sent)
    half_up, sent = halve_columns([w_up], yi, sent)
    half_down, sent = halve_rows(w_down, yi, sent)
    spot.after(vectors, half_proj)
    token_low, token_high = assemble(token_blocks, spot)
    gathered = square_gather(token_low, token_high)
    full_proj = gather_zc(tie(half_proj, token_low))
    full_up = gather_zc(tie(half_up, token_low))
    full_down = gather_zc(tie(half_down, token_low))
    (qkv,) = wide(gathered, full_qkv, spot, False, finish_bias, (qkv_bias,), 1)
    heads_out, logsum = attention(qkv, ids_row, ids_column, spot)
    full = shape_of(LEN, QUARTER)
    low_half = shape_of(HALF, QUARTER, dtype=BF)
    stats_shape = shape_of(8, LEN)
    sums_shape = shape_of(8, QUARTER)

    parts = square_scatter(heads_out, full_proj, spot, True)
    resid, stats_one = elementwise(
        norm_one_sums, spot, (*parts, token_low, token_high, p_bias), PARTS + [LOW, HIGH, VECTOR], [full, stats_shape], [TILE, STATS]
    )
    hidden_low, hidden_high, moments = elementwise(
        norm_one, spot, (resid, *square_stats(stats_one), n_gain, n_shift), [TILE] + [STATS] * 4 + [VECTOR] * 2,
        [low_half, low_half, stats_shape], [LOW, HIGH, STATS],
    )
    hidden_wide = square_gather(hidden_low, hidden_high)
    dy_own, dy_send = split_y(tie(cotangent, hidden_low), yi)
    dy_other = swap(dy_send, Y_BIT)
    act, slope = wide(hidden_wide, full_up, spot, False, finish_gelu, (u_bias,), 2)
    dy = side_by_side(dy_own.reshape(2, LEN, 128), dy_other.reshape(2, LEN, 128), yi, 0)
    dy_blocks, dy_halves = [], []

    def first():
        dy_blocks.append(lax.all_to_all(tie(dy, spot.value), "z", 0, 0, tiled=True))

    def after():
        dy_halves.extend(assemble_whole(dy_blocks[0], spot))

    parts = square_scatter(act, full_down, spot, True, first=first, after=after)
    resid_two, stats_two = elementwise(
        norm_two_sums, spot, (*parts, d_bias, resid, moments, n_gain, n_shift, *dy_halves, f_gain),
        PARTS + [VECTOR, TILE, STATS, VECTOR, VECTOR, LOW, HIGH, VECTOR], [full, stats_shape], [TILE, STATS],
    )
    layer_share, grad_two, ffn_low, ffn_high, sums_two = elementwise(
        norm_two, spot, (resid_two, *square_stats(stats_two), *dy_halves, f_gain, f_shift),
        [TILE] + [STATS] * 4 + [LOW, HIGH, VECTOR, VECTOR],
        [shape_of(4, LEN, 128, dtype=BF), full, low_half, low_half, sums_shape], [BLOCKS, TILE, LOW, HIGH, SUMS],
    )
    ffn_wide = square_gather(ffn_low, ffn_high)
    down = grad_whole(ffn_wide, act, spot, True)
    grad_down = scatter_zc(down)
    layer_parts = from_share(tie(layer_share, down))
    grad_pre, sums_up = wide(ffn_wide, full_down, spot, True, finish_slope, (slope,), 1, 1)
    up = []

    def after():
        spot.after(layer_parts)
        up.append(grad_whole(hidden_wide, grad_pre, spot, False))

    parts = square_scatter(grad_pre, full_up, spot, False, after=after)
    grad_hidden, stats_back, sums_back = elementwise(
        back_one_sums, spot, (*parts, grad_two, resid, moments, n_gain),
        PARTS + [TILE, TILE, STATS, VECTOR], [full, stats_shape, sums_shape], [TILE, STATS, SUMS],
    )
    grad_one, attn_low, attn_high, sums_attn = elementwise(
        back_one, spot, (grad_hidden, *square_stats(stats_back), resid, moments, n_gain),
        [TILE] + [STATS] * 4 + [TILE, STATS, VECTOR],
        [full, low_half, low_half, sums_shape], [TILE, LOW, HIGH, SUMS],
    )
    attn_wide = square_gather(attn_low, attn_high)
    grad_up = scatter_zc(tie(up[0], spot.value))
    spot.after(grad_down)
    (grad_heads,) = wide(attn_wide, full_proj, spot, True, finish_plain, (), 1)
    layer_own, layer_other = swap_y(tie(layer_parts, grad_heads), yi)
    down = exchange_rows(tie(grad_down, grad_heads))
    grad_qkv, sums_qkv = attention_back(qkv, ids_row, ids_column, logsum, grad_heads, spot)
    spot.after(layer_other, down[1])
    sum_last = scatter_zc(grad_pair(gathered, grad_qkv, attn_wide, heads_out, spot))

    kept = []

    def between():
        totals = jnp.stack([tie(stats_one[3], spot.value) * valid, stats_one[2] * valid, stats_two[4] * valid, valid * QUARTER])
        totals = jnp.pad(jnp.sum(totals, axis=1)[None], ((0, 3), (0, 124)))
        vector_sums = jnp.concatenate(
            [
                v.reshape(4, -1)
                for v in (
                    *(tie(sums_qkv[0], spot.value).reshape(4, 3, HD)[:, i] for i in (0, 2)),
                    sums_attn[0], sums_back[0], sums_back[1], sums_two[2], sums_two[0], sums_two[1], sums_up[0], totals,
                )
            ],
            axis=1,
        )
        kept.append((vector_sums, swap(vector_sums, C_BIT)))

    parts = square_scatter(grad_qkv, full_qkv, spot, False, between=between)
    (back,) = elementwise(
        finish_back, spot, (*parts, grad_one), PARTS + [TILE], [shape_of(4, LEN, 128, dtype=BF)], [BLOCKS]
    )
    back_parts = from_share(back)
    up = exchange_columns(tie(grad_up, back))
    sums = kept[0][0] + tie(kept[0][1], back)
    sums = sums + tie(swap(sums, Z_LOW), up[1])
    back_own, back_other = swap_y(back_parts, yi)
    sums = sums + tie(swap(sums, Z_HIGH), back_other)
    last = swap(sum_last[512:], Y_BIT)
    totals = sums[0, 1536:] + swap(sums[0, 1536:], Y_BIT)
    totals = totals + swap(totals, X_BIT)
    norms = jnp.sqrt(totals[:3] / totals[3])
    sums = lax.dynamic_index_in_dim(sums, zi, 0, False)
    other = swap(sums, Y_BIT)
    sums = jnp.where(yi == 0, jnp.stack([sums, other]), jnp.stack([other, sums]))
    vecs = [sums[:, i * 128 : (i + 1) * 128].reshape(-1) for i in range(8)] + [sums[:, 1024:1536].reshape(-1)]
    layer_out = side_by_side(tie(layer_own, back), layer_other, yi, 1)
    grad_tokens = side_by_side(back_own, back_other, yi, 1).astype(F32)
    grad_down = restore_rows((tie(down[0], back), down[1]), yi)
    grad_up = restore_columns(up, yi)
    grad_query, grad_key, grad_value, grad_proj = place_pair(sum_last, last, spot)
    return (
        layer_out, grad_tokens, grad_query, vecs[0], grad_key, grad_value, vecs[1], grad_proj, vecs[2], vecs[3], vecs[4],
        grad_up, vecs[8], grad_down, vecs[5], vecs[6], vecs[7], norms,
    )


def gather_features(piece):
    return lax.all_gather(piece, "col", axis=1, tiled=True)


def scatter_features(partial_sum):
    low = partial_sum.astype(jnp.bfloat16)
    return lax.psum_scatter(low, "col", scatter_dimension=1, tiled=True).astype(F32)


def row_totals(first, second):
    return lax.psum((first, second), "col")


def gather_weights(w_query, w_key, w_value, w_up, w_proj, w_down):
    inner = (
        lax.all_gather(w_query, "row", axis=0, tiled=True),
        lax.all_gather(w_key, "row", axis=0, tiled=True),
        lax.all_gather(w_value, "row", axis=0, tiled=True),
        lax.all_gather(w_up, "row", axis=0, tiled=True),
    )
    outer = (
        lax.all_gather(w_proj, "row", axis=1, tiled=True),
        lax.all_gather(w_down, "row", axis=1, tiled=True),
    )
    return (inner, outer)


def norm_shares(resid, gain, shift):
    width = resid.shape[1] * lax.axis_size("col")
    total, squares = row_totals(jnp.sum(resid, axis=1), jnp.sum(resid * resid, axis=1))
    mean = total / width
    rstd = lax.rsqrt(squares / width - mean * mean + EPS)
    normed = (resid - mean[:, None]) * rstd[:, None]
    return (normed * gain + shift, normed, rstd)


def norm_back(upstream, normed, rstd, gain):
    width = upstream.shape[1] * lax.axis_size("col")
    scaled = upstream * gain
    total, along = row_totals(jnp.sum(scaled, axis=1), jnp.sum(scaled * normed, axis=1))
    back = rstd[:, None] * (scaled - total[:, None] / width - normed * (along[:, None] / width))
    return (back, jnp.sum(upstream * normed, axis=0), jnp.sum(upstream, axis=0))


def attend_forward(pack):
    queries, keys, values, ids = pack
    scale = queries.shape[2] ** (-0.5)
    block = min(512, queries.shape[0])
    same = ids[:, None] == ids[None, :]
    outputs = []
    logsums = []
    for begin in range(0, queries.shape[0], block):
        scores = (
            jnp.einsum(
                "qhd,khd->hqk",
                queries[begin : begin + block],
                keys,
                preferred_element_type=jnp.float32,
            )
            * scale
        )
        scores = jnp.where(same[None, begin : begin + block], scores, NEGATIVE)
        peak = jnp.max(scores, axis=2, keepdims=True)
        expo = jnp.exp(scores - peak)
        total = jnp.sum(expo, axis=2, keepdims=True)
        probs = (expo / total).astype(jnp.bfloat16)
        outputs.append(
            jnp.einsum("hqk,khd->qhd", probs, values, preferred_element_type=jnp.float32)
        )
        logsums.append((peak + jnp.log(total))[:, :, 0])
    return (jnp.concatenate(outputs, axis=0), jnp.concatenate(logsums, axis=1))


def attend_back(pack):
    queries, keys, values, ids, logsum, grad_out = pack
    scale = queries.shape[2] ** (-0.5)
    block = min(512, queries.shape[0])
    same = ids[:, None] == ids[None, :]
    grad_keys = jnp.zeros(keys.shape, jnp.float32)
    grad_values = jnp.zeros(values.shape, jnp.float32)
    grad_queries = []
    for begin in range(0, queries.shape[0], block):
        query_rows = queries[begin : begin + block]
        grad_rows = grad_out[begin : begin + block]
        scores = (
            jnp.einsum("qhd,khd->hqk", query_rows, keys, preferred_element_type=jnp.float32) * scale
        )
        scores = jnp.where(same[None, begin : begin + block], scores, NEGATIVE)
        probs = jnp.exp(scores - logsum[:, begin : begin + block, None])
        grad_probs = jnp.einsum(
            "qhd,khd->hqk", grad_rows, values, preferred_element_type=jnp.float32
        )
        inner = jnp.sum(probs * grad_probs, axis=2, keepdims=True)
        grad_scores = (probs * (grad_probs - inner)).astype(jnp.bfloat16)
        grad_queries.append(
            jnp.einsum("hqk,khd->qhd", grad_scores, keys, preferred_element_type=jnp.float32)
            * scale
        )
        grad_keys = (
            grad_keys
            + jnp.einsum(
                "hqk,qhd->khd", grad_scores, query_rows, preferred_element_type=jnp.float32
            )
            * scale
        )
        grad_values = grad_values + jnp.einsum(
            "hqk,qhd->khd",
            probs.astype(jnp.bfloat16),
            grad_rows,
            preferred_element_type=jnp.float32,
        )
    return (jnp.concatenate(grad_queries, axis=0), grad_keys, grad_values)


def per_device(
    tokens,
    lengths,
    w_query,
    b_query,
    w_key,
    w_value,
    b_value,
    w_proj,
    b_proj,
    norm_gain,
    norm_shift,
    w_up,
    b_up,
    w_down,
    b_down,
    final_gain,
    final_shift,
    cotangent,
):
    rows, share = tokens.shape
    heads = w_query.shape[1] // HD
    ids = segment_ids(lengths)
    seq_count = ids.shape[0]
    valid = (ids.reshape(rows) != lengths.shape[1] - 1).astype(jnp.float32)[:, None]
    inner, outer = gather_weights(w_query, w_key, w_value, w_up, w_proj, w_down)
    full_query, full_key, full_value, full_up = inner
    full_proj, full_down = outer
    stream = tokens.astype(jnp.float32)
    gathered = gather_features(tokens)
    queries = (jnp.dot(gathered, full_query, preferred_element_type=jnp.float32) + b_query).astype(
        jnp.bfloat16
    )
    keys = jnp.dot(gathered, full_key, preferred_element_type=jnp.float32).astype(jnp.bfloat16)
    values = (jnp.dot(gathered, full_value, preferred_element_type=jnp.float32) + b_value).astype(
        jnp.bfloat16
    )
    shape = (seq_count, LEN, heads, HD)
    query_seq = queries.reshape(shape)
    key_seq = keys.reshape(shape)
    value_seq = values.reshape(shape)
    mixed, logsum = lax.map(attend_forward, (query_seq, key_seq, value_seq, ids))
    heads_out = mixed.reshape(rows, heads * HD).astype(jnp.bfloat16)
    attn = (
        scatter_features(jnp.dot(heads_out, full_proj, preferred_element_type=jnp.float32)) + b_proj
    )
    hidden, normed_one, rstd_one = norm_shares(stream + attn, norm_gain, norm_shift)
    hidden_low = gather_features(hidden.astype(jnp.bfloat16))
    pre = jnp.dot(hidden_low, full_up, preferred_element_type=jnp.float32) + b_up
    act, gelu_back = jax.vjp(lambda inputs: jax.nn.gelu(inputs, approximate=True), pre)
    act_low = act.astype(jnp.bfloat16)
    ffn = scatter_features(jnp.dot(act_low, full_down, preferred_element_type=jnp.float32)) + b_down
    result, normed_two, rstd_two = norm_shares(hidden + ffn, final_gain, final_shift)
    totals = lax.psum(
        (
            jnp.sum(valid * stream * stream),
            jnp.sum(valid * attn * attn),
            jnp.sum(valid * ffn * ffn),
            jnp.sum(valid) * share,
        ),
        ("row", "col"),
    )
    norms = jnp.sqrt(jnp.stack([totals[0], totals[1], totals[2]]) / totals[3])
    back_inner, back_outer = gather_weights(w_query, w_key, w_value, w_up, w_proj, w_down)
    full_query, full_key, full_value, full_up = back_inner
    full_proj, full_down = back_outer
    grad_two, grad_fgain, grad_fshift = norm_back(
        cotangent.astype(jnp.float32), normed_two, rstd_two, final_gain
    )
    grad_ffn = grad_two.astype(jnp.bfloat16)
    grad_dbias = jnp.sum(grad_ffn.astype(jnp.float32), axis=0)
    ffn_wide = gather_features(grad_ffn)
    grad_down = jnp.einsum("tf,td->fd", act_low, ffn_wide, preferred_element_type=jnp.float32)
    grad_act = jnp.einsum("td,fd->tf", ffn_wide, full_down, preferred_element_type=jnp.float32)
    grad_pre = gelu_back(grad_act)[0].astype(jnp.bfloat16)
    grad_ubias = jnp.sum(grad_pre.astype(jnp.float32), axis=0)
    grad_up = jnp.einsum("td,tf->df", hidden_low, grad_pre, preferred_element_type=jnp.float32)
    grad_hidden = (
        scatter_features(
            jnp.einsum("tf,df->td", grad_pre, full_up, preferred_element_type=jnp.float32)
        )
        + grad_two
    )
    grad_one, grad_ngain, grad_nshift = norm_back(grad_hidden, normed_one, rstd_one, norm_gain)
    grad_attn = grad_one.astype(jnp.bfloat16)
    grad_pbias = jnp.sum(grad_attn.astype(jnp.float32), axis=0)
    attn_wide = gather_features(grad_attn)
    grad_proj = jnp.einsum("th,td->hd", heads_out, attn_wide, preferred_element_type=jnp.float32)
    grad_heads = jnp.einsum(
        "td,hd->th", attn_wide, full_proj, preferred_element_type=jnp.float32
    ).astype(jnp.bfloat16)
    back_query, back_key, back_value = lax.map(
        attend_back, (query_seq, key_seq, value_seq, ids, logsum, grad_heads.reshape(shape))
    )
    grad_queries = back_query.reshape(rows, heads * HD).astype(jnp.bfloat16)
    grad_keys = back_key.reshape(rows, heads * HD).astype(jnp.bfloat16)
    grad_values = back_value.reshape(rows, heads * HD).astype(jnp.bfloat16)
    grad_qbias = jnp.sum(grad_queries.astype(jnp.float32), axis=0)
    grad_vbias = jnp.sum(grad_values.astype(jnp.float32), axis=0)
    grad_query = jnp.einsum("td,th->dh", gathered, grad_queries, preferred_element_type=jnp.float32)
    grad_key = jnp.einsum("td,th->dh", gathered, grad_keys, preferred_element_type=jnp.float32)
    grad_value = jnp.einsum("td,th->dh", gathered, grad_values, preferred_element_type=jnp.float32)
    partial_back = (
        jnp.einsum("th,dh->td", grad_queries, full_query, preferred_element_type=jnp.float32)
        + jnp.einsum("th,dh->td", grad_keys, full_key, preferred_element_type=jnp.float32)
        + jnp.einsum("th,dh->td", grad_values, full_value, preferred_element_type=jnp.float32)
    )
    grad_tokens = scatter_features(partial_back) + grad_one
    grad_query, grad_key, grad_value, grad_up = (
        lax.psum_scatter(
            grad_query.astype(jnp.bfloat16), "row", scatter_dimension=0, tiled=True
        ).astype(jnp.float32),
        lax.psum_scatter(
            grad_key.astype(jnp.bfloat16), "row", scatter_dimension=0, tiled=True
        ).astype(jnp.float32),
        lax.psum_scatter(
            grad_value.astype(jnp.bfloat16), "row", scatter_dimension=0, tiled=True
        ).astype(jnp.float32),
        lax.psum_scatter(
            grad_up.astype(jnp.bfloat16), "row", scatter_dimension=0, tiled=True
        ).astype(jnp.float32),
    )
    grad_proj, grad_down = (
        lax.psum_scatter(
            grad_proj.astype(jnp.bfloat16), "row", scatter_dimension=1, tiled=True
        ).astype(jnp.float32),
        lax.psum_scatter(
            grad_down.astype(jnp.bfloat16), "row", scatter_dimension=1, tiled=True
        ).astype(jnp.float32),
    )
    vectors = lax.psum(
        (
            grad_qbias,
            grad_vbias,
            grad_pbias,
            grad_ngain,
            grad_nshift,
            grad_ubias,
            grad_dbias,
            grad_fgain,
            grad_fshift,
        ),
        "row",
    )
    return (
        result.astype(jnp.bfloat16),
        grad_tokens,
        grad_query,
        vectors[0],
        grad_key,
        grad_value,
        vectors[1],
        grad_proj,
        vectors[2],
        vectors[3],
        vectors[4],
        grad_up,
        vectors[5],
        grad_down,
        vectors[6],
        vectors[7],
        vectors[8],
        norms,
    )


def placements(row, col):
    grid, turned, share = P(row, col), P(col, row), P(col)
    args = (
        grid, P(row, None), grid, share, grid, grid, share, turned, share, share, share, grid, share, turned, share, share, share, grid,
    )
    outs = (
        grid, grid, grid, share, grid, grid, share, turned, share, share, share, grid, share, turned, share, share, share, P(),
    )
    return (args, outs)


def solution(mesh):
    if mesh.shape["row"] == 4 and mesh.shape["col"] == 8:
        mesh = Mesh(mesh.devices.reshape(2, 2, 4, 2), AXES)
        args, outs = placements(("y", "c"), ("z", "x"))
        body = square_device
    else:
        args, outs = placements("row", "col")
        body = per_device
    return jax.shard_map(body, mesh=mesh, in_specs=args, out_specs=outs, check_vma=False)
```

```python
import functools

import jax
import jax.numpy as jnp
from jax import lax
from jax.experimental import pallas as pl
from jax.experimental.pallas import tpu as pltpu
from jax.sharding import Mesh
from jax.sharding import PartitionSpec as P

HD = 128
LEN = 1024
EPS = 1e-06
NEGATIVE = -1000000000.0
BF = jnp.bfloat16
F32 = jnp.float32


def segment_ids(lengths):
    slots = lengths.shape[1]
    ends = jnp.cumsum(lengths, axis=1)
    places = jnp.arange(LEN, dtype=jnp.int32)
    hits = (places[None, :, None] >= ends[:, None, : slots - 1]).astype(jnp.int32)
    return jnp.sum(hits, axis=2)


AXES = ("y", "c", "z", "x")
X_BIT, Z_LOW, Z_HIGH, C_BIT, Y_BIT = 1, 2, 4, 8, 16
XY_BIT = X_BIT | Y_BIT
QUARTER = 512
HALF = LEN // 2
WIDTH = 2048
NN, NT, TN = ((1,), (0,)), ((1,), (1,)), ((0,), (0,))


def swap(piece, mask):
    return lax.ppermute(piece, AXES, [(i, i ^ mask) for i in range(32)])


def dot(left, right, dims):
    return lax.dot_general(left, right, (dims, ((), ())), preferred_element_type=F32)


def tie(value, *others):
    return lax.optimization_barrier((value, *others))[0]


class Order:
    def __init__(self, value):
        self.value = value

    def after(self, *others):
        self.value = tie(self.value, *others)


LESS = 4


def call(body, grid, spot, ins, in_specs, outs, out_specs, scratch, flops, size):
    result = pl.pallas_call(
        body,
        grid_spec=pltpu.PrefetchScalarGridSpec(
            num_scalar_prefetch=1, grid=grid, in_specs=in_specs, out_specs=out_specs, scratch_shapes=scratch
        ),
        out_shape=outs,
        compiler_params=pltpu.CompilerParams(
            dimension_semantics=("arbitrary",) * len(grid), vmem_limit_bytes=56 * 1024 * 1024
        ),
        cost_estimate=pl.CostEstimate(flops=flops // LESS, bytes_accessed=size // LESS, transcendentals=0),
    )(spot.value, *ins)
    spot.after(result[0])
    return result


def shape_of(*shape, dtype=F32):
    return jax.ShapeDtypeStruct(shape, dtype)


def fixed(shape):
    return pl.BlockSpec(shape, lambda *_: (0,) * len(shape))


def pick(low, high, first):
    return jnp.where(first, low[...], high[...])


SLOTS = (0, 2, 1, 3)


def wide_body(by_rows, finish, count, several, spot, *refs):
    pieces, weights, rest = refs[:8], refs[8], refs[9:]
    extra, outs, kept = rest[: -1 - count], rest[-1 - count : -1], rest[-1]
    t = pl.program_id(1)

    @pl.when(t == 0)
    def _():
        for slot, mask in enumerate(SLOTS):
            start = pl.multiple_of((spot[0] ^ mask) * 128, 128)
            for block in range(4):
                y, c = divmod(block, 2)
                y = y ^ spot[1]
                at = slot * QUARTER + block * 128
                for z in range(several):
                    if by_rows:
                        kept[:, at : at + 128] = weights[0, c, :, pl.ds(pl.multiple_of(y * 512 + start, 128), 128)]
                    else:
                        n = weights.shape[4]
                        kept[at : at + 128, z * n : z * n + n] = weights[z, c, y, pl.ds(start, 128), :]

    total = None
    for slot in range(4):
        tile = pick(pieces[2 * slot], pieces[2 * slot + 1], t == 0)
        part = slice(slot * QUARTER, slot * QUARTER + QUARTER)
        term = dot(tile, kept[:, part], NT) if by_rows else dot(tile, kept[part, :], NN)
        total = term if total is None else total + term
    finish(total, extra, outs)


def wide(pieces, weights, spot, by_rows, finish, extra, count, sums=0, n=None, lane=0):
    several = 1
    if by_rows:
        n = weights.shape[1]
        weights = weights.reshape(4, 2, n, 1024)
        kept = pltpu.VMEM((n, WIDTH), BF)
        block = (1, 2, n, 1024)
    else:
        n = n or weights.shape[2]
        weights = weights.reshape(4, 2, 2, 512, weights.shape[2])
        several = 4 if n < 256 else 1
        kept = pltpu.VMEM((WIDTH, several * n), BF)
        block = (several, 2, 2, 512, n)
    tail = (0,) * (len(block) - 2) + (lane,)
    total = 4 * n
    n = several * n
    bias = pl.BlockSpec((1, n), lambda z, t, *_: (0, z))
    tile = pl.BlockSpec((HALF, n), lambda z, t, *_: (t, z))
    return call(
        functools.partial(wide_body, by_rows, finish, count + sums, several),
        (4 // several, 2),
        spot,
        (*pieces, weights, *extra),
        [fixed(p.shape) for p in pieces]
        + [pl.BlockSpec(block, lambda z, t, *_: (z,) + tail)]
        + [bias if e.shape[0] == 1 else tile for e in extra],
        [shape_of(LEN, total, dtype=BF)] * count + [shape_of(8, total)] * sums,
        [tile] * count + [pl.BlockSpec((8, n), lambda z, t, *_: (0, z))] * sums,
        [kept],
        2 * LEN * WIDTH * total,
        2 * (LEN * WIDTH + WIDTH * total + LEN * total),
    )


def finish_bias(total, extra, outs):
    outs[0][...] = (total + extra[0][...]).astype(BF)


def finish_plain(total, extra, outs):
    outs[0][...] = total.astype(BF)


def finish_gelu(total, extra, outs):
    pre = total + extra[0][...]
    square = pre * pre
    bend = jnp.tanh(0.7978845608028654 * pre * (1.0 + 0.044715 * square))
    rise = 0.5 * (1.0 + bend)
    outs[0][...] = (pre * rise).astype(BF)
    slope = 0.7978845608028654 * (1.0 + 0.134145 * square)
    outs[1][...] = (rise + 0.5 * pre * (1.0 - bend * bend) * slope).astype(BF)


def finish_slope(total, extra, outs):
    rounded = (total * extra[0][...].astype(F32)).astype(BF)
    outs[0][...] = rounded
    add_columns(outs[1], pl.program_id(1), [rounded.astype(F32)])


def partial_body(by_rows, n, spot, local, *rest):
    weights, (low, high) = rest[:-2], rest[-2:]
    t = pl.program_id(0)
    total = None
    for z in range(4):
        tile = local[:, z * n : (z + 1) * n]
        if by_rows:
            kept = jnp.concatenate([weights[y][z, c] for y in range(2) for c in range(2)], axis=1)
            term = dot(tile, kept, NN)
        else:
            kept = jnp.concatenate([weights[0][z, c, y ^ spot[1]] for y in range(2) for c in range(2)], axis=0)
            term = dot(tile, kept, NT)
        total = term if total is None else total + term

    @pl.when(t == 0)
    def _():
        low[...] = total.astype(low.dtype)

    @pl.when(t == 1)
    def _():
        high[...] = total.astype(high.dtype)


def partial(local, weights, spot, by_rows, lane, mask, low, high):
    n = local.shape[1] // 4
    if by_rows:
        weights = weights.reshape(4, 2, n, 1024)
        specs = [
            pl.BlockSpec((4, 2, n, 128), functools.partial(lambda y, t, p: (0, 0, 0, (y ^ p[1]) * 4 + (p[0] ^ mask)), y))
            for y in range(2)
        ]
        ins = (weights, weights)
    else:
        weights = weights.reshape(4, 2, 2, 512, weights.shape[2])
        specs = [pl.BlockSpec((4, 2, 2, 128, n), lambda t, p: (0, 0, 0, p[0] ^ mask, lane))]
        ins = (weights,)
    return call(
        functools.partial(partial_body, by_rows, n),
        (2,),
        spot,
        (local, *ins),
        [pl.BlockSpec((HALF, 4 * n), lambda t, p: (t, 0))] + specs,
        [shape_of(HALF, QUARTER, dtype=low), shape_of(HALF, QUARTER, dtype=high)],
        [fixed((HALF, QUARTER))] * 2,
        [],
        2 * LEN * QUARTER * 4 * n,
        2 * (LEN * 4 * n + QUARTER * 4 * n + LEN * QUARTER),
    )


def grad_whole_body(by_rows, spot, *refs):
    pieces, local, out = refs[:8], refs[8], refs[9]
    for slot, mask in enumerate(SLOTS):
        start = pl.multiple_of((spot[0] ^ mask) * 128, 128)

        def term(piece, tile):
            return dot(tile, piece, TN) if by_rows else dot(piece, tile, TN)

        total = term(pieces[2 * slot][...], local[:HALF, :]) + term(pieces[2 * slot + 1][...], local[HALF:, :])
        for block in range(4):
            y, c = divmod(block, 2)
            y = y ^ spot[1]
            part = slice(block * 128, block * 128 + 128)
            if by_rows:
                out[0, c, :, pl.ds(pl.multiple_of(y * 512 + start, 128), 128)] = total[:, part].astype(BF)
            else:
                out[0, c, y, pl.ds(start, 128), :] = total[part, :].astype(BF)


def grad_whole(pieces, local, spot, by_rows):
    n = local.shape[1] // 4
    shape = (4, 2, n, 1024) if by_rows else (4, 2, 2, 512, n)
    tail = (0,) * (len(shape) - 1)
    (out,) = call(
        functools.partial(grad_whole_body, by_rows),
        (4,),
        spot,
        (*pieces, local),
        [fixed(p.shape) for p in pieces] + [pl.BlockSpec((LEN, n), lambda z, *_: (0, z))],
        [shape_of(*shape, dtype=BF)],
        [pl.BlockSpec((1,) + shape[1:], lambda z, *_: (z,) + tail)],
        [],
        2 * LEN * WIDTH * 4 * n,
        2 * (LEN * WIDTH + WIDTH * 4 * n + LEN * 4 * n),
    )
    return out.reshape(8, n, 1024) if by_rows else out.reshape(8, 1024, n)


def place_pair_body(spot, own, other, query, key, value, proj):
    for side, part in ((spot[1], own), (1 - spot[1], other)):
        at = pl.ds(pl.multiple_of(side * 128, 128), 128)
        for i, out in enumerate((query, key, value)):
            out[:, at] = part[:, i * 128 : i * 128 + 128].astype(F32)
        proj[at, :] = part[:, 384:].astype(F32).T


def place_pair(own, other, spot):
    grid = [shape_of(512, 256)] * 3 + [shape_of(256, 512)]
    return call(
        place_pair_body, (1,), spot, (own, other), [fixed((512, 512))] * 2, grid, [fixed(g.shape) for g in grid], [],
        2 * 512 * 512, 8 * 512 * 512,
    )


def turn_body(spot, piece, out):
    out[...] = piece[...].T


def turn(piece, spot):
    rows, width = piece.shape
    (out,) = call(
        turn_body, (1,), spot, (piece,), [fixed(piece.shape)], [shape_of(width, rows, dtype=BF)], [fixed((width, rows))], [],
        rows * width, 4 * rows * width,
    )
    return out


def grad_pair_body(spot, *refs):
    out = refs[18]
    for slot, mask in enumerate(SLOTS):
        start = pl.multiple_of((spot[0] ^ mask) * 128, 128)
        at = 0
        for pieces, local in ((refs[:8], refs[8]), (refs[9:17], refs[17])):
            total = dot(pieces[2 * slot][...], local[:HALF, :], TN) + dot(pieces[2 * slot + 1][...], local[HALF:, :], TN)
            n = local.shape[1]
            for block in range(4):
                y, c = divmod(block, 2)
                out[0, c, y ^ spot[1], pl.ds(start, 128), at : at + n] = total[block * 128 : block * 128 + 128, :].astype(BF)
            at += n


def grad_pair(first, first_local, second, second_local, spot):
    sizes = [local.shape[1] // 4 for local in (first_local, second_local)]
    n = sum(sizes)
    specs = [fixed(p.shape) for p in first]
    (out,) = call(
        grad_pair_body,
        (4,),
        spot,
        (*first, first_local, *second, second_local),
        specs + [pl.BlockSpec((LEN, sizes[0]), lambda z, *_: (0, z))] + specs + [pl.BlockSpec((LEN, sizes[1]), lambda z, *_: (0, z))],
        [shape_of(4, 2, 2, 512, n, dtype=BF)],
        [pl.BlockSpec((1, 2, 2, 512, n), lambda z, *_: (z, 0, 0, 0, 0))],
        [],
        2 * LEN * WIDTH * 4 * n,
        2 * (2 * LEN * WIDTH + WIDTH * 4 * n + LEN * 4 * n),
    )
    return out.reshape(8, 1024, n)


SCALE = HD ** (-0.5)
LOG2E = 1.4426950408889634
QUERY_BLOCK = 512


def forward_body(spot, queries, whole, ids_row, ids_column, out, logsum):
    scores = dot(whole[:, HD : 2 * HD], queries[:, :HD], NT)
    scores = jnp.where(ids_column[...] == ids_row[...], scores, NEGATIVE)
    peak = jnp.max(scores, axis=0, keepdims=True)
    expo = jnp.exp2((scores - peak) * (SCALE * LOG2E))
    total = jnp.sum(expo, axis=0, keepdims=True)
    probs = (expo * (1.0 / total)).astype(BF)
    mixed = dot(whole[:, 2 * HD :], probs, TN)
    out[...] = mixed.T.astype(BF)
    logsum[0] = peak * (SCALE * LOG2E) + jnp.log2(total)


def head_specs():
    return [
        pl.BlockSpec((QUERY_BLOCK, 3 * HD), lambda h, q, p: (q, h)),
        pl.BlockSpec((LEN, 3 * HD), lambda h, q, p: (0, h)),
        pl.BlockSpec((1, QUERY_BLOCK), lambda h, q, p: (0, q)),
        pl.BlockSpec((LEN, 1), lambda h, q, p: (0, 0)),
    ]


def attention(qkv, ids_row, ids_column, spot):
    return call(
        forward_body,
        (4, LEN // QUERY_BLOCK),
        spot,
        (qkv, qkv, ids_row, ids_column),
        head_specs(),
        [shape_of(LEN, QUARTER, dtype=BF), shape_of(4, 1, LEN)],
        [
            pl.BlockSpec((QUERY_BLOCK, HD), lambda h, q, p: (q, h)),
            pl.BlockSpec((1, 1, QUERY_BLOCK), lambda h, q, p: (h, 0, q)),
        ],
        [],
        64 * LEN * LEN * HD,
        LEN * 4 * HD * 8,
    )


def backward_body(spot, queries, whole, ids_row, ids_column, logsum, grad_out, out, sums, grad_keys, grad_values):
    q = pl.program_id(1)
    block = queries.shape[0]
    keys = whole[:, HD : 2 * HD]
    values = whole[:, 2 * HD :]
    scores = dot(keys, queries[:, :HD], NT) * (SCALE * LOG2E)
    scores = jnp.where(ids_column[...] == ids_row[...], scores, NEGATIVE)
    probs = jnp.exp2(scores - logsum[0])
    grad_probs = dot(values, grad_out[...], NT)
    inner = jnp.sum(probs * grad_probs, axis=0, keepdims=True)
    grad_scores = (probs * (grad_probs - inner)).astype(BF)
    back_query = dot(keys, grad_scores, TN)
    back_query = (back_query.T * SCALE).astype(BF)
    out[pl.ds(q * block, block), :HD] = back_query
    add_columns(sums.at[:, :HD], q, [back_query.astype(F32)])
    back_key = dot(grad_scores, queries[:, :HD], NN)
    back_value = dot(probs.astype(BF), grad_out[...], NN)

    @pl.when(q == 0)
    def _():
        grad_keys[...] = back_key
        grad_values[...] = back_value

    @pl.when(q > 0)
    def _():
        grad_keys[...] += back_key
        grad_values[...] += back_value

    @pl.when(q == pl.num_programs(1) - 1)
    def _():
        out[:, HD : 2 * HD] = (grad_keys[...] * SCALE).astype(BF)
        rounded = grad_values[...].astype(BF)
        out[:, 2 * HD :] = rounded
        sums[:, HD : 2 * HD] = jnp.zeros((8, HD), F32)
        sums[:, 2 * HD :] = column_sums([rounded.astype(F32)])


def attention_back(qkv, ids_row, ids_column, logsum, grad_heads, spot):
    return call(
        backward_body,
        (4, LEN // QUERY_BLOCK),
        spot,
        (qkv, qkv, ids_row, ids_column, logsum, grad_heads),
        head_specs()
        + [
            pl.BlockSpec((1, 1, QUERY_BLOCK), lambda h, q, p: (h, 0, q)),
            pl.BlockSpec((QUERY_BLOCK, HD), lambda h, q, p: (q, h)),
        ],
        [shape_of(LEN, 12 * HD, dtype=BF), shape_of(8, 12 * HD)],
        [pl.BlockSpec((LEN, 3 * HD), lambda h, q, p: (0, h)), pl.BlockSpec((8, 3 * HD), lambda h, q, p: (0, h))],
        [pltpu.VMEM((LEN, HD), F32), pltpu.VMEM((LEN, HD), F32)],
        120 * LEN * LEN * HD,
        LEN * 4 * HD * 16,
    )


def row_sum(value):
    folded = value[:, :128] + value[:, 128:256] + value[:, 256:384] + value[:, 384:512]
    return jnp.sum(folded.T, axis=0, keepdims=True)


def rows_of(values):
    rows = [row_sum(v) for v in values]
    return jnp.concatenate(rows + [jnp.zeros_like(rows[0])] * (8 - len(rows)), axis=0)


def columns_of(rows):
    return rows.T


def column_sums(values):
    sums = [jnp.sum(v, axis=0, keepdims=True) for v in values]
    return jnp.concatenate(sums + [jnp.zeros_like(sums[0])] * (8 - len(sums)), axis=0)


def add_columns(ref, t, values):
    sums = column_sums(values)

    @pl.when(t == 0)
    def _():
        ref[...] = sums

    @pl.when(t > 0)
    def _():
        ref[...] += sums


def moments_of(stats):
    total = (stats[0][...] + stats[1][...] + stats[2][...] + stats[3][...]) / WIDTH
    mean = total[0:1]
    return mean, lax.rsqrt(total[1:2] - mean * mean + EPS), total


def summed(refs, t):
    own, near, last = (pick(refs[2 * i], refs[2 * i + 1], t < STEPS // 2).astype(F32) for i in range(3))
    return own + near + last


STEP = 256
STEPS = LEN // STEP
LOW = pl.BlockSpec((STEP, QUARTER), lambda t, p: (jnp.minimum(t, STEPS // 2 - 1), 0))
HIGH = pl.BlockSpec((STEP, QUARTER), lambda t, p: (jnp.maximum(t - STEPS // 2, 0), 0))
PARTS = [LOW, HIGH] * 3
TILE = pl.BlockSpec((STEP, QUARTER), lambda t, p: (t, 0))
STATS = pl.BlockSpec((8, STEP), lambda t, p: (0, t))
VECTOR = fixed((1, QUARTER))
SUMS = fixed((8, QUARTER))
BLOCKS = pl.BlockSpec((4, STEP, 128), lambda t, p: (0, t, 0))


def elementwise(body, spot, ins, in_specs, outs, out_specs):
    return call(body, (STEPS,), spot, ins, in_specs, outs, out_specs, [], 20 * LEN * QUARTER, 16 * LEN * QUARTER)


def write_blocks(out, value):
    for z in range(4):
        out[z] = value[:, z * 128 : z * 128 + 128].astype(BF)


def whole_of(blocks):
    return jnp.concatenate([blocks[z] for z in range(4)], axis=1).astype(F32)


def norm_one_sums(spot, *refs):
    parts, (low, high, bias, resid, stats) = refs[:6], refs[6:]
    t = pl.program_id(0)
    attn = summed(parts, t) + bias[...]
    stream = pick(low, high, t < STEPS // 2).astype(F32)
    total = stream + attn
    resid[...] = total
    stats[...] = rows_of([total, total * total, attn * attn, stream * stream])


def write_halves(t, low, high, value):
    @pl.when(t < STEPS // 2)
    def _():
        low[...] = value

    @pl.when(t >= STEPS // 2)
    def _():
        high[...] = value


def norm_one(spot, resid, s0, s1, s2, s3, gain, shift, low, high, moments):
    mean, rstd, _ = moments_of((s0, s1, s2, s3))
    rows = jnp.concatenate([mean, rstd] + [mean] * 6, axis=0)
    moments[...] = rows
    columns = columns_of(rows)
    hidden = (resid[...] - columns[:, 0:1]) * columns[:, 1:2] * gain[...] + shift[...]
    write_halves(pl.program_id(0), low, high, hidden.astype(BF))


def norm_two_sums(spot, *refs):
    parts = refs[:6]
    bias, resid, moments, gain, shift, dy, gain_two, resid_two, stats = refs[6:]
    t = pl.program_id(0)
    ffn = summed(parts, t) + bias[...]
    columns = columns_of(moments[...])
    hidden = (resid[...] - columns[:, 0:1]) * columns[:, 1:2] * gain[...] + shift[...]
    total = hidden + ffn
    resid_two[...] = total
    scaled = whole_of(dy) * gain_two[...]
    stats[...] = rows_of([total, total * total, scaled, scaled * total, ffn * ffn])


def norm_two(spot, resid_two, s0, s1, s2, s3, dy, gain, shift, layer_out, grad_two, low, high, sums):
    mean, rstd, total = moments_of((s0, s1, s2, s3))
    mean_e = total[2:3]
    along = rstd * (total[3:4] - mean * mean_e)
    columns = columns_of(jnp.concatenate([mean, rstd, mean_e, along] + [mean] * 4, axis=0))
    normed = (resid_two[...] - columns[:, 0:1]) * columns[:, 1:2]
    t = pl.program_id(0)
    upstream = whole_of(dy)
    write_blocks(layer_out, normed * gain[...] + shift[...])
    back = columns[:, 1:2] * (upstream * gain[...] - columns[:, 2:3] - normed * columns[:, 3:4])
    grad_two[...] = back
    rounded = back.astype(BF)
    write_halves(t, low, high, rounded)
    add_columns(sums, t, [upstream * normed, upstream, rounded.astype(F32)])


def back_one_sums(spot, *refs):
    parts = refs[:6]
    grad_two, resid, moments, gain, grad_hidden, stats, sums = refs[6:]
    t = pl.program_id(0)
    upstream = summed(parts, t) + grad_two[...]
    grad_hidden[...] = upstream
    columns = columns_of(moments[...])
    normed = (resid[...] - columns[:, 0:1]) * columns[:, 1:2]
    scaled = upstream * gain[...]
    stats[...] = rows_of([scaled, scaled * normed])
    add_columns(sums, t, [upstream * normed, upstream])


def back_one(spot, grad_hidden, s0, s1, s2, s3, resid, moments, gain, grad_one, low, high, sums):
    total = (s0[...] + s1[...] + s2[...] + s3[...]) / WIDTH
    means = columns_of(total)
    columns = columns_of(moments[...])
    normed = (resid[...] - columns[:, 0:1]) * columns[:, 1:2]
    back = columns[:, 1:2] * (grad_hidden[...] * gain[...] - means[:, 0:1] - normed * means[:, 1:2])
    grad_one[...] = back
    rounded = back.astype(BF)
    t = pl.program_id(0)
    write_halves(t, low, high, rounded)
    add_columns(sums, t, [rounded.astype(F32)])


def finish_back(spot, *refs):
    parts, (grad_one, out) = refs[:6], refs[6:]
    write_blocks(out, summed(parts, pl.program_id(0)) + grad_one[...])


def pass_on(spot, first, second, third, fourth, low, high):
    low[...] = (first[...] + second[...].astype(F32)).astype(BF)
    high[...] = (third[...] + fourth[...].astype(F32)).astype(BF)


def split_y(piece, yi):
    return lax.dynamic_slice_in_dim(piece, yi * 128, 128, 1), lax.dynamic_slice_in_dim(piece, (1 - yi) * 128, 128, 1)


def spread_z(own, other, yi, zi, *after):
    both = jnp.concatenate([own.reshape(2, LEN, 128), other.reshape(2, LEN, 128)], axis=0)
    blocks = []
    for mask, bits in ((0, 0), (1, Z_LOW), (2, Z_HIGH), (3, Z_LOW | Z_HIGH)):
        block = lax.dynamic_index_in_dim(both, (zi ^ mask) ^ (yi * 2), 0, False)
        blocks.append(swap(tie(block, *after), bits) if mask else block)
    return blocks


def assemble_body(spot, *refs):
    blocks, (low, high) = refs[:4], refs[4:]
    t = pl.program_id(0)
    for out, when in ((low, t < STEPS // 2), (high, t >= STEPS // 2)):

        @pl.when(when)
        def _():
            for mask, block in enumerate(blocks):
                out[:, pl.ds(pl.multiple_of((spot[3] ^ mask) * 128, 128), 128)] = block[...]


def assemble(blocks, spot):
    half = shape_of(HALF, QUARTER, dtype=BF)
    return elementwise(
        assemble_body, spot, blocks, [pl.BlockSpec((STEP, 128), lambda t, p: (t, 0))] * 4, [half, half], [LOW, HIGH]
    )


def from_share(share):
    return lax.all_to_all(share, "z", 0, 0, tiled=True).reshape(2, 2 * LEN, 128)


def swap_y(parts, yi):
    own = lax.dynamic_index_in_dim(parts, yi, 0, False)
    return own, swap(lax.dynamic_index_in_dim(parts, 1 - yi, 0, False), Y_BIT)


def side_by_side(own, other, yi, axis):
    return jnp.where(yi == 0, jnp.concatenate([own, other], axis), jnp.concatenate([other, own], axis))


def square_gather(low, high):
    x_low = swap(low, X_BIT)
    y_high = swap(high, Y_BIT)
    x_high = swap(high, X_BIT)
    y_low = swap(low, Y_BIT)
    xy_low = swap(x_low, Y_BIT)
    xy_high = swap(y_high, X_BIT)
    return (low, high, x_low, x_high, y_low, y_high, xy_low, xy_high)


def square_scatter(local, weights, spot, by_rows, lane=0, first=lambda: None, middle=lambda: None, between=lambda: None, after=lambda: None):
    term = functools.partial(partial, local, weights, spot, by_rows, lane)
    far_low, far_high = term(3, BF, BF)
    far_low = swap(far_low, X_BIT)
    far_high = swap(far_high, Y_BIT)
    near_low, x_high = term(2, BF, F32)
    near_low = swap(near_low, X_BIT)
    first()
    y_low, near_high = term(1, F32, BF)
    near_high = swap(near_high, Y_BIT)
    middle()
    half = fixed((HALF, QUARTER))
    last_low, last_high = call(
        pass_on, (1,), spot, (y_low, far_low, x_high, far_high), [half] * 4, [shape_of(HALF, QUARTER, dtype=BF)] * 2,
        [half] * 2, [], LEN * QUARTER, 8 * LEN * QUARTER,
    )
    last_low = swap(last_low, Y_BIT)
    last_high = swap(last_high, X_BIT)
    between()
    spot.after(near_low, near_high)
    own_low, own_high = term(0, F32, F32)
    after()
    return (own_low, own_high, near_low, near_high, last_low, last_high)


def square_stats(stats):
    return (stats, swap(stats, X_BIT), swap(stats, Y_BIT), swap(stats, XY_BIT))


def halve_columns(pieces, yi, *after):
    n = pieces[0].shape[1] // 2
    own = jnp.concatenate([lax.dynamic_slice_in_dim(p, yi * n, n, 1) for p in pieces], axis=1)
    send = tie(jnp.concatenate([lax.dynamic_slice_in_dim(p, (1 - yi) * n, n, 1) for p in pieces], axis=1), *after)
    return jnp.concatenate([own, swap(send, Y_BIT)], axis=0), send


def halve_rows(piece, yi, *after):
    n = piece.shape[0] // 2
    own = lax.dynamic_slice_in_dim(piece, yi * n, n, 0)
    send = tie(lax.dynamic_slice_in_dim(piece, (1 - yi) * n, n, 0), *after)
    return jnp.concatenate([own, swap(send, Y_BIT)], axis=1), send


def gather_zc(piece):
    return lax.all_gather(piece, ("z", "c"), axis=0)


def scatter_zc(full):
    return lax.psum_scatter(full, ("z", "c"), scatter_dimension=0)


def exchange_columns(piece):
    return piece[:512], swap(piece[512:], Y_BIT)


def exchange_rows(piece):
    return piece[:, :512], swap(piece[:, 512:], Y_BIT)


def restore_columns(pair, yi, begin=0, n=None):
    own, other = pair
    n = n or own.shape[1]
    own, other = own[:, begin : begin + n], other[:, begin : begin + n]
    return side_by_side(own.astype(F32), other.astype(F32), yi, 1)


def restore_rows(pair, yi):
    return side_by_side(pair[0].astype(F32), pair[1].astype(F32), yi, 0)


def square_device(
    tokens, lengths, w_query, b_query, w_key, w_value, b_value, w_proj, b_proj, norm_gain, norm_shift,
    w_up, b_up, w_down, b_down, final_gain, final_shift, cotangent,
):
    yi = lax.axis_index("y")
    zi = lax.axis_index("z")
    spot = Order(jnp.stack([lax.axis_index("x") * 2 + yi, yi, lax.axis_index("c"), zi]).astype(jnp.int32))

    token_own, token_send = split_y(tokens, yi)
    token_other = swap(token_send, Y_BIT)
    half_qkv, sent = halve_columns([w_query, w_key, w_value, turn(w_proj, spot)], yi, token_send)
    vectors = jnp.concatenate(
        [v.reshape(2, -1) for v in (b_query, b_value, b_proj, norm_gain, norm_shift, b_down, final_gain, final_shift, b_up)],
        axis=1,
    )
    vectors = lax.dynamic_slice_in_dim(vectors, yi, 1, 0)
    vectors = lax.all_to_all(jnp.broadcast_to(vectors, (4, vectors.shape[1])), "z", 0, 0, tiled=True)
    small = [vectors[:, i * 128 : (i + 1) * 128] for i in range(8)]
    q_bias, v_bias = small[:2]
    p_bias, n_gain, n_shift, d_bias, f_gain, f_shift = (v.reshape(1, QUARTER) for v in small[2:])
    u_bias = vectors[:, 1024:].reshape(1, -1)
    qkv_bias = jnp.stack([q_bias, jnp.zeros_like(q_bias), v_bias], axis=1).reshape(1, -1)

    both = side_by_side(lengths, swap(lengths, Y_BIT), yi, 0)
    ids = segment_ids(lax.dynamic_slice_in_dim(both, zi, 1, 0))[0]
    valid = (ids != lengths.shape[1] - 1).astype(F32)
    ids_row, ids_column = ids[None], ids[:, None]

    full_qkv = gather_zc(tie(half_qkv, vectors))
    token_blocks = spread_z(token_own, token_other, yi, zi)
    half_up, sent = halve_columns([w_up], yi, sent)
    spot.after(vectors, half_up)
    token_low, token_high = assemble(token_blocks, spot)
    gathered = square_gather(token_low, token_high)
    full_up = gather_zc(tie(half_up, token_low))
    (qkv,) = wide(gathered, full_qkv, spot, False, finish_bias, (qkv_bias,), 1, n=384)
    half_down, sent = halve_rows(tie(w_down, qkv), yi)
    heads_out, logsum = attention(qkv, ids_row, ids_column, spot)
    spot.after(half_down)
    full_down = gather_zc(half_down)
    full = shape_of(LEN, QUARTER)
    low_half = shape_of(HALF, QUARTER, dtype=BF)
    stats_shape = shape_of(8, LEN)
    sums_shape = shape_of(8, QUARTER)

    parts = square_scatter(heads_out, full_qkv, spot, False, 3)
    resid, stats_one = elementwise(
        norm_one_sums, spot, (*parts, token_low, token_high, p_bias), PARTS + [LOW, HIGH, VECTOR], [full, stats_shape], [TILE, STATS]
    )
    hidden_low, hidden_high, moments = elementwise(
        norm_one, spot, (resid, *square_stats(stats_one), n_gain, n_shift), [TILE] + [STATS] * 4 + [VECTOR] * 2,
        [low_half, low_half, stats_shape], [LOW, HIGH, STATS],
    )
    hidden_wide = square_gather(hidden_low, hidden_high)
    dy_own, dy_send = split_y(tie(cotangent, hidden_low), yi)
    dy_other = swap(dy_send, Y_BIT)
    act, slope = wide(hidden_wide, full_up, spot, False, finish_gelu, (u_bias,), 2)
    dy = side_by_side(dy_own.reshape(2, LEN, 128), dy_other.reshape(2, LEN, 128), yi, 0)
    dy = lax.all_to_all(tie(dy, act), "z", 0, 0, tiled=True)
    parts = square_scatter(act, full_down, spot, True)
    resid_two, stats_two = elementwise(
        norm_two_sums, spot, (*parts, d_bias, resid, moments, n_gain, n_shift, dy, f_gain),
        PARTS + [VECTOR, TILE, STATS, VECTOR, VECTOR, BLOCKS, VECTOR], [full, stats_shape], [TILE, STATS],
    )
    layer_share, grad_two, ffn_low, ffn_high, sums_two = elementwise(
        norm_two, spot, (resid_two, *square_stats(stats_two), dy, f_gain, f_shift),
        [TILE] + [STATS] * 4 + [BLOCKS, VECTOR, VECTOR],
        [shape_of(4, LEN, 128, dtype=BF), full, low_half, low_half, sums_shape], [BLOCKS, TILE, LOW, HIGH, SUMS],
    )
    ffn_wide = square_gather(ffn_low, ffn_high)
    down = grad_whole(ffn_wide, act, spot, True)
    grad_down = scatter_zc(down)
    layer_parts = from_share(tie(layer_share, down))
    grad_pre, sums_up = wide(ffn_wide, full_down, spot, True, finish_slope, (slope,), 1, 1)
    up = []

    def after():
        spot.after(layer_parts)
        up.append(grad_whole(hidden_wide, grad_pre, spot, False))

    parts = square_scatter(grad_pre, full_up, spot, False, after=after)
    grad_hidden, stats_back, sums_back = elementwise(
        back_one_sums, spot, (*parts, grad_two, resid, moments, n_gain),
        PARTS + [TILE, TILE, STATS, VECTOR], [full, stats_shape, sums_shape], [TILE, STATS, SUMS],
    )
    grad_one, attn_low, attn_high, sums_attn = elementwise(
        back_one, spot, (grad_hidden, *square_stats(stats_back), resid, moments, n_gain),
        [TILE] + [STATS] * 4 + [TILE, STATS, VECTOR],
        [full, low_half, low_half, sums_shape], [TILE, LOW, HIGH, SUMS],
    )
    attn_wide = square_gather(attn_low, attn_high)
    grad_up = scatter_zc(tie(up[0], spot.value))
    spot.after(grad_down)
    (grad_heads,) = wide(attn_wide, full_qkv, spot, False, finish_plain, (), 1, n=128, lane=3)
    layer_own, layer_other = swap_y(tie(layer_parts, grad_heads), yi)
    down = exchange_rows(tie(grad_down, grad_heads))
    grad_qkv, sums_qkv = attention_back(qkv, ids_row, ids_column, logsum, grad_heads, spot)
    spot.after(layer_other, down[1])
    sum_last = scatter_zc(grad_pair(gathered, grad_qkv, attn_wide, heads_out, spot))

    kept = []

    def between():
        totals = jnp.stack([tie(stats_one[3], spot.value) * valid, stats_one[2] * valid, stats_two[4] * valid, valid * QUARTER])
        totals = jnp.pad(jnp.sum(totals, axis=1)[None], ((0, 3), (0, 124)))
        vector_sums = jnp.concatenate(
            [
                v.reshape(4, -1)
                for v in (
                    *(tie(sums_qkv[0], spot.value).reshape(4, 3, HD)[:, i] for i in (0, 2)),
                    sums_attn[0], sums_back[0], sums_back[1], sums_two[2], sums_two[0], sums_two[1], sums_up[0], totals,
                )
            ],
            axis=1,
        )
        kept.append((vector_sums, swap(vector_sums, C_BIT)))

    parts = square_scatter(grad_qkv, full_qkv, spot, False, between=between)
    (back,) = elementwise(
        finish_back, spot, (*parts, grad_one), PARTS + [TILE], [shape_of(4, LEN, 128, dtype=BF)], [BLOCKS]
    )
    back_parts = from_share(back)
    up = exchange_columns(tie(grad_up, back))
    sums = kept[0][0] + tie(kept[0][1], back)
    sums = sums + tie(swap(sums, Z_LOW), up[1])
    back_own, back_other = swap_y(back_parts, yi)
    sums = sums + tie(swap(sums, Z_HIGH), back_other)
    last = swap(sum_last[512:], Y_BIT)
    totals = sums[0, 1536:] + swap(sums[0, 1536:], Y_BIT)
    totals = totals + swap(totals, X_BIT)
    norms = jnp.sqrt(totals[:3] / totals[3])
    sums = lax.dynamic_index_in_dim(sums, zi, 0, False)
    other = swap(sums, Y_BIT)
    sums = jnp.where(yi == 0, jnp.stack([sums, other]), jnp.stack([other, sums]))
    vecs = [sums[:, i * 128 : (i + 1) * 128].reshape(-1) for i in range(8)] + [sums[:, 1024:1536].reshape(-1)]
    layer_out = side_by_side(tie(layer_own, back), layer_other, yi, 1)
    grad_tokens = side_by_side(back_own, back_other, yi, 1).astype(F32)
    grad_down = restore_rows((tie(down[0], back), down[1]), yi)
    grad_up = restore_columns(up, yi)
    grad_query, grad_key, grad_value, grad_proj = place_pair(sum_last, last, spot)
    return (
        layer_out, grad_tokens, grad_query, vecs[0], grad_key, grad_value, vecs[1], grad_proj, vecs[2], vecs[3], vecs[4],
        grad_up, vecs[8], grad_down, vecs[5], vecs[6], vecs[7], norms,
    )


def gather_features(piece):
    return lax.all_gather(piece, "col", axis=1, tiled=True)


def scatter_features(partial_sum):
    low = partial_sum.astype(jnp.bfloat16)
    return lax.psum_scatter(low, "col", scatter_dimension=1, tiled=True).astype(F32)


def row_totals(first, second):
    return lax.psum((first, second), "col")


def gather_weights(w_query, w_key, w_value, w_up, w_proj, w_down):
    inner = (
        lax.all_gather(w_query, "row", axis=0, tiled=True),
        lax.all_gather(w_key, "row", axis=0, tiled=True),
        lax.all_gather(w_value, "row", axis=0, tiled=True),
        lax.all_gather(w_up, "row", axis=0, tiled=True),
    )
    outer = (
        lax.all_gather(w_proj, "row", axis=1, tiled=True),
        lax.all_gather(w_down, "row", axis=1, tiled=True),
    )
    return (inner, outer)


def norm_shares(resid, gain, shift):
    width = resid.shape[1] * lax.axis_size("col")
    total, squares = row_totals(jnp.sum(resid, axis=1), jnp.sum(resid * resid, axis=1))
    mean = total / width
    rstd = lax.rsqrt(squares / width - mean * mean + EPS)
    normed = (resid - mean[:, None]) * rstd[:, None]
    return (normed * gain + shift, normed, rstd)


def norm_back(upstream, normed, rstd, gain):
    width = upstream.shape[1] * lax.axis_size("col")
    scaled = upstream * gain
    total, along = row_totals(jnp.sum(scaled, axis=1), jnp.sum(scaled * normed, axis=1))
    back = rstd[:, None] * (scaled - total[:, None] / width - normed * (along[:, None] / width))
    return (back, jnp.sum(upstream * normed, axis=0), jnp.sum(upstream, axis=0))


def attend_forward(pack):
    queries, keys, values, ids = pack
    scale = queries.shape[2] ** (-0.5)
    block = min(512, queries.shape[0])
    same = ids[:, None] == ids[None, :]
    outputs = []
    logsums = []
    for begin in range(0, queries.shape[0], block):
        scores = (
            jnp.einsum(
                "qhd,khd->hqk",
                queries[begin : begin + block],
                keys,
                preferred_element_type=jnp.float32,
            )
            * scale
        )
        scores = jnp.where(same[None, begin : begin + block], scores, NEGATIVE)
        peak = jnp.max(scores, axis=2, keepdims=True)
        expo = jnp.exp(scores - peak)
        total = jnp.sum(expo, axis=2, keepdims=True)
        probs = (expo / total).astype(jnp.bfloat16)
        outputs.append(
            jnp.einsum("hqk,khd->qhd", probs, values, preferred_element_type=jnp.float32)
        )
        logsums.append((peak + jnp.log(total))[:, :, 0])
    return (jnp.concatenate(outputs, axis=0), jnp.concatenate(logsums, axis=1))


def attend_back(pack):
    queries, keys, values, ids, logsum, grad_out = pack
    scale = queries.shape[2] ** (-0.5)
    block = min(512, queries.shape[0])
    same = ids[:, None] == ids[None, :]
    grad_keys = jnp.zeros(keys.shape, jnp.float32)
    grad_values = jnp.zeros(values.shape, jnp.float32)
    grad_queries = []
    for begin in range(0, queries.shape[0], block):
        query_rows = queries[begin : begin + block]
        grad_rows = grad_out[begin : begin + block]
        scores = (
            jnp.einsum("qhd,khd->hqk", query_rows, keys, preferred_element_type=jnp.float32) * scale
        )
        scores = jnp.where(same[None, begin : begin + block], scores, NEGATIVE)
        probs = jnp.exp(scores - logsum[:, begin : begin + block, None])
        grad_probs = jnp.einsum(
            "qhd,khd->hqk", grad_rows, values, preferred_element_type=jnp.float32
        )
        inner = jnp.sum(probs * grad_probs, axis=2, keepdims=True)
        grad_scores = (probs * (grad_probs - inner)).astype(jnp.bfloat16)
        grad_queries.append(
            jnp.einsum("hqk,khd->qhd", grad_scores, keys, preferred_element_type=jnp.float32)
            * scale
        )
        grad_keys = (
            grad_keys
            + jnp.einsum(
                "hqk,qhd->khd", grad_scores, query_rows, preferred_element_type=jnp.float32
            )
            * scale
        )
        grad_values = grad_values + jnp.einsum(
            "hqk,qhd->khd",
            probs.astype(jnp.bfloat16),
            grad_rows,
            preferred_element_type=jnp.float32,
        )
    return (jnp.concatenate(grad_queries, axis=0), grad_keys, grad_values)


def per_device(
    tokens,
    lengths,
    w_query,
    b_query,
    w_key,
    w_value,
    b_value,
    w_proj,
    b_proj,
    norm_gain,
    norm_shift,
    w_up,
    b_up,
    w_down,
    b_down,
    final_gain,
    final_shift,
    cotangent,
):
    rows, share = tokens.shape
    heads = w_query.shape[1] // HD
    ids = segment_ids(lengths)
    seq_count = ids.shape[0]
    valid = (ids.reshape(rows) != lengths.shape[1] - 1).astype(jnp.float32)[:, None]
    inner, outer = gather_weights(w_query, w_key, w_value, w_up, w_proj, w_down)
    full_query, full_key, full_value, full_up = inner
    full_proj, full_down = outer
    stream = tokens.astype(jnp.float32)
    gathered = gather_features(tokens)
    queries = (jnp.dot(gathered, full_query, preferred_element_type=jnp.float32) + b_query).astype(
        jnp.bfloat16
    )
    keys = jnp.dot(gathered, full_key, preferred_element_type=jnp.float32).astype(jnp.bfloat16)
    values = (jnp.dot(gathered, full_value, preferred_element_type=jnp.float32) + b_value).astype(
        jnp.bfloat16
    )
    shape = (seq_count, LEN, heads, HD)
    query_seq = queries.reshape(shape)
    key_seq = keys.reshape(shape)
    value_seq = values.reshape(shape)
    mixed, logsum = lax.map(attend_forward, (query_seq, key_seq, value_seq, ids))
    heads_out = mixed.reshape(rows, heads * HD).astype(jnp.bfloat16)
    attn = (
        scatter_features(jnp.dot(heads_out, full_proj, preferred_element_type=jnp.float32)) + b_proj
    )
    hidden, normed_one, rstd_one = norm_shares(stream + attn, norm_gain, norm_shift)
    hidden_low = gather_features(hidden.astype(jnp.bfloat16))
    pre = jnp.dot(hidden_low, full_up, preferred_element_type=jnp.float32) + b_up
    act, gelu_back = jax.vjp(lambda inputs: jax.nn.gelu(inputs, approximate=True), pre)
    act_low = act.astype(jnp.bfloat16)
    ffn = scatter_features(jnp.dot(act_low, full_down, preferred_element_type=jnp.float32)) + b_down
    result, normed_two, rstd_two = norm_shares(hidden + ffn, final_gain, final_shift)
    totals = lax.psum(
        (
            jnp.sum(valid * stream * stream),
            jnp.sum(valid * attn * attn),
            jnp.sum(valid * ffn * ffn),
            jnp.sum(valid) * share,
        ),
        ("row", "col"),
    )
    norms = jnp.sqrt(jnp.stack([totals[0], totals[1], totals[2]]) / totals[3])
    back_inner, back_outer = gather_weights(w_query, w_key, w_value, w_up, w_proj, w_down)
    full_query, full_key, full_value, full_up = back_inner
    full_proj, full_down = back_outer
    grad_two, grad_fgain, grad_fshift = norm_back(
        cotangent.astype(jnp.float32), normed_two, rstd_two, final_gain
    )
    grad_ffn = grad_two.astype(jnp.bfloat16)
    grad_dbias = jnp.sum(grad_ffn.astype(jnp.float32), axis=0)
    ffn_wide = gather_features(grad_ffn)
    grad_down = jnp.einsum("tf,td->fd", act_low, ffn_wide, preferred_element_type=jnp.float32)
    grad_act = jnp.einsum("td,fd->tf", ffn_wide, full_down, preferred_element_type=jnp.float32)
    grad_pre = gelu_back(grad_act)[0].astype(jnp.bfloat16)
    grad_ubias = jnp.sum(grad_pre.astype(jnp.float32), axis=0)
    grad_up = jnp.einsum("td,tf->df", hidden_low, grad_pre, preferred_element_type=jnp.float32)
    grad_hidden = (
        scatter_features(
            jnp.einsum("tf,df->td", grad_pre, full_up, preferred_element_type=jnp.float32)
        )
        + grad_two
    )
    grad_one, grad_ngain, grad_nshift = norm_back(grad_hidden, normed_one, rstd_one, norm_gain)
    grad_attn = grad_one.astype(jnp.bfloat16)
    grad_pbias = jnp.sum(grad_attn.astype(jnp.float32), axis=0)
    attn_wide = gather_features(grad_attn)
    grad_proj = jnp.einsum("th,td->hd", heads_out, attn_wide, preferred_element_type=jnp.float32)
    grad_heads = jnp.einsum(
        "td,hd->th", attn_wide, full_proj, preferred_element_type=jnp.float32
    ).astype(jnp.bfloat16)
    back_query, back_key, back_value = lax.map(
        attend_back, (query_seq, key_seq, value_seq, ids, logsum, grad_heads.reshape(shape))
    )
    grad_queries = back_query.reshape(rows, heads * HD).astype(jnp.bfloat16)
    grad_keys = back_key.reshape(rows, heads * HD).astype(jnp.bfloat16)
    grad_values = back_value.reshape(rows, heads * HD).astype(jnp.bfloat16)
    grad_qbias = jnp.sum(grad_queries.astype(jnp.float32), axis=0)
    grad_vbias = jnp.sum(grad_values.astype(jnp.float32), axis=0)
    grad_query = jnp.einsum("td,th->dh", gathered, grad_queries, preferred_element_type=jnp.float32)
    grad_key = jnp.einsum("td,th->dh", gathered, grad_keys, preferred_element_type=jnp.float32)
    grad_value = jnp.einsum("td,th->dh", gathered, grad_values, preferred_element_type=jnp.float32)
    partial_back = (
        jnp.einsum("th,dh->td", grad_queries, full_query, preferred_element_type=jnp.float32)
        + jnp.einsum("th,dh->td", grad_keys, full_key, preferred_element_type=jnp.float32)
        + jnp.einsum("th,dh->td", grad_values, full_value, preferred_element_type=jnp.float32)
    )
    grad_tokens = scatter_features(partial_back) + grad_one
    grad_query, grad_key, grad_value, grad_up = (
        lax.psum_scatter(
            grad_query.astype(jnp.bfloat16), "row", scatter_dimension=0, tiled=True
        ).astype(jnp.float32),
        lax.psum_scatter(
            grad_key.astype(jnp.bfloat16), "row", scatter_dimension=0, tiled=True
        ).astype(jnp.float32),
        lax.psum_scatter(
            grad_value.astype(jnp.bfloat16), "row", scatter_dimension=0, tiled=True
        ).astype(jnp.float32),
        lax.psum_scatter(
            grad_up.astype(jnp.bfloat16), "row", scatter_dimension=0, tiled=True
        ).astype(jnp.float32),
    )
    grad_proj, grad_down = (
        lax.psum_scatter(
            grad_proj.astype(jnp.bfloat16), "row", scatter_dimension=1, tiled=True
        ).astype(jnp.float32),
        lax.psum_scatter(
            grad_down.astype(jnp.bfloat16), "row", scatter_dimension=1, tiled=True
        ).astype(jnp.float32),
    )
    vectors = lax.psum(
        (
            grad_qbias,
            grad_vbias,
            grad_pbias,
            grad_ngain,
            grad_nshift,
            grad_ubias,
            grad_dbias,
            grad_fgain,
            grad_fshift,
        ),
        "row",
    )
    return (
        result.astype(jnp.bfloat16),
        grad_tokens,
        grad_query,
        vectors[0],
        grad_key,
        grad_value,
        vectors[1],
        grad_proj,
        vectors[2],
        vectors[3],
        vectors[4],
        grad_up,
        vectors[5],
        grad_down,
        vectors[6],
        vectors[7],
        vectors[8],
        norms,
    )


def placements(row, col):
    grid, turned, share = P(row, col), P(col, row), P(col)
    args = (
        grid, P(row, None), grid, share, grid, grid, share, turned, share, share, share, grid, share, turned, share, share, share, grid,
    )
    outs = (
        grid, grid, grid, share, grid, grid, share, turned, share, share, share, grid, share, turned, share, share, share, P(),
    )
    return (args, outs)


def solution(mesh):
    if mesh.shape["row"] == 4 and mesh.shape["col"] == 8:
        mesh = Mesh(mesh.devices.reshape(2, 2, 4, 2), AXES)
        args, outs = placements(("y", "c"), ("z", "x"))
        body = square_device
    else:
        args, outs = placements("row", "col")
        body = per_device
    return jax.shard_map(body, mesh=mesh, in_specs=args, out_specs=outs, check_vma=False)
```

```python
import functools

import jax
import jax.numpy as jnp
from jax import lax
from jax.experimental import pallas as pl
from jax.experimental.pallas import tpu as pltpu
from jax.sharding import Mesh
from jax.sharding import PartitionSpec as P

HD = 128
LEN = 1024
EPS = 1e-06
NEGATIVE = -1000000000.0
BF = jnp.bfloat16
F32 = jnp.float32


def segment_ids(lengths):
    slots = lengths.shape[1]
    ends = jnp.cumsum(lengths, axis=1)
    places = jnp.arange(LEN, dtype=jnp.int32)
    hits = (places[None, :, None] >= ends[:, None, : slots - 1]).astype(jnp.int32)
    return jnp.sum(hits, axis=2)


AXES = ("y", "c", "z", "x")
X_BIT, Z_LOW, Z_HIGH, C_BIT, Y_BIT = 1, 2, 4, 8, 16
XY_BIT = X_BIT | Y_BIT
QUARTER = 512
HALF = LEN // 2
WIDTH = 2048
NN, NT, TN = ((1,), (0,)), ((1,), (1,)), ((0,), (0,))


def swap(piece, mask):
    return lax.ppermute(piece, AXES, [(i, i ^ mask) for i in range(32)])


def dot(left, right, dims):
    return lax.dot_general(left, right, (dims, ((), ())), preferred_element_type=F32)


def tie(value, *others):
    return lax.optimization_barrier((value, *others))[0]


class Order:
    def __init__(self, value):
        self.value = value

    def after(self, *others):
        self.value = tie(self.value, *others)


LESS = 4


def call(body, grid, spot, ins, in_specs, outs, out_specs, scratch, flops, size):
    result = pl.pallas_call(
        body,
        grid_spec=pltpu.PrefetchScalarGridSpec(
            num_scalar_prefetch=1, grid=grid, in_specs=in_specs, out_specs=out_specs, scratch_shapes=scratch
        ),
        out_shape=outs,
        compiler_params=pltpu.CompilerParams(
            dimension_semantics=("arbitrary",) * len(grid), vmem_limit_bytes=56 * 1024 * 1024
        ),
        cost_estimate=pl.CostEstimate(flops=flops // LESS, bytes_accessed=size // LESS, transcendentals=0),
    )(spot.value, *ins)
    spot.after(result[0])
    return result


def shape_of(*shape, dtype=F32):
    return jax.ShapeDtypeStruct(shape, dtype)


def fixed(shape):
    return pl.BlockSpec(shape, lambda *_: (0,) * len(shape))


def pick(low, high, first):
    return jnp.where(first, low[...], high[...])


SLOTS = (0, 2, 1, 3)


def wide_body(by_rows, finish, count, several, spot, *refs):
    pieces, weights, rest = refs[:8], refs[8], refs[9:]
    extra, outs, kept = rest[: -1 - count], rest[-1 - count : -1], rest[-1]
    t = pl.program_id(1)

    @pl.when(t == 0)
    def _():
        for slot, mask in enumerate(SLOTS):
            start = pl.multiple_of((spot[0] ^ mask) * 128, 128)
            for block in range(4):
                y, c = divmod(block, 2)
                y = y ^ spot[1]
                at = slot * QUARTER + block * 128
                for z in range(several):
                    if by_rows:
                        kept[:, at : at + 128] = weights[0, c, :, pl.ds(pl.multiple_of(y * 512 + start, 128), 128)]
                    else:
                        n = weights.shape[4]
                        kept[at : at + 128, z * n : z * n + n] = weights[z, c, y, pl.ds(start, 128), :]

    total = None
    for slot in range(4):
        tile = pick(pieces[2 * slot], pieces[2 * slot + 1], t == 0)
        part = slice(slot * QUARTER, slot * QUARTER + QUARTER)
        term = dot(tile, kept[:, part], NT) if by_rows else dot(tile, kept[part, :], NN)
        total = term if total is None else total + term
    finish(total, extra, outs)


def wide(pieces, weights, spot, by_rows, finish, extra, count, sums=0, n=None, lane=0):
    several = 1
    if by_rows:
        n = weights.shape[1]
        weights = weights.reshape(4, 2, n, 1024)
        kept = pltpu.VMEM((n, WIDTH), BF)
        block = (1, 2, n, 1024)
    else:
        n = n or weights.shape[2]
        weights = weights.reshape(4, 2, 2, 512, weights.shape[2])
        several = 4 if n < 256 else 1
        kept = pltpu.VMEM((WIDTH, several * n), BF)
        block = (several, 2, 2, 512, n)
    tail = (0,) * (len(block) - 2) + (lane,)
    total = 4 * n
    n = several * n
    bias = pl.BlockSpec((1, n), lambda z, t, *_: (0, z))
    tile = pl.BlockSpec((HALF, n), lambda z, t, *_: (t, z))
    return call(
        functools.partial(wide_body, by_rows, finish, count + sums, several),
        (4 // several, 2),
        spot,
        (*pieces, weights, *extra),
        [fixed(p.shape) for p in pieces]
        + [pl.BlockSpec(block, lambda z, t, *_: (z,) + tail)]
        + [bias if e.shape[0] == 1 else tile for e in extra],
        [shape_of(LEN, total, dtype=BF)] * count + [shape_of(8, total)] * sums,
        [tile] * count + [pl.BlockSpec((8, n), lambda z, t, *_: (0, z))] * sums,
        [kept],
        2 * LEN * WIDTH * total,
        2 * (LEN * WIDTH + WIDTH * total + LEN * total),
    )


def finish_bias(total, extra, outs):
    outs[0][...] = (total + extra[0][...]).astype(BF)


def finish_plain(total, extra, outs):
    outs[0][...] = total.astype(BF)


def finish_gelu(total, extra, outs):
    pre = total + extra[0][...]
    square = pre * pre
    bend = jnp.tanh(0.7978845608028654 * pre * (1.0 + 0.044715 * square))
    rise = 0.5 * (1.0 + bend)
    outs[0][...] = (pre * rise).astype(BF)
    slope = 0.7978845608028654 * (1.0 + 0.134145 * square)
    outs[1][...] = (rise + 0.5 * pre * (1.0 - bend * bend) * slope).astype(BF)


def finish_slope(total, extra, outs):
    rounded = (total * extra[0][...].astype(F32)).astype(BF)
    outs[0][...] = rounded
    add_columns(outs[1], pl.program_id(1), [rounded.astype(F32)])


def partial_body(by_rows, n, spot, local, *rest):
    weights, (low, high) = rest[:-2], rest[-2:]
    t = pl.program_id(0)
    total = None
    for z in range(4):
        tile = local[:, z * n : (z + 1) * n]
        if by_rows:
            kept = jnp.concatenate([weights[y][z, c] for y in range(2) for c in range(2)], axis=1)
            term = dot(tile, kept, NN)
        else:
            kept = jnp.concatenate([weights[0][z, c, y ^ spot[1]] for y in range(2) for c in range(2)], axis=0)
            term = dot(tile, kept, NT)
        total = term if total is None else total + term

    @pl.when(t == 0)
    def _():
        low[...] = total.astype(low.dtype)

    @pl.when(t == 1)
    def _():
        high[...] = total.astype(high.dtype)


def partial(local, weights, spot, by_rows, lane, mask, low, high):
    n = local.shape[1] // 4
    if by_rows:
        weights = weights.reshape(4, 2, n, 1024)
        specs = [
            pl.BlockSpec((4, 2, n, 128), functools.partial(lambda y, t, p: (0, 0, 0, (y ^ p[1]) * 4 + (p[0] ^ mask)), y))
            for y in range(2)
        ]
        ins = (weights, weights)
    else:
        weights = weights.reshape(4, 2, 2, 512, weights.shape[2])
        specs = [pl.BlockSpec((4, 2, 2, 128, n), lambda t, p: (0, 0, 0, p[0] ^ mask, lane))]
        ins = (weights,)
    return call(
        functools.partial(partial_body, by_rows, n),
        (2,),
        spot,
        (local, *ins),
        [pl.BlockSpec((HALF, 4 * n), lambda t, p: (t, 0))] + specs,
        [shape_of(HALF, QUARTER, dtype=low), shape_of(HALF, QUARTER, dtype=high)],
        [fixed((HALF, QUARTER))] * 2,
        [],
        2 * LEN * QUARTER * 4 * n,
        2 * (LEN * 4 * n + QUARTER * 4 * n + LEN * QUARTER),
    )


def grad_whole_body(by_rows, spot, *refs):
    pieces, local, out = refs[:8], refs[8], refs[9]
    for slot, mask in enumerate(SLOTS):
        start = pl.multiple_of((spot[0] ^ mask) * 128, 128)

        def term(piece, tile):
            return dot(tile, piece, TN) if by_rows else dot(piece, tile, TN)

        total = term(pieces[2 * slot][...], local[:HALF, :]) + term(pieces[2 * slot + 1][...], local[HALF:, :])
        for block in range(4):
            y, c = divmod(block, 2)
            y = y ^ spot[1]
            part = slice(block * 128, block * 128 + 128)
            if by_rows:
                out[0, c, :, pl.ds(pl.multiple_of(y * 512 + start, 128), 128)] = total[:, part].astype(BF)
            else:
                out[0, c, y, pl.ds(start, 128), :] = total[part, :].astype(BF)


def grad_whole(pieces, local, spot, by_rows):
    n = local.shape[1] // 4
    shape = (4, 2, n, 1024) if by_rows else (4, 2, 2, 512, n)
    tail = (0,) * (len(shape) - 1)
    (out,) = call(
        functools.partial(grad_whole_body, by_rows),
        (4,),
        spot,
        (*pieces, local),
        [fixed(p.shape) for p in pieces] + [pl.BlockSpec((LEN, n), lambda z, *_: (0, z))],
        [shape_of(*shape, dtype=BF)],
        [pl.BlockSpec((1,) + shape[1:], lambda z, *_: (z,) + tail)],
        [],
        2 * LEN * WIDTH * 4 * n,
        2 * (LEN * WIDTH + WIDTH * 4 * n + LEN * 4 * n),
    )
    return out.reshape(8, n, 1024) if by_rows else out.reshape(8, 1024, n)


def place_pair_body(spot, own, other, query, key, value, proj):
    for side, part in ((spot[1], own), (1 - spot[1], other)):
        at = pl.ds(pl.multiple_of(side * 128, 128), 128)
        for i, out in enumerate((query, key, value)):
            out[:, at] = part[:, i * 128 : i * 128 + 128].astype(F32)
        proj[at, :] = part[:, 384:].astype(F32).T


def place_pair(own, other, spot):
    grid = [shape_of(512, 256)] * 3 + [shape_of(256, 512)]
    return call(
        place_pair_body, (1,), spot, (own, other), [fixed((512, 512))] * 2, grid, [fixed(g.shape) for g in grid], [],
        2 * 512 * 512, 8 * 512 * 512,
    )


def turn_body(spot, piece, out):
    out[...] = piece[...].T


def turn(piece, spot):
    rows, width = piece.shape
    (out,) = call(
        turn_body, (1,), spot, (piece,), [fixed(piece.shape)], [shape_of(width, rows, dtype=BF)], [fixed((width, rows))], [],
        rows * width, 4 * rows * width,
    )
    return out


def grad_pair_body(spot, *refs):
    out = refs[18]
    for slot, mask in enumerate(SLOTS):
        start = pl.multiple_of((spot[0] ^ mask) * 128, 128)
        at = 0
        for pieces, local in ((refs[:8], refs[8]), (refs[9:17], refs[17])):
            total = dot(pieces[2 * slot][...], local[:HALF, :], TN) + dot(pieces[2 * slot + 1][...], local[HALF:, :], TN)
            n = local.shape[1]
            for block in range(4):
                y, c = divmod(block, 2)
                out[0, c, y ^ spot[1], pl.ds(start, 128), at : at + n] = total[block * 128 : block * 128 + 128, :].astype(BF)
            at += n


def grad_pair(first, first_local, second, second_local, spot):
    sizes = [local.shape[1] // 4 for local in (first_local, second_local)]
    n = sum(sizes)
    specs = [fixed(p.shape) for p in first]
    (out,) = call(
        grad_pair_body,
        (4,),
        spot,
        (*first, first_local, *second, second_local),
        specs + [pl.BlockSpec((LEN, sizes[0]), lambda z, *_: (0, z))] + specs + [pl.BlockSpec((LEN, sizes[1]), lambda z, *_: (0, z))],
        [shape_of(4, 2, 2, 512, n, dtype=BF)],
        [pl.BlockSpec((1, 2, 2, 512, n), lambda z, *_: (z, 0, 0, 0, 0))],
        [],
        2 * LEN * WIDTH * 4 * n,
        2 * (2 * LEN * WIDTH + WIDTH * 4 * n + LEN * 4 * n),
    )
    return out.reshape(8, 1024, n)


SCALE = HD ** (-0.5)
LOG2E = 1.4426950408889634
QUERY_BLOCK = 512


def forward_body(spot, queries, whole, ids_row, ids_column, out, logsum):
    scores = dot(whole[:, HD : 2 * HD], queries[:, :HD], NT)
    scores = jnp.where(ids_column[...] == ids_row[...], scores, NEGATIVE)
    peak = jnp.max(scores, axis=0, keepdims=True)
    expo = jnp.exp2((scores - peak) * (SCALE * LOG2E))
    total = jnp.sum(expo, axis=0, keepdims=True)
    probs = (expo * (1.0 / total)).astype(BF)
    mixed = dot(whole[:, 2 * HD :], probs, TN)
    out[...] = mixed.T.astype(BF)
    logsum[0] = peak * (SCALE * LOG2E) + jnp.log2(total)


def head_specs():
    return [
        pl.BlockSpec((QUERY_BLOCK, 3 * HD), lambda h, q, p: (q, h)),
        pl.BlockSpec((LEN, 3 * HD), lambda h, q, p: (0, h)),
        pl.BlockSpec((1, QUERY_BLOCK), lambda h, q, p: (0, q)),
        pl.BlockSpec((LEN, 1), lambda h, q, p: (0, 0)),
    ]


def attention(qkv, ids_row, ids_column, spot):
    return call(
        forward_body,
        (4, LEN // QUERY_BLOCK),
        spot,
        (qkv, qkv, ids_row, ids_column),
        head_specs(),
        [shape_of(LEN, QUARTER, dtype=BF), shape_of(4, 1, LEN)],
        [
            pl.BlockSpec((QUERY_BLOCK, HD), lambda h, q, p: (q, h)),
            pl.BlockSpec((1, 1, QUERY_BLOCK), lambda h, q, p: (h, 0, q)),
        ],
        [],
        64 * LEN * LEN * HD,
        LEN * 4 * HD * 8,
    )


def backward_body(spot, queries, whole, ids_row, ids_column, logsum, grad_out, out, sums, grad_keys, grad_values):
    q = pl.program_id(1)
    block = queries.shape[0]
    keys = whole[:, HD : 2 * HD]
    values = whole[:, 2 * HD :]
    scores = dot(keys, queries[:, :HD], NT) * (SCALE * LOG2E)
    scores = jnp.where(ids_column[...] == ids_row[...], scores, NEGATIVE)
    probs = jnp.exp2(scores - logsum[0])
    grad_probs = dot(values, grad_out[...], NT)
    inner = jnp.sum(probs * grad_probs, axis=0, keepdims=True)
    grad_scores = (probs * (grad_probs - inner)).astype(BF)
    back_query = dot(keys, grad_scores, TN)
    back_query = (back_query.T * SCALE).astype(BF)
    out[pl.ds(q * block, block), :HD] = back_query
    add_columns(sums.at[:, :HD], q, [back_query.astype(F32)])
    back_key = dot(grad_scores, queries[:, :HD], NN)
    back_value = dot(probs.astype(BF), grad_out[...], NN)

    @pl.when(q == 0)
    def _():
        grad_keys[...] = back_key
        grad_values[...] = back_value

    @pl.when(q > 0)
    def _():
        grad_keys[...] += back_key
        grad_values[...] += back_value

    @pl.when(q == pl.num_programs(1) - 1)
    def _():
        out[:, HD : 2 * HD] = (grad_keys[...] * SCALE).astype(BF)
        rounded = grad_values[...].astype(BF)
        out[:, 2 * HD :] = rounded
        sums[:, HD : 2 * HD] = jnp.zeros((8, HD), F32)
        sums[:, 2 * HD :] = column_sums([rounded.astype(F32)])


def attention_back(qkv, ids_row, ids_column, logsum, grad_heads, spot):
    return call(
        backward_body,
        (4, LEN // QUERY_BLOCK),
        spot,
        (qkv, qkv, ids_row, ids_column, logsum, grad_heads),
        head_specs()
        + [
            pl.BlockSpec((1, 1, QUERY_BLOCK), lambda h, q, p: (h, 0, q)),
            pl.BlockSpec((QUERY_BLOCK, HD), lambda h, q, p: (q, h)),
        ],
        [shape_of(LEN, 12 * HD, dtype=BF), shape_of(8, 12 * HD)],
        [pl.BlockSpec((LEN, 3 * HD), lambda h, q, p: (0, h)), pl.BlockSpec((8, 3 * HD), lambda h, q, p: (0, h))],
        [pltpu.VMEM((LEN, HD), F32), pltpu.VMEM((LEN, HD), F32)],
        120 * LEN * LEN * HD,
        LEN * 4 * HD * 16,
    )


def row_sum(value):
    folded = value[:, :128] + value[:, 128:256] + value[:, 256:384] + value[:, 384:512]
    return jnp.sum(folded.T, axis=0, keepdims=True)


def rows_of(values):
    rows = [row_sum(v) for v in values]
    return jnp.concatenate(rows + [jnp.zeros_like(rows[0])] * (8 - len(rows)), axis=0)


def columns_of(rows):
    return rows.T


def column_sums(values):
    sums = [jnp.sum(v, axis=0, keepdims=True) for v in values]
    return jnp.concatenate(sums + [jnp.zeros_like(sums[0])] * (8 - len(sums)), axis=0)


def add_columns(ref, t, values):
    sums = column_sums(values)

    @pl.when(t == 0)
    def _():
        ref[...] = sums

    @pl.when(t > 0)
    def _():
        ref[...] += sums


def moments_of(stats):
    total = (stats[0][...] + stats[1][...] + stats[2][...] + stats[3][...]) / WIDTH
    mean = total[0:1]
    return mean, lax.rsqrt(total[1:2] - mean * mean + EPS), total


def summed(refs, t):
    own, near, last = (pick(refs[2 * i], refs[2 * i + 1], t < STEPS // 2).astype(F32) for i in range(3))
    return own + near + last


STEP = 256
STEPS = LEN // STEP
LOW = pl.BlockSpec((STEP, QUARTER), lambda t, p: (jnp.minimum(t, STEPS // 2 - 1), 0))
HIGH = pl.BlockSpec((STEP, QUARTER), lambda t, p: (jnp.maximum(t - STEPS // 2, 0), 0))
PARTS = [LOW, HIGH] * 3
TILE = pl.BlockSpec((STEP, QUARTER), lambda t, p: (t, 0))
STATS = pl.BlockSpec((8, STEP), lambda t, p: (0, t))
VECTOR = fixed((1, QUARTER))
SUMS = fixed((8, QUARTER))
BLOCKS = pl.BlockSpec((4, STEP, 128), lambda t, p: (0, t, 0))


def elementwise(body, spot, ins, in_specs, outs, out_specs):
    return call(body, (STEPS,), spot, ins, in_specs, outs, out_specs, [], 20 * LEN * QUARTER, 16 * LEN * QUARTER)


def write_blocks(out, value):
    for z in range(4):
        out[z] = value[:, z * 128 : z * 128 + 128].astype(BF)


def whole_of(blocks):
    return jnp.concatenate([blocks[z] for z in range(4)], axis=1).astype(F32)


def norm_one_sums(spot, *refs):
    parts, (low, high, bias, resid, stats) = refs[:6], refs[6:]
    t = pl.program_id(0)
    attn = summed(parts, t) + bias[...]
    stream = pick(low, high, t < STEPS // 2).astype(F32)
    total = stream + attn
    resid[...] = total
    stats[...] = rows_of([total, total * total, attn * attn, stream * stream])


def write_halves(t, low, high, value):
    @pl.when(t < STEPS // 2)
    def _():
        low[...] = value

    @pl.when(t >= STEPS // 2)
    def _():
        high[...] = value


def norm_one(spot, resid, s0, s1, s2, s3, gain, shift, low, high, moments):
    mean, rstd, _ = moments_of((s0, s1, s2, s3))
    rows = jnp.concatenate([mean, rstd] + [mean] * 6, axis=0)
    moments[...] = rows
    columns = columns_of(rows)
    hidden = (resid[...] - columns[:, 0:1]) * columns[:, 1:2] * gain[...] + shift[...]
    write_halves(pl.program_id(0), low, high, hidden.astype(BF))


def norm_two_sums(spot, *refs):
    parts = refs[:6]
    bias, resid, moments, gain, shift, dy, gain_two, resid_two, stats = refs[6:]
    t = pl.program_id(0)
    ffn = summed(parts, t) + bias[...]
    columns = columns_of(moments[...])
    hidden = (resid[...] - columns[:, 0:1]) * columns[:, 1:2] * gain[...] + shift[...]
    total = hidden + ffn
    resid_two[...] = total
    scaled = whole_of(dy) * gain_two[...]
    stats[...] = rows_of([total, total * total, scaled, scaled * total, ffn * ffn])


def norm_two(spot, resid_two, s0, s1, s2, s3, dy, gain, shift, layer_out, grad_two, low, high, sums):
    mean, rstd, total = moments_of((s0, s1, s2, s3))
    mean_e = total[2:3]
    along = rstd * (total[3:4] - mean * mean_e)
    columns = columns_of(jnp.concatenate([mean, rstd, mean_e, along] + [mean] * 4, axis=0))
    normed = (resid_two[...] - columns[:, 0:1]) * columns[:, 1:2]
    t = pl.program_id(0)
    upstream = whole_of(dy)
    write_blocks(layer_out, normed * gain[...] + shift[...])
    back = columns[:, 1:2] * (upstream * gain[...] - columns[:, 2:3] - normed * columns[:, 3:4])
    grad_two[...] = back
    rounded = back.astype(BF)
    write_halves(t, low, high, rounded)
    add_columns(sums, t, [upstream * normed, upstream, rounded.astype(F32)])


def back_one_sums(spot, *refs):
    parts = refs[:6]
    grad_two, resid, moments, gain, grad_hidden, stats, sums = refs[6:]
    t = pl.program_id(0)
    upstream = summed(parts, t) + grad_two[...]
    grad_hidden[...] = upstream
    columns = columns_of(moments[...])
    normed = (resid[...] - columns[:, 0:1]) * columns[:, 1:2]
    scaled = upstream * gain[...]
    stats[...] = rows_of([scaled, scaled * normed])
    add_columns(sums, t, [upstream * normed, upstream])


def back_one(spot, grad_hidden, s0, s1, s2, s3, resid, moments, gain, grad_one, low, high, sums):
    total = (s0[...] + s1[...] + s2[...] + s3[...]) / WIDTH
    means = columns_of(total)
    columns = columns_of(moments[...])
    normed = (resid[...] - columns[:, 0:1]) * columns[:, 1:2]
    back = columns[:, 1:2] * (grad_hidden[...] * gain[...] - means[:, 0:1] - normed * means[:, 1:2])
    grad_one[...] = back
    rounded = back.astype(BF)
    t = pl.program_id(0)
    write_halves(t, low, high, rounded)
    add_columns(sums, t, [rounded.astype(F32)])


def finish_back(spot, *refs):
    parts, (grad_one, out) = refs[:6], refs[6:]
    write_blocks(out, summed(parts, pl.program_id(0)) + grad_one[...])


def pass_on(spot, first, second, third, fourth, low, high):
    low[...] = (first[...] + second[...].astype(F32)).astype(BF)
    high[...] = (third[...] + fourth[...].astype(F32)).astype(BF)


def split_y(piece, yi):
    return lax.dynamic_slice_in_dim(piece, yi * 128, 128, 1), lax.dynamic_slice_in_dim(piece, (1 - yi) * 128, 128, 1)


def spread_z(own, other, yi, zi, *after):
    both = jnp.concatenate([own.reshape(2, LEN, 128), other.reshape(2, LEN, 128)], axis=0)
    blocks = []
    for mask, bits in ((0, 0), (1, Z_LOW), (2, Z_HIGH), (3, Z_LOW | Z_HIGH)):
        block = lax.dynamic_index_in_dim(both, (zi ^ mask) ^ (yi * 2), 0, False)
        blocks.append(swap(tie(block, *after), bits) if mask else block)
    return blocks


def assemble_body(spot, *refs):
    blocks, (low, high) = refs[:4], refs[4:]
    t = pl.program_id(0)
    for out, when in ((low, t < STEPS // 2), (high, t >= STEPS // 2)):

        @pl.when(when)
        def _():
            for mask, block in enumerate(blocks):
                out[:, pl.ds(pl.multiple_of((spot[3] ^ mask) * 128, 128), 128)] = block[...]


def assemble(blocks, spot):
    half = shape_of(HALF, QUARTER, dtype=BF)
    return elementwise(
        assemble_body, spot, blocks, [pl.BlockSpec((STEP, 128), lambda t, p: (t, 0))] * 4, [half, half], [LOW, HIGH]
    )


def from_share(share):
    return lax.all_to_all(share, "z", 0, 0, tiled=True).reshape(2, 2 * LEN, 128)


def swap_y(parts, yi):
    own = lax.dynamic_index_in_dim(parts, yi, 0, False)
    return own, swap(lax.dynamic_index_in_dim(parts, 1 - yi, 0, False), Y_BIT)


def side_by_side(own, other, yi, axis):
    return jnp.where(yi == 0, jnp.concatenate([own, other], axis), jnp.concatenate([other, own], axis))


def square_gather(low, high):
    x_low = swap(low, X_BIT)
    y_high = swap(high, Y_BIT)
    x_high = swap(high, X_BIT)
    y_low = swap(low, Y_BIT)
    xy_low = swap(x_low, Y_BIT)
    xy_high = swap(y_high, X_BIT)
    return (low, high, x_low, x_high, y_low, y_high, xy_low, xy_high)


def square_scatter(local, weights, spot, by_rows, lane=0, first=lambda: None, middle=lambda: None, between=lambda: None, after=lambda: None):
    term = functools.partial(partial, local, weights, spot, by_rows, lane)
    far_low, far_high = term(3, BF, BF)
    far_low = swap(far_low, X_BIT)
    far_high = swap(far_high, Y_BIT)
    near_low, x_high = term(2, BF, F32)
    near_low = swap(near_low, X_BIT)
    first()
    y_low, near_high = term(1, F32, BF)
    near_high = swap(near_high, Y_BIT)
    middle()
    half = fixed((HALF, QUARTER))
    last_low, last_high = call(
        pass_on, (1,), spot, (y_low, far_low, x_high, far_high), [half] * 4, [shape_of(HALF, QUARTER, dtype=BF)] * 2,
        [half] * 2, [], LEN * QUARTER, 8 * LEN * QUARTER,
    )
    last_low = swap(last_low, Y_BIT)
    last_high = swap(last_high, X_BIT)
    between()
    spot.after(near_low, near_high)
    own_low, own_high = term(0, F32, F32)
    after()
    return (own_low, own_high, near_low, near_high, last_low, last_high)


def square_stats(stats):
    return (stats, swap(stats, X_BIT), swap(stats, Y_BIT), swap(stats, XY_BIT))


def halve_columns(pieces, yi, *after):
    n = pieces[0].shape[1] // 2
    own = jnp.concatenate([lax.dynamic_slice_in_dim(p, yi * n, n, 1) for p in pieces], axis=1)
    send = tie(jnp.concatenate([lax.dynamic_slice_in_dim(p, (1 - yi) * n, n, 1) for p in pieces], axis=1), *after)
    return jnp.concatenate([own, swap(send, Y_BIT)], axis=0), send


def halve_rows(piece, yi, *after):
    n = piece.shape[0] // 2
    own = lax.dynamic_slice_in_dim(piece, yi * n, n, 0)
    send = tie(lax.dynamic_slice_in_dim(piece, (1 - yi) * n, n, 0), *after)
    return jnp.concatenate([own, swap(send, Y_BIT)], axis=1), send


def gather_zc(piece):
    return lax.all_gather(piece, ("z", "c"), axis=0)


def scatter_zc(full):
    return lax.psum_scatter(full, ("z", "c"), scatter_dimension=0)


def exchange_columns(piece):
    return piece[:512], swap(piece[512:], Y_BIT)


def exchange_rows(piece):
    return piece[:, :512], swap(piece[:, 512:], Y_BIT)


def restore_columns(pair, yi, begin=0, n=None):
    own, other = pair
    n = n or own.shape[1]
    own, other = own[:, begin : begin + n], other[:, begin : begin + n]
    return side_by_side(own.astype(F32), other.astype(F32), yi, 1)


def restore_rows(pair, yi):
    return side_by_side(pair[0].astype(F32), pair[1].astype(F32), yi, 0)


def square_device(
    tokens, lengths, w_query, b_query, w_key, w_value, b_value, w_proj, b_proj, norm_gain, norm_shift,
    w_up, b_up, w_down, b_down, final_gain, final_shift, cotangent,
):
    yi = lax.axis_index("y")
    zi = lax.axis_index("z")
    spot = Order(jnp.stack([lax.axis_index("x") * 2 + yi, yi, lax.axis_index("c"), zi]).astype(jnp.int32))

    token_own, token_send = split_y(tokens, yi)
    token_other = swap(token_send, Y_BIT)
    half_qkv, sent = halve_columns([w_query, w_key, w_value, turn(w_proj, spot)], yi, token_send)
    vectors = jnp.concatenate(
        [v.reshape(2, -1) for v in (b_query, b_value, b_proj, norm_gain, norm_shift, b_down, final_gain, final_shift, b_up)],
        axis=1,
    )
    vectors = lax.dynamic_slice_in_dim(vectors, yi, 1, 0)
    vectors = lax.all_to_all(jnp.broadcast_to(vectors, (4, vectors.shape[1])), "z", 0, 0, tiled=True)
    small = [vectors[:, i * 128 : (i + 1) * 128] for i in range(8)]
    q_bias, v_bias = small[:2]
    p_bias, n_gain, n_shift, d_bias, f_gain, f_shift = (v.reshape(1, QUARTER) for v in small[2:])
    u_bias = vectors[:, 1024:].reshape(1, -1)
    qkv_bias = jnp.stack([q_bias, jnp.zeros_like(q_bias), v_bias], axis=1).reshape(1, -1)

    both = side_by_side(lengths, swap(lengths, Y_BIT), yi, 0)
    ids = segment_ids(lax.dynamic_slice_in_dim(both, zi, 1, 0))[0]
    valid = (ids != lengths.shape[1] - 1).astype(F32)
    ids_row, ids_column = ids[None], ids[:, None]

    full_qkv = gather_zc(half_qkv)
    token_blocks = spread_z(token_own, token_other, yi, zi)
    half_up, sent = halve_columns([w_up], yi, sent)
    spot.after(vectors, half_up)
    token_low, token_high = assemble(token_blocks, spot)
    gathered = square_gather(token_low, token_high)
    full_up = gather_zc(tie(half_up, token_low))
    (qkv,) = wide(gathered, full_qkv, spot, False, finish_bias, (qkv_bias,), 1, n=384)
    half_down, sent = halve_rows(tie(w_down, qkv), yi)
    heads_out, logsum = attention(qkv, ids_row, ids_column, spot)
    spot.after(half_down)
    full_down = gather_zc(half_down)
    full = shape_of(LEN, QUARTER)
    low_half = shape_of(HALF, QUARTER, dtype=BF)
    stats_shape = shape_of(8, LEN)
    sums_shape = shape_of(8, QUARTER)

    parts = square_scatter(heads_out, full_qkv, spot, False, 3)
    resid, stats_one = elementwise(
        norm_one_sums, spot, (*parts, token_low, token_high, p_bias), PARTS + [LOW, HIGH, VECTOR], [full, stats_shape], [TILE, STATS]
    )
    hidden_low, hidden_high, moments = elementwise(
        norm_one, spot, (resid, *square_stats(stats_one), n_gain, n_shift), [TILE] + [STATS] * 4 + [VECTOR] * 2,
        [low_half, low_half, stats_shape], [LOW, HIGH, STATS],
    )
    hidden_wide = square_gather(hidden_low, hidden_high)
    dy_own, dy_send = split_y(tie(cotangent, hidden_low), yi)
    dy_other = swap(dy_send, Y_BIT)
    act, slope = wide(hidden_wide, full_up, spot, False, finish_gelu, (u_bias,), 2)
    dy = side_by_side(dy_own.reshape(2, LEN, 128), dy_other.reshape(2, LEN, 128), yi, 0)
    dy = lax.all_to_all(tie(dy, act), "z", 0, 0, tiled=True)
    parts = square_scatter(act, full_down, spot, True)
    resid_two, stats_two = elementwise(
        norm_two_sums, spot, (*parts, d_bias, resid, moments, n_gain, n_shift, dy, f_gain),
        PARTS + [VECTOR, TILE, STATS, VECTOR, VECTOR, BLOCKS, VECTOR], [full, stats_shape], [TILE, STATS],
    )
    layer_share, grad_two, ffn_low, ffn_high, sums_two = elementwise(
        norm_two, spot, (resid_two, *square_stats(stats_two), dy, f_gain, f_shift),
        [TILE] + [STATS] * 4 + [BLOCKS, VECTOR, VECTOR],
        [shape_of(4, LEN, 128, dtype=BF), full, low_half, low_half, sums_shape], [BLOCKS, TILE, LOW, HIGH, SUMS],
    )
    ffn_wide = square_gather(ffn_low, ffn_high)
    down = grad_whole(ffn_wide, act, spot, True)
    grad_down = scatter_zc(down)
    layer_parts = from_share(tie(layer_share, down))
    grad_pre, sums_up = wide(ffn_wide, full_down, spot, True, finish_slope, (slope,), 1, 1)
    up = []

    def after():
        spot.after(layer_parts)
        up.append(grad_whole(hidden_wide, grad_pre, spot, False))

    parts = square_scatter(grad_pre, full_up, spot, False, after=after)
    grad_hidden, stats_back, sums_back = elementwise(
        back_one_sums, spot, (*parts, grad_two, resid, moments, n_gain),
        PARTS + [TILE, TILE, STATS, VECTOR], [full, stats_shape, sums_shape], [TILE, STATS, SUMS],
    )
    grad_one, attn_low, attn_high, sums_attn = elementwise(
        back_one, spot, (grad_hidden, *square_stats(stats_back), resid, moments, n_gain),
        [TILE] + [STATS] * 4 + [TILE, STATS, VECTOR],
        [full, low_half, low_half, sums_shape], [TILE, LOW, HIGH, SUMS],
    )
    attn_wide = square_gather(attn_low, attn_high)
    grad_up = scatter_zc(tie(up[0], spot.value))
    spot.after(grad_down)
    (grad_heads,) = wide(attn_wide, full_qkv, spot, False, finish_plain, (), 1, n=128, lane=3)
    layer_own, layer_other = swap_y(tie(layer_parts, grad_heads), yi)
    down = exchange_rows(tie(grad_down, grad_heads))
    grad_qkv, sums_qkv = attention_back(qkv, ids_row, ids_column, logsum, grad_heads, spot)
    spot.after(layer_other, down[1])
    sum_last = scatter_zc(grad_pair(gathered, grad_qkv, attn_wide, heads_out, spot))

    kept = []

    def between():
        totals = jnp.stack([tie(stats_one[3], spot.value) * valid, stats_one[2] * valid, stats_two[4] * valid, valid * QUARTER])
        totals = jnp.pad(jnp.sum(totals, axis=1)[None], ((0, 3), (0, 124)))
        vector_sums = jnp.concatenate(
            [
                v.reshape(4, -1)
                for v in (
                    *(tie(sums_qkv[0], spot.value).reshape(4, 3, HD)[:, i] for i in (0, 2)),
                    sums_attn[0], sums_back[0], sums_back[1], sums_two[2], sums_two[0], sums_two[1], sums_up[0], totals,
                )
            ],
            axis=1,
        )
        kept.append((vector_sums, swap(vector_sums, C_BIT)))

    parts = square_scatter(grad_qkv, full_qkv, spot, False, between=between)
    (back,) = elementwise(
        finish_back, spot, (*parts, grad_one), PARTS + [TILE], [shape_of(4, LEN, 128, dtype=BF)], [BLOCKS]
    )
    back_parts = from_share(back)
    up = exchange_columns(tie(grad_up, back))
    sums = kept[0][0] + tie(kept[0][1], back)
    sums = sums + tie(swap(sums, Z_LOW), up[1])
    back_own, back_other = swap_y(back_parts, yi)
    sums = sums + tie(swap(sums, Z_HIGH), back_other)
    last = swap(sum_last[512:], Y_BIT)
    totals = sums[0, 1536:] + swap(sums[0, 1536:], Y_BIT)
    totals = totals + swap(totals, X_BIT)
    norms = jnp.sqrt(totals[:3] / totals[3])
    sums = lax.dynamic_index_in_dim(sums, zi, 0, False)
    other = swap(sums, Y_BIT)
    sums = jnp.where(yi == 0, jnp.stack([sums, other]), jnp.stack([other, sums]))
    vecs = [sums[:, i * 128 : (i + 1) * 128].reshape(-1) for i in range(8)] + [sums[:, 1024:1536].reshape(-1)]
    layer_out = side_by_side(tie(layer_own, back), layer_other, yi, 1)
    grad_tokens = side_by_side(back_own, back_other, yi, 1).astype(F32)
    grad_down = restore_rows((tie(down[0], back), down[1]), yi)
    grad_up = restore_columns(up, yi)
    grad_query, grad_key, grad_value, grad_proj = place_pair(sum_last, last, spot)
    return (
        layer_out, grad_tokens, grad_query, vecs[0], grad_key, grad_value, vecs[1], grad_proj, vecs[2], vecs[3], vecs[4],
        grad_up, vecs[8], grad_down, vecs[5], vecs[6], vecs[7], norms,
    )


def gather_features(piece):
    return lax.all_gather(piece, "col", axis=1, tiled=True)


def scatter_features(partial_sum):
    low = partial_sum.astype(jnp.bfloat16)
    return lax.psum_scatter(low, "col", scatter_dimension=1, tiled=True).astype(F32)


def row_totals(first, second):
    return lax.psum((first, second), "col")


def gather_weights(w_query, w_key, w_value, w_up, w_proj, w_down):
    inner = (
        lax.all_gather(w_query, "row", axis=0, tiled=True),
        lax.all_gather(w_key, "row", axis=0, tiled=True),
        lax.all_gather(w_value, "row", axis=0, tiled=True),
        lax.all_gather(w_up, "row", axis=0, tiled=True),
    )
    outer = (
        lax.all_gather(w_proj, "row", axis=1, tiled=True),
        lax.all_gather(w_down, "row", axis=1, tiled=True),
    )
    return (inner, outer)


def norm_shares(resid, gain, shift):
    width = resid.shape[1] * lax.axis_size("col")
    total, squares = row_totals(jnp.sum(resid, axis=1), jnp.sum(resid * resid, axis=1))
    mean = total / width
    rstd = lax.rsqrt(squares / width - mean * mean + EPS)
    normed = (resid - mean[:, None]) * rstd[:, None]
    return (normed * gain + shift, normed, rstd)


def norm_back(upstream, normed, rstd, gain):
    width = upstream.shape[1] * lax.axis_size("col")
    scaled = upstream * gain
    total, along = row_totals(jnp.sum(scaled, axis=1), jnp.sum(scaled * normed, axis=1))
    back = rstd[:, None] * (scaled - total[:, None] / width - normed * (along[:, None] / width))
    return (back, jnp.sum(upstream * normed, axis=0), jnp.sum(upstream, axis=0))


def attend_forward(pack):
    queries, keys, values, ids = pack
    scale = queries.shape[2] ** (-0.5)
    block = min(512, queries.shape[0])
    same = ids[:, None] == ids[None, :]
    outputs = []
    logsums = []
    for begin in range(0, queries.shape[0], block):
        scores = (
            jnp.einsum(
                "qhd,khd->hqk",
                queries[begin : begin + block],
                keys,
                preferred_element_type=jnp.float32,
            )
            * scale
        )
        scores = jnp.where(same[None, begin : begin + block], scores, NEGATIVE)
        peak = jnp.max(scores, axis=2, keepdims=True)
        expo = jnp.exp(scores - peak)
        total = jnp.sum(expo, axis=2, keepdims=True)
        probs = (expo / total).astype(jnp.bfloat16)
        outputs.append(
            jnp.einsum("hqk,khd->qhd", probs, values, preferred_element_type=jnp.float32)
        )
        logsums.append((peak + jnp.log(total))[:, :, 0])
    return (jnp.concatenate(outputs, axis=0), jnp.concatenate(logsums, axis=1))


def attend_back(pack):
    queries, keys, values, ids, logsum, grad_out = pack
    scale = queries.shape[2] ** (-0.5)
    block = min(512, queries.shape[0])
    same = ids[:, None] == ids[None, :]
    grad_keys = jnp.zeros(keys.shape, jnp.float32)
    grad_values = jnp.zeros(values.shape, jnp.float32)
    grad_queries = []
    for begin in range(0, queries.shape[0], block):
        query_rows = queries[begin : begin + block]
        grad_rows = grad_out[begin : begin + block]
        scores = (
            jnp.einsum("qhd,khd->hqk", query_rows, keys, preferred_element_type=jnp.float32) * scale
        )
        scores = jnp.where(same[None, begin : begin + block], scores, NEGATIVE)
        probs = jnp.exp(scores - logsum[:, begin : begin + block, None])
        grad_probs = jnp.einsum(
            "qhd,khd->hqk", grad_rows, values, preferred_element_type=jnp.float32
        )
        inner = jnp.sum(probs * grad_probs, axis=2, keepdims=True)
        grad_scores = (probs * (grad_probs - inner)).astype(jnp.bfloat16)
        grad_queries.append(
            jnp.einsum("hqk,khd->qhd", grad_scores, keys, preferred_element_type=jnp.float32)
            * scale
        )
        grad_keys = (
            grad_keys
            + jnp.einsum(
                "hqk,qhd->khd", grad_scores, query_rows, preferred_element_type=jnp.float32
            )
            * scale
        )
        grad_values = grad_values + jnp.einsum(
            "hqk,qhd->khd",
            probs.astype(jnp.bfloat16),
            grad_rows,
            preferred_element_type=jnp.float32,
        )
    return (jnp.concatenate(grad_queries, axis=0), grad_keys, grad_values)


def per_device(
    tokens,
    lengths,
    w_query,
    b_query,
    w_key,
    w_value,
    b_value,
    w_proj,
    b_proj,
    norm_gain,
    norm_shift,
    w_up,
    b_up,
    w_down,
    b_down,
    final_gain,
    final_shift,
    cotangent,
):
    rows, share = tokens.shape
    heads = w_query.shape[1] // HD
    ids = segment_ids(lengths)
    seq_count = ids.shape[0]
    valid = (ids.reshape(rows) != lengths.shape[1] - 1).astype(jnp.float32)[:, None]
    inner, outer = gather_weights(w_query, w_key, w_value, w_up, w_proj, w_down)
    full_query, full_key, full_value, full_up = inner
    full_proj, full_down = outer
    stream = tokens.astype(jnp.float32)
    gathered = gather_features(tokens)
    queries = (jnp.dot(gathered, full_query, preferred_element_type=jnp.float32) + b_query).astype(
        jnp.bfloat16
    )
    keys = jnp.dot(gathered, full_key, preferred_element_type=jnp.float32).astype(jnp.bfloat16)
    values = (jnp.dot(gathered, full_value, preferred_element_type=jnp.float32) + b_value).astype(
        jnp.bfloat16
    )
    shape = (seq_count, LEN, heads, HD)
    query_seq = queries.reshape(shape)
    key_seq = keys.reshape(shape)
    value_seq = values.reshape(shape)
    mixed, logsum = lax.map(attend_forward, (query_seq, key_seq, value_seq, ids))
    heads_out = mixed.reshape(rows, heads * HD).astype(jnp.bfloat16)
    attn = (
        scatter_features(jnp.dot(heads_out, full_proj, preferred_element_type=jnp.float32)) + b_proj
    )
    hidden, normed_one, rstd_one = norm_shares(stream + attn, norm_gain, norm_shift)
    hidden_low = gather_features(hidden.astype(jnp.bfloat16))
    pre = jnp.dot(hidden_low, full_up, preferred_element_type=jnp.float32) + b_up
    act, gelu_back = jax.vjp(lambda inputs: jax.nn.gelu(inputs, approximate=True), pre)
    act_low = act.astype(jnp.bfloat16)
    ffn = scatter_features(jnp.dot(act_low, full_down, preferred_element_type=jnp.float32)) + b_down
    result, normed_two, rstd_two = norm_shares(hidden + ffn, final_gain, final_shift)
    totals = lax.psum(
        (
            jnp.sum(valid * stream * stream),
            jnp.sum(valid * attn * attn),
            jnp.sum(valid * ffn * ffn),
            jnp.sum(valid) * share,
        ),
        ("row", "col"),
    )
    norms = jnp.sqrt(jnp.stack([totals[0], totals[1], totals[2]]) / totals[3])
    back_inner, back_outer = gather_weights(w_query, w_key, w_value, w_up, w_proj, w_down)
    full_query, full_key, full_value, full_up = back_inner
    full_proj, full_down = back_outer
    grad_two, grad_fgain, grad_fshift = norm_back(
        cotangent.astype(jnp.float32), normed_two, rstd_two, final_gain
    )
    grad_ffn = grad_two.astype(jnp.bfloat16)
    grad_dbias = jnp.sum(grad_ffn.astype(jnp.float32), axis=0)
    ffn_wide = gather_features(grad_ffn)
    grad_down = jnp.einsum("tf,td->fd", act_low, ffn_wide, preferred_element_type=jnp.float32)
    grad_act = jnp.einsum("td,fd->tf", ffn_wide, full_down, preferred_element_type=jnp.float32)
    grad_pre = gelu_back(grad_act)[0].astype(jnp.bfloat16)
    grad_ubias = jnp.sum(grad_pre.astype(jnp.float32), axis=0)
    grad_up = jnp.einsum("td,tf->df", hidden_low, grad_pre, preferred_element_type=jnp.float32)
    grad_hidden = (
        scatter_features(
            jnp.einsum("tf,df->td", grad_pre, full_up, preferred_element_type=jnp.float32)
        )
        + grad_two
    )
    grad_one, grad_ngain, grad_nshift = norm_back(grad_hidden, normed_one, rstd_one, norm_gain)
    grad_attn = grad_one.astype(jnp.bfloat16)
    grad_pbias = jnp.sum(grad_attn.astype(jnp.float32), axis=0)
    attn_wide = gather_features(grad_attn)
    grad_proj = jnp.einsum("th,td->hd", heads_out, attn_wide, preferred_element_type=jnp.float32)
    grad_heads = jnp.einsum(
        "td,hd->th", attn_wide, full_proj, preferred_element_type=jnp.float32
    ).astype(jnp.bfloat16)
    back_query, back_key, back_value = lax.map(
        attend_back, (query_seq, key_seq, value_seq, ids, logsum, grad_heads.reshape(shape))
    )
    grad_queries = back_query.reshape(rows, heads * HD).astype(jnp.bfloat16)
    grad_keys = back_key.reshape(rows, heads * HD).astype(jnp.bfloat16)
    grad_values = back_value.reshape(rows, heads * HD).astype(jnp.bfloat16)
    grad_qbias = jnp.sum(grad_queries.astype(jnp.float32), axis=0)
    grad_vbias = jnp.sum(grad_values.astype(jnp.float32), axis=0)
    grad_query = jnp.einsum("td,th->dh", gathered, grad_queries, preferred_element_type=jnp.float32)
    grad_key = jnp.einsum("td,th->dh", gathered, grad_keys, preferred_element_type=jnp.float32)
    grad_value = jnp.einsum("td,th->dh", gathered, grad_values, preferred_element_type=jnp.float32)
    partial_back = (
        jnp.einsum("th,dh->td", grad_queries, full_query, preferred_element_type=jnp.float32)
        + jnp.einsum("th,dh->td", grad_keys, full_key, preferred_element_type=jnp.float32)
        + jnp.einsum("th,dh->td", grad_values, full_value, preferred_element_type=jnp.float32)
    )
    grad_tokens = scatter_features(partial_back) + grad_one
    grad_query, grad_key, grad_value, grad_up = (
        lax.psum_scatter(
            grad_query.astype(jnp.bfloat16), "row", scatter_dimension=0, tiled=True
        ).astype(jnp.float32),
        lax.psum_scatter(
            grad_key.astype(jnp.bfloat16), "row", scatter_dimension=0, tiled=True
        ).astype(jnp.float32),
        lax.psum_scatter(
            grad_value.astype(jnp.bfloat16), "row", scatter_dimension=0, tiled=True
        ).astype(jnp.float32),
        lax.psum_scatter(
            grad_up.astype(jnp.bfloat16), "row", scatter_dimension=0, tiled=True
        ).astype(jnp.float32),
    )
    grad_proj, grad_down = (
        lax.psum_scatter(
            grad_proj.astype(jnp.bfloat16), "row", scatter_dimension=1, tiled=True
        ).astype(jnp.float32),
        lax.psum_scatter(
            grad_down.astype(jnp.bfloat16), "row", scatter_dimension=1, tiled=True
        ).astype(jnp.float32),
    )
    vectors = lax.psum(
        (
            grad_qbias,
            grad_vbias,
            grad_pbias,
            grad_ngain,
            grad_nshift,
            grad_ubias,
            grad_dbias,
            grad_fgain,
            grad_fshift,
        ),
        "row",
    )
    return (
        result.astype(jnp.bfloat16),
        grad_tokens,
        grad_query,
        vectors[0],
        grad_key,
        grad_value,
        vectors[1],
        grad_proj,
        vectors[2],
        vectors[3],
        vectors[4],
        grad_up,
        vectors[5],
        grad_down,
        vectors[6],
        vectors[7],
        vectors[8],
        norms,
    )


def placements(row, col):
    grid, turned, share = P(row, col), P(col, row), P(col)
    args = (
        grid, P(row, None), grid, share, grid, grid, share, turned, share, share, share, grid, share, turned, share, share, share, grid,
    )
    outs = (
        grid, grid, grid, share, grid, grid, share, turned, share, share, share, grid, share, turned, share, share, share, P(),
    )
    return (args, outs)


def solution(mesh):
    if mesh.shape["row"] == 4 and mesh.shape["col"] == 8:
        mesh = Mesh(mesh.devices.reshape(2, 2, 4, 2), AXES)
        args, outs = placements(("y", "c"), ("z", "x"))
        body = square_device
    else:
        args, outs = placements("row", "col")
        body = per_device
    return jax.shard_map(body, mesh=mesh, in_specs=args, out_specs=outs, check_vma=False)
```

```python
import functools

import jax
import jax.numpy as jnp
from jax import lax
from jax.experimental import pallas as pl
from jax.experimental.pallas import tpu as pltpu
from jax.sharding import Mesh
from jax.sharding import PartitionSpec as P

HD = 128
LEN = 1024
EPS = 1e-06
NEGATIVE = -1000000000.0
BF = jnp.bfloat16
F32 = jnp.float32


def segment_ids(lengths):
    slots = lengths.shape[1]
    ends = jnp.cumsum(lengths, axis=1)
    places = jnp.arange(LEN, dtype=jnp.int32)
    hits = (places[None, :, None] >= ends[:, None, : slots - 1]).astype(jnp.int32)
    return jnp.sum(hits, axis=2)


AXES = ("y", "c", "z", "x")
X_BIT, Z_LOW, Z_HIGH, C_BIT, Y_BIT = 1, 2, 4, 8, 16
XY_BIT = X_BIT | Y_BIT
QUARTER = 512
HALF = LEN // 2
WIDTH = 2048
NN, NT, TN = ((1,), (0,)), ((1,), (1,)), ((0,), (0,))


def swap(piece, mask):
    return lax.ppermute(piece, AXES, [(i, i ^ mask) for i in range(32)])


def dot(left, right, dims):
    return lax.dot_general(left, right, (dims, ((), ())), preferred_element_type=F32)


def tie(value, *others):
    return lax.optimization_barrier((value, *others))[0]


class Order:
    def __init__(self, value):
        self.value = value

    def after(self, *others):
        self.value = tie(self.value, *others)


LESS = 4


def call(body, grid, spot, ins, in_specs, outs, out_specs, scratch, flops, size):
    result = pl.pallas_call(
        body,
        grid_spec=pltpu.PrefetchScalarGridSpec(
            num_scalar_prefetch=1, grid=grid, in_specs=in_specs, out_specs=out_specs, scratch_shapes=scratch
        ),
        out_shape=outs,
        compiler_params=pltpu.CompilerParams(
            dimension_semantics=("arbitrary",) * len(grid), vmem_limit_bytes=56 * 1024 * 1024
        ),
        cost_estimate=pl.CostEstimate(flops=flops // LESS, bytes_accessed=size // LESS, transcendentals=0),
    )(spot.value, *ins)
    spot.after(result[0])
    return result


def shape_of(*shape, dtype=F32):
    return jax.ShapeDtypeStruct(shape, dtype)


def fixed(shape):
    return pl.BlockSpec(shape, lambda *_: (0,) * len(shape))


def pick(low, high, first):
    return jnp.where(first, low[...], high[...])


SLOTS = (0, 2, 1, 3)


def wide_body(by_rows, finish, count, several, spot, *refs):
    pieces, weights, rest = refs[:8], refs[8], refs[9:]
    extra, outs, kept = rest[: -1 - count], rest[-1 - count : -1], rest[-1]
    t = pl.program_id(1)

    @pl.when(t == 0)
    def _():
        for slot, mask in enumerate(SLOTS):
            start = pl.multiple_of((spot[0] ^ mask) * 128, 128)
            for block in range(4):
                y, c = divmod(block, 2)
                y = y ^ spot[1]
                at = slot * QUARTER + block * 128
                for z in range(several):
                    if by_rows:
                        kept[:, at : at + 128] = weights[0, c, :, pl.ds(pl.multiple_of(y * 512 + start, 128), 128)]
                    else:
                        n = weights.shape[4]
                        kept[at : at + 128, z * n : z * n + n] = weights[z, c, y, pl.ds(start, 128), :]

    total = None
    for slot in range(4):
        tile = pick(pieces[2 * slot], pieces[2 * slot + 1], t == 0)
        part = slice(slot * QUARTER, slot * QUARTER + QUARTER)
        term = dot(tile, kept[:, part], NT) if by_rows else dot(tile, kept[part, :], NN)
        total = term if total is None else total + term
    finish(total, extra, outs)


def wide(pieces, weights, spot, by_rows, finish, extra, count, sums=0, n=None, lane=0):
    several = 1
    if by_rows:
        n = weights.shape[1]
        weights = weights.reshape(4, 2, n, 1024)
        kept = pltpu.VMEM((n, WIDTH), BF)
        block = (1, 2, n, 1024)
    else:
        n = n or weights.shape[2]
        weights = weights.reshape(4, 2, 2, 512, weights.shape[2])
        several = 4 if n < 256 else 1
        kept = pltpu.VMEM((WIDTH, several * n), BF)
        block = (several, 2, 2, 512, n)
    tail = (0,) * (len(block) - 2) + (lane,)
    total = 4 * n
    n = several * n
    bias = pl.BlockSpec((1, n), lambda z, t, *_: (0, z))
    tile = pl.BlockSpec((HALF, n), lambda z, t, *_: (t, z))
    return call(
        functools.partial(wide_body, by_rows, finish, count + sums, several),
        (4 // several, 2),
        spot,
        (*pieces, weights, *extra),
        [fixed(p.shape) for p in pieces]
        + [pl.BlockSpec(block, lambda z, t, *_: (z,) + tail)]
        + [bias if e.shape[0] == 1 else tile for e in extra],
        [shape_of(LEN, total, dtype=BF)] * count + [shape_of(8, total)] * sums,
        [tile] * count + [pl.BlockSpec((8, n), lambda z, t, *_: (0, z))] * sums,
        [kept],
        2 * LEN * WIDTH * total,
        2 * (LEN * WIDTH + WIDTH * total + LEN * total),
    )


def finish_bias(total, extra, outs):
    outs[0][...] = (total + extra[0][...]).astype(BF)


def finish_plain(total, extra, outs):
    outs[0][...] = total.astype(BF)


def finish_gelu(total, extra, outs):
    pre = total + extra[0][...]
    square = pre * pre
    bend = jnp.tanh(0.7978845608028654 * pre * (1.0 + 0.044715 * square))
    rise = 0.5 * (1.0 + bend)
    outs[0][...] = (pre * rise).astype(BF)
    slope = 0.7978845608028654 * (1.0 + 0.134145 * square)
    outs[1][...] = (rise + 0.5 * pre * (1.0 - bend * bend) * slope).astype(BF)


def finish_slope(total, extra, outs):
    rounded = (total * extra[0][...].astype(F32)).astype(BF)
    outs[0][...] = rounded
    add_columns(outs[1], pl.program_id(1), [rounded.astype(F32)])


def partial_body(by_rows, n, spot, local, *rest):
    weights, (low, high) = rest[:-2], rest[-2:]
    t = pl.program_id(0)
    total = None
    for z in range(4):
        tile = local[:, z * n : (z + 1) * n]
        if by_rows:
            kept = jnp.concatenate([weights[y][z, c] for y in range(2) for c in range(2)], axis=1)
            term = dot(tile, kept, NN)
        else:
            kept = jnp.concatenate([weights[0][z, c, y ^ spot[1]] for y in range(2) for c in range(2)], axis=0)
            term = dot(tile, kept, NT)
        total = term if total is None else total + term

    @pl.when(t == 0)
    def _():
        low[...] = total.astype(low.dtype)

    @pl.when(t == 1)
    def _():
        high[...] = total.astype(high.dtype)


def partial(local, weights, spot, by_rows, lane, mask, low, high):
    n = local.shape[1] // 4
    if by_rows:
        weights = weights.reshape(4, 2, n, 1024)
        specs = [
            pl.BlockSpec((4, 2, n, 128), functools.partial(lambda y, t, p: (0, 0, 0, (y ^ p[1]) * 4 + (p[0] ^ mask)), y))
            for y in range(2)
        ]
        ins = (weights, weights)
    else:
        weights = weights.reshape(4, 2, 2, 512, weights.shape[2])
        specs = [pl.BlockSpec((4, 2, 2, 128, n), lambda t, p: (0, 0, 0, p[0] ^ mask, lane))]
        ins = (weights,)
    return call(
        functools.partial(partial_body, by_rows, n),
        (2,),
        spot,
        (local, *ins),
        [pl.BlockSpec((HALF, 4 * n), lambda t, p: (t, 0))] + specs,
        [shape_of(HALF, QUARTER, dtype=low), shape_of(HALF, QUARTER, dtype=high)],
        [fixed((HALF, QUARTER))] * 2,
        [],
        2 * LEN * QUARTER * 4 * n,
        2 * (LEN * 4 * n + QUARTER * 4 * n + LEN * QUARTER),
    )


def grad_whole_body(by_rows, spot, *refs):
    pieces, local, out = refs[:8], refs[8], refs[9]
    for slot, mask in enumerate(SLOTS):
        start = pl.multiple_of((spot[0] ^ mask) * 128, 128)

        def term(piece, tile):
            return dot(tile, piece, TN) if by_rows else dot(piece, tile, TN)

        total = term(pieces[2 * slot][...], local[:HALF, :]) + term(pieces[2 * slot + 1][...], local[HALF:, :])
        for block in range(4):
            y, c = divmod(block, 2)
            y = y ^ spot[1]
            part = slice(block * 128, block * 128 + 128)
            if by_rows:
                out[0, c, :, pl.ds(pl.multiple_of(y * 512 + start, 128), 128)] = total[:, part].astype(BF)
            else:
                out[0, c, y, pl.ds(start, 128), :] = total[part, :].astype(BF)


def grad_whole(pieces, local, spot, by_rows):
    n = local.shape[1] // 4
    shape = (4, 2, n, 1024) if by_rows else (4, 2, 2, 512, n)
    tail = (0,) * (len(shape) - 1)
    (out,) = call(
        functools.partial(grad_whole_body, by_rows),
        (4,),
        spot,
        (*pieces, local),
        [fixed(p.shape) for p in pieces] + [pl.BlockSpec((LEN, n), lambda z, *_: (0, z))],
        [shape_of(*shape, dtype=BF)],
        [pl.BlockSpec((1,) + shape[1:], lambda z, *_: (z,) + tail)],
        [],
        2 * LEN * WIDTH * 4 * n,
        2 * (LEN * WIDTH + WIDTH * 4 * n + LEN * 4 * n),
    )
    return out.reshape(8, n, 1024) if by_rows else out.reshape(8, 1024, n)


def place_pair_body(spot, own, other, query, key, value, proj):
    for side, part in ((spot[1], own), (1 - spot[1], other)):
        at = pl.ds(pl.multiple_of(side * 128, 128), 128)
        for i, out in enumerate((query, key, value)):
            out[:, at] = part[:, i * 128 : i * 128 + 128].astype(F32)
        proj[at, :] = part[:, 384:].astype(F32).T


def place_pair(own, other, spot):
    grid = [shape_of(512, 256)] * 3 + [shape_of(256, 512)]
    return call(
        place_pair_body, (1,), spot, (own, other), [fixed((512, 512))] * 2, grid, [fixed(g.shape) for g in grid], [],
        2 * 512 * 512, 8 * 512 * 512,
    )


def turn_body(spot, piece, out):
    out[...] = piece[...].T


def turn(piece, spot):
    rows, width = piece.shape
    (out,) = call(
        turn_body, (1,), spot, (piece,), [fixed(piece.shape)], [shape_of(width, rows, dtype=BF)], [fixed((width, rows))], [],
        rows * width, 4 * rows * width,
    )
    return out


def grad_pair_body(spot, *refs):
    out = refs[18]
    for slot, mask in enumerate(SLOTS):
        start = pl.multiple_of((spot[0] ^ mask) * 128, 128)
        at = 0
        for pieces, local in ((refs[:8], refs[8]), (refs[9:17], refs[17])):
            total = dot(pieces[2 * slot][...], local[:HALF, :], TN) + dot(pieces[2 * slot + 1][...], local[HALF:, :], TN)
            n = local.shape[1]
            for block in range(4):
                y, c = divmod(block, 2)
                out[0, c, y ^ spot[1], pl.ds(start, 128), at : at + n] = total[block * 128 : block * 128 + 128, :].astype(BF)
            at += n


def grad_pair(first, first_local, second, second_local, spot):
    sizes = [local.shape[1] // 4 for local in (first_local, second_local)]
    n = sum(sizes)
    specs = [fixed(p.shape) for p in first]
    (out,) = call(
        grad_pair_body,
        (4,),
        spot,
        (*first, first_local, *second, second_local),
        specs + [pl.BlockSpec((LEN, sizes[0]), lambda z, *_: (0, z))] + specs + [pl.BlockSpec((LEN, sizes[1]), lambda z, *_: (0, z))],
        [shape_of(4, 2, 2, 512, n, dtype=BF)],
        [pl.BlockSpec((1, 2, 2, 512, n), lambda z, *_: (z, 0, 0, 0, 0))],
        [],
        2 * LEN * WIDTH * 4 * n,
        2 * (2 * LEN * WIDTH + WIDTH * 4 * n + LEN * 4 * n),
    )
    return out.reshape(8, 1024, n)


SCALE = HD ** (-0.5)
LOG2E = 1.4426950408889634
QUERY_BLOCK = 512


def forward_body(spot, queries, whole, ids_row, ids_column, out, logsum):
    scores = dot(whole[:, HD : 2 * HD], queries[:, :HD], NT)
    scores = jnp.where(ids_column[...] == ids_row[...], scores, NEGATIVE)
    peak = jnp.max(scores, axis=0, keepdims=True)
    expo = jnp.exp2((scores - peak) * (SCALE * LOG2E))
    total = jnp.sum(expo, axis=0, keepdims=True)
    probs = (expo * (1.0 / total)).astype(BF)
    mixed = dot(whole[:, 2 * HD :], probs, TN)
    out[...] = mixed.T.astype(BF)
    logsum[0] = peak * (SCALE * LOG2E) + jnp.log2(total)


def head_specs():
    return [
        pl.BlockSpec((QUERY_BLOCK, 3 * HD), lambda h, q, p: (q, h)),
        pl.BlockSpec((LEN, 3 * HD), lambda h, q, p: (0, h)),
        pl.BlockSpec((1, QUERY_BLOCK), lambda h, q, p: (0, q)),
        pl.BlockSpec((LEN, 1), lambda h, q, p: (0, 0)),
    ]


def attention(qkv, ids_row, ids_column, spot):
    return call(
        forward_body,
        (4, LEN // QUERY_BLOCK),
        spot,
        (qkv, qkv, ids_row, ids_column),
        head_specs(),
        [shape_of(LEN, QUARTER, dtype=BF), shape_of(4, 1, LEN)],
        [
            pl.BlockSpec((QUERY_BLOCK, HD), lambda h, q, p: (q, h)),
            pl.BlockSpec((1, 1, QUERY_BLOCK), lambda h, q, p: (h, 0, q)),
        ],
        [],
        64 * LEN * LEN * HD,
        LEN * 4 * HD * 8,
    )


def backward_body(spot, queries, whole, ids_row, ids_column, logsum, grad_out, out, sums, grad_keys, grad_values):
    q = pl.program_id(1)
    block = queries.shape[0]
    keys = whole[:, HD : 2 * HD]
    values = whole[:, 2 * HD :]
    scores = dot(keys, queries[:, :HD], NT) * (SCALE * LOG2E)
    scores = jnp.where(ids_column[...] == ids_row[...], scores, NEGATIVE)
    probs = jnp.exp2(scores - logsum[0])
    grad_probs = dot(values, grad_out[...], NT)
    inner = jnp.sum(probs * grad_probs, axis=0, keepdims=True)
    grad_scores = (probs * (grad_probs - inner)).astype(BF)
    back_query = dot(keys, grad_scores, TN)
    back_query = (back_query.T * SCALE).astype(BF)
    out[pl.ds(q * block, block), :HD] = back_query
    add_columns(sums.at[:, :HD], q, [back_query.astype(F32)])
    back_key = dot(grad_scores, queries[:, :HD], NN)
    back_value = dot(probs.astype(BF), grad_out[...], NN)

    @pl.when(q == 0)
    def _():
        grad_keys[...] = back_key
        grad_values[...] = back_value

    @pl.when(q > 0)
    def _():
        grad_keys[...] += back_key
        grad_values[...] += back_value

    @pl.when(q == pl.num_programs(1) - 1)
    def _():
        out[:, HD : 2 * HD] = (grad_keys[...] * SCALE).astype(BF)
        rounded = grad_values[...].astype(BF)
        out[:, 2 * HD :] = rounded
        sums[:, HD : 2 * HD] = jnp.zeros((8, HD), F32)
        sums[:, 2 * HD :] = column_sums([rounded.astype(F32)])


def attention_back(qkv, ids_row, ids_column, logsum, grad_heads, spot):
    return call(
        backward_body,
        (4, LEN // QUERY_BLOCK),
        spot,
        (qkv, qkv, ids_row, ids_column, logsum, grad_heads),
        head_specs()
        + [
            pl.BlockSpec((1, 1, QUERY_BLOCK), lambda h, q, p: (h, 0, q)),
            pl.BlockSpec((QUERY_BLOCK, HD), lambda h, q, p: (q, h)),
        ],
        [shape_of(LEN, 12 * HD, dtype=BF), shape_of(8, 12 * HD)],
        [pl.BlockSpec((LEN, 3 * HD), lambda h, q, p: (0, h)), pl.BlockSpec((8, 3 * HD), lambda h, q, p: (0, h))],
        [pltpu.VMEM((LEN, HD), F32), pltpu.VMEM((LEN, HD), F32)],
        120 * LEN * LEN * HD,
        LEN * 4 * HD * 16,
    )


def row_sum(value):
    folded = value[:, :128] + value[:, 128:256] + value[:, 256:384] + value[:, 384:512]
    return jnp.sum(folded.T, axis=0, keepdims=True)


def rows_of(values):
    rows = [row_sum(v) for v in values]
    return jnp.concatenate(rows + [jnp.zeros_like(rows[0])] * (8 - len(rows)), axis=0)


def columns_of(rows):
    return rows.T


def column_sums(values):
    sums = [jnp.sum(v, axis=0, keepdims=True) for v in values]
    return jnp.concatenate(sums + [jnp.zeros_like(sums[0])] * (8 - len(sums)), axis=0)


def add_columns(ref, t, values):
    sums = column_sums(values)

    @pl.when(t == 0)
    def _():
        ref[...] = sums

    @pl.when(t > 0)
    def _():
        ref[...] += sums


def moments_of(stats):
    total = (stats[0][...] + stats[1][...] + stats[2][...] + stats[3][...]) / WIDTH
    mean = total[0:1]
    return mean, lax.rsqrt(total[1:2] - mean * mean + EPS), total


def summed(refs, t):
    own, near, last = (pick(refs[2 * i], refs[2 * i + 1], t < STEPS // 2).astype(F32) for i in range(3))
    return own + near + last


STEP = 256
STEPS = LEN // STEP
LOW = pl.BlockSpec((STEP, QUARTER), lambda t, p: (jnp.minimum(t, STEPS // 2 - 1), 0))
HIGH = pl.BlockSpec((STEP, QUARTER), lambda t, p: (jnp.maximum(t - STEPS // 2, 0), 0))
PARTS = [LOW, HIGH] * 3
TILE = pl.BlockSpec((STEP, QUARTER), lambda t, p: (t, 0))
STATS = pl.BlockSpec((8, STEP), lambda t, p: (0, t))
VECTOR = fixed((1, QUARTER))
SUMS = fixed((8, QUARTER))
BLOCKS = pl.BlockSpec((4, STEP, 128), lambda t, p: (0, t, 0))


def elementwise(body, spot, ins, in_specs, outs, out_specs):
    return call(body, (STEPS,), spot, ins, in_specs, outs, out_specs, [], 20 * LEN * QUARTER, 16 * LEN * QUARTER)


def write_blocks(out, value):
    for z in range(4):
        out[z] = value[:, z * 128 : z * 128 + 128].astype(BF)


def whole_of(blocks):
    return jnp.concatenate([blocks[z] for z in range(4)], axis=1).astype(F32)


def norm_one_sums(spot, *refs):
    parts, (low, high, bias, resid, stats) = refs[:6], refs[6:]
    t = pl.program_id(0)
    attn = summed(parts, t) + bias[...]
    stream = pick(low, high, t < STEPS // 2).astype(F32)
    total = stream + attn
    resid[...] = total
    stats[...] = rows_of([total, total * total, attn * attn, stream * stream])


def write_halves(t, low, high, value):
    @pl.when(t < STEPS // 2)
    def _():
        low[...] = value

    @pl.when(t >= STEPS // 2)
    def _():
        high[...] = value


def norm_one(spot, resid, s0, s1, s2, s3, gain, shift, low, high, moments):
    mean, rstd, _ = moments_of((s0, s1, s2, s3))
    rows = jnp.concatenate([mean, rstd] + [mean] * 6, axis=0)
    moments[...] = rows
    columns = columns_of(rows)
    hidden = (resid[...] - columns[:, 0:1]) * columns[:, 1:2] * gain[...] + shift[...]
    write_halves(pl.program_id(0), low, high, hidden.astype(BF))


def norm_two_sums(spot, *refs):
    parts = refs[:6]
    bias, resid, moments, gain, shift, dy, gain_two, resid_two, stats = refs[6:]
    t = pl.program_id(0)
    ffn = summed(parts, t) + bias[...]
    columns = columns_of(moments[...])
    hidden = (resid[...] - columns[:, 0:1]) * columns[:, 1:2] * gain[...] + shift[...]
    total = hidden + ffn
    resid_two[...] = total
    scaled = whole_of(dy) * gain_two[...]
    stats[...] = rows_of([total, total * total, scaled, scaled * total, ffn * ffn])


def norm_two(spot, resid_two, s0, s1, s2, s3, dy, gain, shift, layer_out, grad_two, low, high, sums):
    mean, rstd, total = moments_of((s0, s1, s2, s3))
    mean_e = total[2:3]
    along = rstd * (total[3:4] - mean * mean_e)
    columns = columns_of(jnp.concatenate([mean, rstd, mean_e, along] + [mean] * 4, axis=0))
    normed = (resid_two[...] - columns[:, 0:1]) * columns[:, 1:2]
    t = pl.program_id(0)
    upstream = whole_of(dy)
    write_blocks(layer_out, normed * gain[...] + shift[...])
    back = columns[:, 1:2] * (upstream * gain[...] - columns[:, 2:3] - normed * columns[:, 3:4])
    grad_two[...] = back
    rounded = back.astype(BF)
    write_halves(t, low, high, rounded)
    add_columns(sums, t, [upstream * normed, upstream, rounded.astype(F32)])


def back_one_sums(spot, *refs):
    parts = refs[:6]
    grad_two, resid, moments, gain, grad_hidden, stats, sums = refs[6:]
    t = pl.program_id(0)
    upstream = summed(parts, t) + grad_two[...]
    grad_hidden[...] = upstream
    columns = columns_of(moments[...])
    normed = (resid[...] - columns[:, 0:1]) * columns[:, 1:2]
    scaled = upstream * gain[...]
    stats[...] = rows_of([scaled, scaled * normed])
    add_columns(sums, t, [upstream * normed, upstream])


def back_one(spot, grad_hidden, s0, s1, s2, s3, resid, moments, gain, grad_one, low, high, sums):
    total = (s0[...] + s1[...] + s2[...] + s3[...]) / WIDTH
    means = columns_of(total)
    columns = columns_of(moments[...])
    normed = (resid[...] - columns[:, 0:1]) * columns[:, 1:2]
    back = columns[:, 1:2] * (grad_hidden[...] * gain[...] - means[:, 0:1] - normed * means[:, 1:2])
    grad_one[...] = back
    rounded = back.astype(BF)
    t = pl.program_id(0)
    write_halves(t, low, high, rounded)
    add_columns(sums, t, [rounded.astype(F32)])


def finish_back(spot, *refs):
    parts, (grad_one, out) = refs[:6], refs[6:]
    write_blocks(out, summed(parts, pl.program_id(0)) + grad_one[...])


def pass_on(spot, first, second, third, fourth, low, high):
    low[...] = (first[...] + second[...].astype(F32)).astype(BF)
    high[...] = (third[...] + fourth[...].astype(F32)).astype(BF)


def split_y(piece, yi):
    return lax.dynamic_slice_in_dim(piece, yi * 128, 128, 1), lax.dynamic_slice_in_dim(piece, (1 - yi) * 128, 128, 1)


def spread_z(own, other, yi, zi, *after):
    both = jnp.concatenate([own.reshape(2, LEN, 128), other.reshape(2, LEN, 128)], axis=0)
    blocks = []
    for mask, bits in ((0, 0), (1, Z_LOW), (2, Z_HIGH), (3, Z_LOW | Z_HIGH)):
        block = lax.dynamic_index_in_dim(both, (zi ^ mask) ^ (yi * 2), 0, False)
        blocks.append(swap(tie(block, *after), bits) if mask else block)
    return blocks


def assemble_body(spot, *refs):
    blocks, (low, high) = refs[:4], refs[4:]
    t = pl.program_id(0)
    for out, when in ((low, t < STEPS // 2), (high, t >= STEPS // 2)):

        @pl.when(when)
        def _():
            for mask, block in enumerate(blocks):
                out[:, pl.ds(pl.multiple_of((spot[3] ^ mask) * 128, 128), 128)] = block[...]


def assemble(blocks, spot):
    half = shape_of(HALF, QUARTER, dtype=BF)
    return elementwise(
        assemble_body, spot, blocks, [pl.BlockSpec((STEP, 128), lambda t, p: (t, 0))] * 4, [half, half], [LOW, HIGH]
    )


def from_share(share):
    return lax.all_to_all(share, "z", 0, 0, tiled=True).reshape(2, 2 * LEN, 128)


def swap_y(parts, yi):
    own = lax.dynamic_index_in_dim(parts, yi, 0, False)
    return own, swap(lax.dynamic_index_in_dim(parts, 1 - yi, 0, False), Y_BIT)


def side_by_side(own, other, yi, axis):
    return jnp.where(yi == 0, jnp.concatenate([own, other], axis), jnp.concatenate([other, own], axis))


def square_gather(low, high):
    x_low = swap(low, X_BIT)
    y_high = swap(high, Y_BIT)
    x_high = swap(high, X_BIT)
    y_low = swap(low, Y_BIT)
    xy_low = swap(x_low, Y_BIT)
    xy_high = swap(y_high, X_BIT)
    return (low, high, x_low, x_high, y_low, y_high, xy_low, xy_high)


def square_scatter(local, weights, spot, by_rows, lane=0, first=lambda: None, middle=lambda: None, between=lambda: None, after=lambda: None):
    term = functools.partial(partial, local, weights, spot, by_rows, lane)
    far_low, far_high = term(3, BF, BF)
    far_low = swap(far_low, X_BIT)
    far_high = swap(far_high, Y_BIT)
    near_low, x_high = term(2, BF, F32)
    near_low = swap(near_low, X_BIT)
    first()
    y_low, near_high = term(1, F32, BF)
    near_high = swap(near_high, Y_BIT)
    middle()
    half = fixed((HALF, QUARTER))
    last_low, last_high = call(
        pass_on, (1,), spot, (y_low, far_low, x_high, far_high), [half] * 4, [shape_of(HALF, QUARTER, dtype=BF)] * 2,
        [half] * 2, [], LEN * QUARTER, 8 * LEN * QUARTER,
    )
    last_low = swap(last_low, Y_BIT)
    last_high = swap(last_high, X_BIT)
    between()
    spot.after(near_low, near_high)
    own_low, own_high = term(0, F32, F32)
    after()
    return (own_low, own_high, near_low, near_high, last_low, last_high)


def square_stats(stats):
    return (stats, swap(stats, X_BIT), swap(stats, Y_BIT), swap(stats, XY_BIT))


def halve_columns(pieces, yi, *after):
    n = pieces[0].shape[1] // 2
    own = jnp.concatenate([lax.dynamic_slice_in_dim(p, yi * n, n, 1) for p in pieces], axis=1)
    send = tie(jnp.concatenate([lax.dynamic_slice_in_dim(p, (1 - yi) * n, n, 1) for p in pieces], axis=1), *after)
    return jnp.concatenate([own, swap(send, Y_BIT)], axis=0), send


def halve_rows(piece, yi, *after):
    n = piece.shape[0] // 2
    own = lax.dynamic_slice_in_dim(piece, yi * n, n, 0)
    send = tie(lax.dynamic_slice_in_dim(piece, (1 - yi) * n, n, 0), *after)
    return jnp.concatenate([own, swap(send, Y_BIT)], axis=1), send


def gather_zc(piece):
    return lax.all_gather(piece, ("z", "c"), axis=0)


def scatter_zc(full):
    return lax.psum_scatter(full, ("z", "c"), scatter_dimension=0)


def exchange_columns(piece):
    return piece[:512], swap(piece[512:], Y_BIT)


def exchange_rows(piece):
    return piece[:, :512], swap(piece[:, 512:], Y_BIT)


def restore_columns(pair, yi, begin=0, n=None):
    own, other = pair
    n = n or own.shape[1]
    own, other = own[:, begin : begin + n], other[:, begin : begin + n]
    return side_by_side(own.astype(F32), other.astype(F32), yi, 1)


def restore_rows(pair, yi):
    return side_by_side(pair[0].astype(F32), pair[1].astype(F32), yi, 0)


def square_device(
    tokens, lengths, w_query, b_query, w_key, w_value, b_value, w_proj, b_proj, norm_gain, norm_shift,
    w_up, b_up, w_down, b_down, final_gain, final_shift, cotangent,
):
    yi = lax.axis_index("y")
    zi = lax.axis_index("z")
    spot = Order(jnp.stack([lax.axis_index("x") * 2 + yi, yi, lax.axis_index("c"), zi]).astype(jnp.int32))

    token_own, token_send = split_y(tokens, yi)
    token_other = swap(token_send, Y_BIT)
    half_qkv, sent = halve_columns([w_query, w_key, w_value, turn(w_proj, spot)], yi, token_send)
    vectors = jnp.concatenate(
        [v.reshape(2, -1) for v in (b_query, b_value, b_proj, norm_gain, norm_shift, b_down, final_gain, final_shift, b_up)],
        axis=1,
    )
    vectors = lax.dynamic_slice_in_dim(vectors, yi, 1, 0)
    vectors = lax.all_to_all(jnp.broadcast_to(vectors, (4, vectors.shape[1])), "z", 0, 0, tiled=True)
    small = [vectors[:, i * 128 : (i + 1) * 128] for i in range(8)]
    q_bias, v_bias = small[:2]
    p_bias, n_gain, n_shift, d_bias, f_gain, f_shift = (v.reshape(1, QUARTER) for v in small[2:])
    u_bias = vectors[:, 1024:].reshape(1, -1)
    qkv_bias = jnp.stack([q_bias, jnp.zeros_like(q_bias), v_bias], axis=1).reshape(1, -1)

    both = side_by_side(lengths, swap(lengths, Y_BIT), yi, 0)
    ids = segment_ids(lax.dynamic_slice_in_dim(both, zi, 1, 0))[0]
    valid = (ids != lengths.shape[1] - 1).astype(F32)
    ids_row, ids_column = ids[None], ids[:, None]

    full_qkv = gather_zc(half_qkv)
    token_blocks = spread_z(token_own, token_other, yi, zi)
    half_up, sent = halve_columns([w_up], yi, sent)
    spot.after(vectors, half_up)
    token_low, token_high = assemble(token_blocks, spot)
    gathered = square_gather(token_low, token_high)
    full_up = gather_zc(tie(half_up, token_low))
    (qkv,) = wide(gathered, full_qkv, spot, False, finish_bias, (qkv_bias,), 1, n=384)
    half_down, sent = halve_rows(tie(w_down, qkv), yi)
    heads_out, logsum = attention(qkv, ids_row, ids_column, spot)
    spot.after(half_down)
    full_down = gather_zc(half_down)
    full = shape_of(LEN, QUARTER)
    low_half = shape_of(HALF, QUARTER, dtype=BF)
    stats_shape = shape_of(8, LEN)
    sums_shape = shape_of(8, QUARTER)

    parts = square_scatter(heads_out, full_qkv, spot, False, 3)
    resid, stats_one = elementwise(
        norm_one_sums, spot, (*parts, token_low, token_high, p_bias), PARTS + [LOW, HIGH, VECTOR], [full, stats_shape], [TILE, STATS]
    )
    hidden_low, hidden_high, moments = elementwise(
        norm_one, spot, (resid, *square_stats(stats_one), n_gain, n_shift), [TILE] + [STATS] * 4 + [VECTOR] * 2,
        [low_half, low_half, stats_shape], [LOW, HIGH, STATS],
    )
    hidden_wide = square_gather(hidden_low, hidden_high)
    dy_own, dy_send = split_y(tie(cotangent, hidden_low), yi)
    dy_other = swap(dy_send, Y_BIT)
    act, slope = wide(hidden_wide, full_up, spot, False, finish_gelu, (u_bias,), 2)
    dy = side_by_side(dy_own.reshape(2, LEN, 128), dy_other.reshape(2, LEN, 128), yi, 0)
    dy = lax.all_to_all(tie(dy, act), "z", 0, 0, tiled=True)
    parts = square_scatter(act, full_down, spot, True)
    resid_two, stats_two = elementwise(
        norm_two_sums, spot, (*parts, d_bias, resid, moments, n_gain, n_shift, dy, f_gain),
        PARTS + [VECTOR, TILE, STATS, VECTOR, VECTOR, BLOCKS, VECTOR], [full, stats_shape], [TILE, STATS],
    )
    layer_share, grad_two, ffn_low, ffn_high, sums_two = elementwise(
        norm_two, spot, (resid_two, *square_stats(stats_two), dy, f_gain, f_shift),
        [TILE] + [STATS] * 4 + [BLOCKS, VECTOR, VECTOR],
        [shape_of(4, LEN, 128, dtype=BF), full, low_half, low_half, sums_shape], [BLOCKS, TILE, LOW, HIGH, SUMS],
    )
    ffn_wide = square_gather(ffn_low, ffn_high)
    layer_parts = from_share(layer_share)
    spot.after(layer_parts)
    down = grad_whole(ffn_wide, act, spot, True)
    grad_down = scatter_zc(down)
    grad_pre, sums_up = wide(ffn_wide, full_down, spot, True, finish_slope, (slope,), 1, 1)
    up = []

    def after():
        up.append(grad_whole(hidden_wide, grad_pre, spot, False))

    parts = square_scatter(grad_pre, full_up, spot, False, after=after)
    grad_hidden, stats_back, sums_back = elementwise(
        back_one_sums, spot, (*parts, grad_two, resid, moments, n_gain),
        PARTS + [TILE, TILE, STATS, VECTOR], [full, stats_shape, sums_shape], [TILE, STATS, SUMS],
    )
    grad_one, attn_low, attn_high, sums_attn = elementwise(
        back_one, spot, (grad_hidden, *square_stats(stats_back), resid, moments, n_gain),
        [TILE] + [STATS] * 4 + [TILE, STATS, VECTOR],
        [full, low_half, low_half, sums_shape], [TILE, LOW, HIGH, SUMS],
    )
    attn_wide = square_gather(attn_low, attn_high)
    grad_up = scatter_zc(tie(up[0], spot.value))
    spot.after(grad_down)
    (grad_heads,) = wide(attn_wide, full_qkv, spot, False, finish_plain, (), 1, n=128, lane=3)
    layer_own, layer_other = swap_y(tie(layer_parts, grad_heads), yi)
    down = exchange_rows(tie(grad_down, grad_heads))
    grad_qkv, sums_qkv = attention_back(qkv, ids_row, ids_column, logsum, grad_heads, spot)
    spot.after(layer_other, down[1])
    sum_last = scatter_zc(grad_pair(gathered, grad_qkv, attn_wide, heads_out, spot))

    kept = []

    def between():
        totals = jnp.stack([tie(stats_one[3], spot.value) * valid, stats_one[2] * valid, stats_two[4] * valid, valid * QUARTER])
        totals = jnp.pad(jnp.sum(totals, axis=1)[None], ((0, 3), (0, 124)))
        vector_sums = jnp.concatenate(
            [
                v.reshape(4, -1)
                for v in (
                    *(tie(sums_qkv[0], spot.value).reshape(4, 3, HD)[:, i] for i in (0, 2)),
                    sums_attn[0], sums_back[0], sums_back[1], sums_two[2], sums_two[0], sums_two[1], sums_up[0], totals,
                )
            ],
            axis=1,
        )
        kept.append((vector_sums, swap(vector_sums, C_BIT)))

    parts = square_scatter(grad_qkv, full_qkv, spot, False, between=between)
    (back,) = elementwise(
        finish_back, spot, (*parts, grad_one), PARTS + [TILE], [shape_of(4, LEN, 128, dtype=BF)], [BLOCKS]
    )
    back_parts = from_share(back)
    up = exchange_columns(tie(grad_up, back))
    sums = kept[0][0] + tie(kept[0][1], back)
    sums = sums + tie(swap(sums, Z_LOW), up[1])
    back_own, back_other = swap_y(back_parts, yi)
    sums = sums + tie(swap(sums, Z_HIGH), back_other)
    last = swap(sum_last[512:], Y_BIT)
    totals = sums[0, 1536:] + swap(sums[0, 1536:], Y_BIT)
    totals = totals + swap(totals, X_BIT)
    norms = jnp.sqrt(totals[:3] / totals[3])
    sums = lax.dynamic_index_in_dim(sums, zi, 0, False)
    other = swap(sums, Y_BIT)
    sums = jnp.where(yi == 0, jnp.stack([sums, other]), jnp.stack([other, sums]))
    vecs = [sums[:, i * 128 : (i + 1) * 128].reshape(-1) for i in range(8)] + [sums[:, 1024:1536].reshape(-1)]
    layer_out = side_by_side(tie(layer_own, back), layer_other, yi, 1)
    grad_tokens = side_by_side(back_own, back_other, yi, 1).astype(F32)
    grad_down = restore_rows((tie(down[0], back), down[1]), yi)
    grad_up = restore_columns(up, yi)
    grad_query, grad_key, grad_value, grad_proj = place_pair(sum_last, last, spot)
    return (
        layer_out, grad_tokens, grad_query, vecs[0], grad_key, grad_value, vecs[1], grad_proj, vecs[2], vecs[3], vecs[4],
        grad_up, vecs[8], grad_down, vecs[5], vecs[6], vecs[7], norms,
    )


def gather_features(piece):
    return lax.all_gather(piece, "col", axis=1, tiled=True)


def scatter_features(partial_sum):
    low = partial_sum.astype(jnp.bfloat16)
    return lax.psum_scatter(low, "col", scatter_dimension=1, tiled=True).astype(F32)


def row_totals(first, second):
    return lax.psum((first, second), "col")


def gather_weights(w_query, w_key, w_value, w_up, w_proj, w_down):
    inner = (
        lax.all_gather(w_query, "row", axis=0, tiled=True),
        lax.all_gather(w_key, "row", axis=0, tiled=True),
        lax.all_gather(w_value, "row", axis=0, tiled=True),
        lax.all_gather(w_up, "row", axis=0, tiled=True),
    )
    outer = (
        lax.all_gather(w_proj, "row", axis=1, tiled=True),
        lax.all_gather(w_down, "row", axis=1, tiled=True),
    )
    return (inner, outer)


def norm_shares(resid, gain, shift):
    width = resid.shape[1] * lax.axis_size("col")
    total, squares = row_totals(jnp.sum(resid, axis=1), jnp.sum(resid * resid, axis=1))
    mean = total / width
    rstd = lax.rsqrt(squares / width - mean * mean + EPS)
    normed = (resid - mean[:, None]) * rstd[:, None]
    return (normed * gain + shift, normed, rstd)


def norm_back(upstream, normed, rstd, gain):
    width = upstream.shape[1] * lax.axis_size("col")
    scaled = upstream * gain
    total, along = row_totals(jnp.sum(scaled, axis=1), jnp.sum(scaled * normed, axis=1))
    back = rstd[:, None] * (scaled - total[:, None] / width - normed * (along[:, None] / width))
    return (back, jnp.sum(upstream * normed, axis=0), jnp.sum(upstream, axis=0))


def attend_forward(pack):
    queries, keys, values, ids = pack
    scale = queries.shape[2] ** (-0.5)
    block = min(512, queries.shape[0])
    same = ids[:, None] == ids[None, :]
    outputs = []
    logsums = []
    for begin in range(0, queries.shape[0], block):
        scores = (
            jnp.einsum(
                "qhd,khd->hqk",
                queries[begin : begin + block],
                keys,
                preferred_element_type=jnp.float32,
            )
            * scale
        )
        scores = jnp.where(same[None, begin : begin + block], scores, NEGATIVE)
        peak = jnp.max(scores, axis=2, keepdims=True)
        expo = jnp.exp(scores - peak)
        total = jnp.sum(expo, axis=2, keepdims=True)
        probs = (expo / total).astype(jnp.bfloat16)
        outputs.append(
            jnp.einsum("hqk,khd->qhd", probs, values, preferred_element_type=jnp.float32)
        )
        logsums.append((peak + jnp.log(total))[:, :, 0])
    return (jnp.concatenate(outputs, axis=0), jnp.concatenate(logsums, axis=1))


def attend_back(pack):
    queries, keys, values, ids, logsum, grad_out = pack
    scale = queries.shape[2] ** (-0.5)
    block = min(512, queries.shape[0])
    same = ids[:, None] == ids[None, :]
    grad_keys = jnp.zeros(keys.shape, jnp.float32)
    grad_values = jnp.zeros(values.shape, jnp.float32)
    grad_queries = []
    for begin in range(0, queries.shape[0], block):
        query_rows = queries[begin : begin + block]
        grad_rows = grad_out[begin : begin + block]
        scores = (
            jnp.einsum("qhd,khd->hqk", query_rows, keys, preferred_element_type=jnp.float32) * scale
        )
        scores = jnp.where(same[None, begin : begin + block], scores, NEGATIVE)
        probs = jnp.exp(scores - logsum[:, begin : begin + block, None])
        grad_probs = jnp.einsum(
            "qhd,khd->hqk", grad_rows, values, preferred_element_type=jnp.float32
        )
        inner = jnp.sum(probs * grad_probs, axis=2, keepdims=True)
        grad_scores = (probs * (grad_probs - inner)).astype(jnp.bfloat16)
        grad_queries.append(
            jnp.einsum("hqk,khd->qhd", grad_scores, keys, preferred_element_type=jnp.float32)
            * scale
        )
        grad_keys = (
            grad_keys
            + jnp.einsum(
                "hqk,qhd->khd", grad_scores, query_rows, preferred_element_type=jnp.float32
            )
            * scale
        )
        grad_values = grad_values + jnp.einsum(
            "hqk,qhd->khd",
            probs.astype(jnp.bfloat16),
            grad_rows,
            preferred_element_type=jnp.float32,
        )
    return (jnp.concatenate(grad_queries, axis=0), grad_keys, grad_values)


def per_device(
    tokens,
    lengths,
    w_query,
    b_query,
    w_key,
    w_value,
    b_value,
    w_proj,
    b_proj,
    norm_gain,
    norm_shift,
    w_up,
    b_up,
    w_down,
    b_down,
    final_gain,
    final_shift,
    cotangent,
):
    rows, share = tokens.shape
    heads = w_query.shape[1] // HD
    ids = segment_ids(lengths)
    seq_count = ids.shape[0]
    valid = (ids.reshape(rows) != lengths.shape[1] - 1).astype(jnp.float32)[:, None]
    inner, outer = gather_weights(w_query, w_key, w_value, w_up, w_proj, w_down)
    full_query, full_key, full_value, full_up = inner
    full_proj, full_down = outer
    stream = tokens.astype(jnp.float32)
    gathered = gather_features(tokens)
    queries = (jnp.dot(gathered, full_query, preferred_element_type=jnp.float32) + b_query).astype(
        jnp.bfloat16
    )
    keys = jnp.dot(gathered, full_key, preferred_element_type=jnp.float32).astype(jnp.bfloat16)
    values = (jnp.dot(gathered, full_value, preferred_element_type=jnp.float32) + b_value).astype(
        jnp.bfloat16
    )
    shape = (seq_count, LEN, heads, HD)
    query_seq = queries.reshape(shape)
    key_seq = keys.reshape(shape)
    value_seq = values.reshape(shape)
    mixed, logsum = lax.map(attend_forward, (query_seq, key_seq, value_seq, ids))
    heads_out = mixed.reshape(rows, heads * HD).astype(jnp.bfloat16)
    attn = (
        scatter_features(jnp.dot(heads_out, full_proj, preferred_element_type=jnp.float32)) + b_proj
    )
    hidden, normed_one, rstd_one = norm_shares(stream + attn, norm_gain, norm_shift)
    hidden_low = gather_features(hidden.astype(jnp.bfloat16))
    pre = jnp.dot(hidden_low, full_up, preferred_element_type=jnp.float32) + b_up
    act, gelu_back = jax.vjp(lambda inputs: jax.nn.gelu(inputs, approximate=True), pre)
    act_low = act.astype(jnp.bfloat16)
    ffn = scatter_features(jnp.dot(act_low, full_down, preferred_element_type=jnp.float32)) + b_down
    result, normed_two, rstd_two = norm_shares(hidden + ffn, final_gain, final_shift)
    totals = lax.psum(
        (
            jnp.sum(valid * stream * stream),
            jnp.sum(valid * attn * attn),
            jnp.sum(valid * ffn * ffn),
            jnp.sum(valid) * share,
        ),
        ("row", "col"),
    )
    norms = jnp.sqrt(jnp.stack([totals[0], totals[1], totals[2]]) / totals[3])
    back_inner, back_outer = gather_weights(w_query, w_key, w_value, w_up, w_proj, w_down)
    full_query, full_key, full_value, full_up = back_inner
    full_proj, full_down = back_outer
    grad_two, grad_fgain, grad_fshift = norm_back(
        cotangent.astype(jnp.float32), normed_two, rstd_two, final_gain
    )
    grad_ffn = grad_two.astype(jnp.bfloat16)
    grad_dbias = jnp.sum(grad_ffn.astype(jnp.float32), axis=0)
    ffn_wide = gather_features(grad_ffn)
    grad_down = jnp.einsum("tf,td->fd", act_low, ffn_wide, preferred_element_type=jnp.float32)
    grad_act = jnp.einsum("td,fd->tf", ffn_wide, full_down, preferred_element_type=jnp.float32)
    grad_pre = gelu_back(grad_act)[0].astype(jnp.bfloat16)
    grad_ubias = jnp.sum(grad_pre.astype(jnp.float32), axis=0)
    grad_up = jnp.einsum("td,tf->df", hidden_low, grad_pre, preferred_element_type=jnp.float32)
    grad_hidden = (
        scatter_features(
            jnp.einsum("tf,df->td", grad_pre, full_up, preferred_element_type=jnp.float32)
        )
        + grad_two
    )
    grad_one, grad_ngain, grad_nshift = norm_back(grad_hidden, normed_one, rstd_one, norm_gain)
    grad_attn = grad_one.astype(jnp.bfloat16)
    grad_pbias = jnp.sum(grad_attn.astype(jnp.float32), axis=0)
    attn_wide = gather_features(grad_attn)
    grad_proj = jnp.einsum("th,td->hd", heads_out, attn_wide, preferred_element_type=jnp.float32)
    grad_heads = jnp.einsum(
        "td,hd->th", attn_wide, full_proj, preferred_element_type=jnp.float32
    ).astype(jnp.bfloat16)
    back_query, back_key, back_value = lax.map(
        attend_back, (query_seq, key_seq, value_seq, ids, logsum, grad_heads.reshape(shape))
    )
    grad_queries = back_query.reshape(rows, heads * HD).astype(jnp.bfloat16)
    grad_keys = back_key.reshape(rows, heads * HD).astype(jnp.bfloat16)
    grad_values = back_value.reshape(rows, heads * HD).astype(jnp.bfloat16)
    grad_qbias = jnp.sum(grad_queries.astype(jnp.float32), axis=0)
    grad_vbias = jnp.sum(grad_values.astype(jnp.float32), axis=0)
    grad_query = jnp.einsum("td,th->dh", gathered, grad_queries, preferred_element_type=jnp.float32)
    grad_key = jnp.einsum("td,th->dh", gathered, grad_keys, preferred_element_type=jnp.float32)
    grad_value = jnp.einsum("td,th->dh", gathered, grad_values, preferred_element_type=jnp.float32)
    partial_back = (
        jnp.einsum("th,dh->td", grad_queries, full_query, preferred_element_type=jnp.float32)
        + jnp.einsum("th,dh->td", grad_keys, full_key, preferred_element_type=jnp.float32)
        + jnp.einsum("th,dh->td", grad_values, full_value, preferred_element_type=jnp.float32)
    )
    grad_tokens = scatter_features(partial_back) + grad_one
    grad_query, grad_key, grad_value, grad_up = (
        lax.psum_scatter(
            grad_query.astype(jnp.bfloat16), "row", scatter_dimension=0, tiled=True
        ).astype(jnp.float32),
        lax.psum_scatter(
            grad_key.astype(jnp.bfloat16), "row", scatter_dimension=0, tiled=True
        ).astype(jnp.float32),
        lax.psum_scatter(
            grad_value.astype(jnp.bfloat16), "row", scatter_dimension=0, tiled=True
        ).astype(jnp.float32),
        lax.psum_scatter(
            grad_up.astype(jnp.bfloat16), "row", scatter_dimension=0, tiled=True
        ).astype(jnp.float32),
    )
    grad_proj, grad_down = (
        lax.psum_scatter(
            grad_proj.astype(jnp.bfloat16), "row", scatter_dimension=1, tiled=True
        ).astype(jnp.float32),
        lax.psum_scatter(
            grad_down.astype(jnp.bfloat16), "row", scatter_dimension=1, tiled=True
        ).astype(jnp.float32),
    )
    vectors = lax.psum(
        (
            grad_qbias,
            grad_vbias,
            grad_pbias,
            grad_ngain,
            grad_nshift,
            grad_ubias,
            grad_dbias,
            grad_fgain,
            grad_fshift,
        ),
        "row",
    )
    return (
        result.astype(jnp.bfloat16),
        grad_tokens,
        grad_query,
        vectors[0],
        grad_key,
        grad_value,
        vectors[1],
        grad_proj,
        vectors[2],
        vectors[3],
        vectors[4],
        grad_up,
        vectors[5],
        grad_down,
        vectors[6],
        vectors[7],
        vectors[8],
        norms,
    )


def placements(row, col):
    grid, turned, share = P(row, col), P(col, row), P(col)
    args = (
        grid, P(row, None), grid, share, grid, grid, share, turned, share, share, share, grid, share, turned, share, share, share, grid,
    )
    outs = (
        grid, grid, grid, share, grid, grid, share, turned, share, share, share, grid, share, turned, share, share, share, P(),
    )
    return (args, outs)


def solution(mesh):
    if mesh.shape["row"] == 4 and mesh.shape["col"] == 8:
        mesh = Mesh(mesh.devices.reshape(2, 2, 4, 2), AXES)
        args, outs = placements(("y", "c"), ("z", "x"))
        body = square_device
    else:
        args, outs = placements("row", "col")
        body = per_device
    return jax.shard_map(body, mesh=mesh, in_specs=args, out_specs=outs, check_vma=False)
```
